32 devices in a mesh: dp: 16 (over z, y, x), mp: 2 (over core).
Axes of the slice: x: 2, y: 2, z: 4, core: 2. Of those that a mesh axis runs over, the one named last changes fastest.
Arguments:
- dec_input: bfloat16 [32, 128, 768], P('dp'), may hold values from -6 to 6
- enc_output: bfloat16 [32, 512, 768], P('dp'), may hold values from -6 to 6
- dec_lengths: int32 [16, 2], P('dp'), may hold values from 1 to 128, 192 in all within a row
- enc_lengths: int32 [16, 2], P('dp'), may hold values from 1 to 512, 768 in all within a row
- self_query: bfloat16 [768, 768], P(None, 'mp'), may hold values from -0.0546875 to 0.0546875
- self_key: bfloat16 [768, 768], P(None, 'mp'), may hold values from -0.21875 to 0.21875
- self_value: bfloat16 [768, 768], P(None, 'mp'), may hold values from -0.21875 to 0.21875
- self_output: bfloat16 [768, 768], P('mp'), may hold values from -0.625 to 0.625
- self_gain: float32 [768], replicated, may hold values from 0.1 to 1.9
- rel_bias: float32 [32, 12], P(None, 'mp'), may hold values from -4 to 4
- cross_query: bfloat16 [768, 768], P(None, 'mp'), may hold values from -0.0546875 to 0.0546875
- cross_key: bfloat16 [768, 768], P(None, 'mp'), may hold values from -0.21875 to 0.21875
- cross_value: bfloat16 [768, 768], P(None, 'mp'), may hold values from -0.21875 to 0.21875
- cross_output: bfloat16 [768, 768], P('mp'), may hold values from -0.625 to 0.625
- cross_gain: float32 [768], replicated, may hold values from 0.1 to 1.9
- ffn_in: bfloat16 [768, 3072], P(None, 'mp'), may hold values from -0.21875 to 0.21875
- ffn_out: bfloat16 [3072, 768], P('mp'), may hold values from -0.15625 to 0.15625
- ffn_gain: float32 [768], replicated, may hold values from 0.1 to 1.9
- cotangent: bfloat16 [32, 128, 768], P('dp'), may hold values from -6 to 6
Outputs:
- layer_output: bfloat16 [32, 128, 768], P('dp')
- dec_grad: bfloat16 [32, 128, 768], P('dp')
- enc_grad: bfloat16 [32, 512, 768], P('dp')
- self_query_grad: float32 [768, 768], P('dp', 'mp')
- self_key_grad: float32 [768, 768], P('dp', 'mp')
- self_value_grad: float32 [768, 768], P('dp', 'mp')
- self_output_grad: float32 [768, 768], P('mp', 'dp')
- self_gain_grad: float32 [768], replicated
- rel_bias_grad: float32 [32, 12], P(None, 'mp')
- cross_query_grad: float32 [768, 768], P('dp', 'mp')
- cross_key_grad: float32 [768, 768], P('dp', 'mp')
- cross_value_grad: float32 [768, 768], P('dp', 'mp')
- cross_output_grad: float32 [768, 768], P('mp', 'dp')
- cross_gain_grad: float32 [768], replicated
- ffn_in_grad: float32 [768, 3072], P('dp', 'mp')
- ffn_out_grad: float32 [3072, 768], P('mp', 'dp')
- ffn_gain_grad: float32 [768], replicated
The draws below stay inside these ranges and needn't reach their ends.
Inputs may be any that keep to these rules, and one draw needn't show every extreme that they name: `dec_lengths`: each device's 2 decoder lengths sum to 192. `enc_lengths`: each device's 2 encoder lengths sum to 768.
All inputs are finite; a program needn't handle non-finite values.
Results may differ from the reference program's by a relative error of at most 0.024.
The reference program's roundings to bfloat16 on the way count: a program that leaves them out, or rounds other values in their place, can miss the bound.
Values sent between devices are 32-bit elements; how exact they have to be, the bound alone decides.
No kernel may reach another device: no remote copies, remote signals or barrier semaphores. Data moves between devices by JAX's collectives and lax.ppermute only.
A program may use at most 128 MiB of HBM per device.

```python
import math
import jax
import jax.numpy as jnp
import numpy as np
from jax import lax

D = 768
H = 12
FF = 3072
BUCKETS = 32
LEN = 128
ENC = 512
SEQ_DEV = 2
INNER = 768
EXAMPLES = 32
N_DP = 16


def with_spikes(entries, own_key, source, target, parts, factor):
    owner, partner = [(jnp.arange(entries.shape[dim]) // (entries.shape[dim] // parts)).reshape([-1 if axis == dim else 1 for axis in range(entries.ndim)]) for dim in (source, target)]
    chosen = jax.random.permutation(own_key, parts)[partner]
    strong = (owner == chosen) | (owner == (partner + parts // 2) % parts)
    return jnp.where(strong, factor * entries, entries)


def steps_of(stream_key, dims, shards, smallest, largest):
    factor_of, own = 1.0, jax.random.fold_in(stream_key, 6)
    for position, blocks in shards:
        heights = jnp.exp(jax.random.uniform(jax.random.fold_in(own, position), (blocks,), jnp.float32, smallest / len(shards), largest / len(shards)))
        factor_of = factor_of * jnp.repeat(heights, dims[position] // blocks).reshape([-1 if axis == position else 1 for axis in range(len(dims))])
    return factor_of


def profile(count, total, reach, skew):
    portions = [(1 << 20) // math.isqrt(grade ** skew) + 1 for grade in range(2, count + 1)]
    spare, given = total - reach - (count - 1), [1] * (count - 1)
    while spare > 0:
        candidates = [i for i in range(count - 1) if given[i] < reach]
        mass, budget = sum([portions[i] for i in candidates]), spare
        for i in candidates:
            extra = min(reach - given[i], max(1, budget * portions[i] // mass), spare)
            given[i] = given[i] + extra
            spare = spare - extra
    return np.array([reach] + given)


def uneven(stream_key, count, total, limit, lean):
    if count == 2:
        one = jax.random.randint(stream_key, (), max(1, total - limit), min(limit, total - 1) + 1)
        return jnp.stack([one, total - one])
    lengths = jnp.asarray(profile(count, total, limit, lean), jnp.int32)
    couples = (count - 1) // 2
    donor, receiver = lengths[1:1 + 2 * couples:2], lengths[2:2 + 2 * couples:2]
    margin = jnp.minimum(donor - 1, limit - receiver)
    shifted = jax.random.randint(jax.random.fold_in(stream_key, 1), (couples,), 0, 1 << 20) % (margin + 1)
    lengths = lengths.at[1:1 + 2 * couples:2].set(donor - shifted).at[2:2 + 2 * couples:2].set(receiver + shifted)
    return lengths[jax.random.permutation(jax.random.fold_in(stream_key, 2), count)]


def normal_values(stream_key, shape, width, most, pieces=(), kind=jnp.bfloat16):
    gain = steps_of(stream_key, shape, pieces, -0.22, 0.18) if pieces else 1.0
    drawn = jax.random.normal(stream_key, shape, jnp.float32) * width * gain
    return jnp.minimum(jnp.maximum(drawn, -most), most).astype(kind)


def bell_draw_with(stream_key, extent, scale, limit, shards, heavy, kind=jnp.bfloat16):
    result = scale * jax.random.normal(stream_key, extent, jnp.float32)
    if shards:
        result = result * steps_of(stream_key, extent, shards, -0.22, 0.18)
    return jnp.clip(with_spikes(result, jax.random.fold_in(stream_key, 3), *heavy), -limit, limit).astype(kind)


def setup_inputs(seed: int = 0) -> dict:
    splits = jax.random.split(jax.random.key(seed), 20)
    return {
        "dec_input": normal_values(splits[0], (EXAMPLES, LEN, D), 1.0, 6.0, ((0, 16),)),
        "enc_output": normal_values(splits[1], (EXAMPLES, ENC, D), 1.0, 6.0, ((0, 16),)),
        "dec_lengths": jax.vmap(lambda own: uneven(own, SEQ_DEV, 3 * LEN * SEQ_DEV // 4, LEN, 1))(jax.random.split(splits[2], N_DP)).reshape((N_DP, SEQ_DEV)).astype(jnp.int32),
        "enc_lengths": jax.vmap(lambda own: uneven(own, SEQ_DEV, 3 * ENC * SEQ_DEV // 4, ENC, 1))(jax.random.split(splits[3], N_DP)).reshape((N_DP, SEQ_DEV)).astype(jnp.int32),
        "self_query": normal_values(splits[4], (D, INNER), (16 * D) ** -0.5, 0.0546875, ((1, 2),)),
        "self_key": normal_values(splits[5], (D, INNER), D ** -0.5, 0.21875, ((1, 2),)),
        "self_value": normal_values(splits[6], (D, INNER), D ** -0.5, 0.21875, ((1, 2),)),
        "self_output": normal_values(splits[7], (INNER, D), (INNER // 8) ** -0.5, 0.625, ((0, 2),)),
        "self_gain": jnp.clip(1.0 + 0.18 * jax.random.normal(splits[8], (D,), jnp.float32), 0.1, 1.9),
        "rel_bias": normal_values(splits[9], (BUCKETS, H), 1.0, 4.0, ((1, 2),), jnp.float32),
        "cross_query": normal_values(splits[10], (D, INNER), (16 * D) ** -0.5, 0.0546875, ((1, 2),)),
        "cross_key": normal_values(splits[11], (D, INNER), D ** -0.5, 0.21875, ((1, 2),)),
        "cross_value": normal_values(splits[12], (D, INNER), D ** -0.5, 0.21875, ((1, 2),)),
        "cross_output": normal_values(splits[13], (INNER, D), (INNER // 8) ** -0.5, 0.625, ((0, 2),)),
        "cross_gain": jnp.clip(1.0 + 0.18 * jax.random.normal(splits[14], (D,), jnp.float32), 0.1, 1.9),
        "ffn_in": normal_values(splits[15], (D, FF), D ** -0.5, 0.21875, ((1, 2),)),
        "ffn_out": normal_values(splits[16], (FF, D), (FF // 2) ** -0.5, 0.15625, ((0, 2),)),
        "ffn_gain": jnp.clip(1.0 + 0.18 * jax.random.normal(splits[17], (D,), jnp.float32), 0.1, 1.9),
        "cotangent": bell_draw_with(splits[18], (EXAMPLES, LEN, D), 1.0, 6.0, ((0, 16),), (0, 2, 16, 2.0)),
    }


@jax.custom_vjp
def low(v):
    return lax.optimization_barrier(v.astype(jnp.bfloat16)).astype(jnp.float32)

@jax.custom_vjp
def low_back(v):
    return v

def low_keep(v):
    return (low(v), None)

def low_pass(kept, grad):
    return (grad,)

def back_keep(v):
    return (v, None)

def back_low(kept, grad):
    return (low(grad),)
low.defvjp(low_keep, low_pass)
low_back.defvjp(back_keep, back_low)
epsilon = 1e-06
highest = lax.Precision.HIGHEST
masked_value = -1e+30

def bucket_table(seq_len, buckets):
    half_count = buckets // 2
    distance = np.maximum(np.arange(seq_len)[:, None] - np.arange(seq_len)[None, :], 0)
    bounds = np.ceil(16.0 * 8.0 ** (np.arange(1, half_count) / half_count))
    coarse = half_count + (distance[:, :, None] >= bounds[None, None, :]).sum(-1)
    chosen = np.where(distance < half_count, distance, coarse)
    return (chosen[:, :, None] == np.arange(buckets)[None, None, :]).astype(np.float32)

def smooth(values):
    return jax.nn.gelu(values, approximate=True)

def rms_norm(values, gain_vector):
    return values * lax.rsqrt(lax.optimization_barrier(jnp.mean(values * values, axis=-1, keepdims=True)) + epsilon) * gain_vector

def project(values, weight):
    return jnp.einsum('gld,de->gle', values, weight, precision=highest)

def both_low(values):
    return low(low_back(values))

def attend(queries, key_heads, value_heads, bias_heads, allowed):
    raw_scores = low_back(jnp.einsum('gqhc,gkhc->ghqk', queries, key_heads, precision=highest))
    logits = jnp.where(allowed, raw_scores + bias_heads, masked_value)
    row_max = lax.optimization_barrier(jnp.max(logits, axis=-1, keepdims=True))
    weights = jnp.exp(logits - row_max)
    softmax_weights = weights / lax.optimization_barrier(jnp.sum(weights, axis=-1, keepdims=True))
    return jnp.einsum('ghqk,gkhc->gqhc', low(softmax_weights), value_heads, precision=highest)

def decoder_layer(dec_block, enc_block, dec_len, enc_len, params):
    self_query, self_key, self_value, self_output, self_gain, rel_bias, cross_query, cross_key, cross_value, cross_output, cross_gain, ffn_in, ffn_out, ffn_gain = params
    group_size = dec_block.shape[0]
    seq_len = dec_block.shape[1]
    enc_steps = enc_block.shape[1]
    head_count = rel_bias.shape[1]

    def split_heads(values):
        return values.reshape(values.shape[0], values.shape[1], head_count, -1)
    places = jnp.arange(seq_len, dtype=jnp.int32)
    dec_valid = places[None, :] < dec_len[:, None]
    enc_valid = jnp.arange(enc_steps, dtype=jnp.int32)[None, :] < enc_len[:, None]
    self_allowed = (places[:, None] >= places[None, :])[None, None] & dec_valid[:, None, None, :]
    cross_allowed = enc_valid[:, None, None, :]
    onehot = jnp.asarray(bucket_table(seq_len, rel_bias.shape[0]))
    bias_heads = jnp.einsum('qkb,bh->hqk', onehot, rel_bias, precision=highest)[None]
    normed = low(rms_norm(dec_block, self_gain))
    query_heads = split_heads(both_low(project(normed, self_query)))
    key_heads = split_heads(both_low(project(normed, self_key)))
    value_heads = split_heads(both_low(project(normed, self_value)))
    attended = attend(query_heads, key_heads, value_heads, bias_heads, self_allowed)
    attended = both_low(attended.reshape(group_size, seq_len, -1))
    after_self = dec_block + low_back(project(attended, self_output))
    normed = low(rms_norm(after_self, cross_gain))
    query_heads = split_heads(both_low(project(normed, cross_query)))
    key_heads = split_heads(both_low(project(enc_block, cross_key)))
    value_heads = split_heads(both_low(project(enc_block, cross_value)))
    attended = attend(query_heads, key_heads, value_heads, 0.0, cross_allowed)
    attended = both_low(attended.reshape(group_size, seq_len, -1))
    after_cross = after_self + low_back(project(attended, cross_output))
    normed = low(rms_norm(after_cross, ffn_gain))
    hidden = low_back(project(normed, ffn_in))
    after_ffn = after_cross + low_back(project(low(smooth(hidden)), ffn_out))
    return after_ffn * dec_valid[:, :, None].astype(jnp.float32)

def reference(dec_input, enc_output, dec_lengths, enc_lengths, self_query, self_key, self_value, self_output, self_gain, rel_bias, cross_query, cross_key, cross_value, cross_output, cross_gain, ffn_in, ffn_out, ffn_gain, cotangent):
    group_size = math.gcd(EXAMPLES, max(1, 4096 // LEN))
    blocks = EXAMPLES // group_size
    dec_len = dec_lengths.reshape(blocks, group_size).astype(jnp.int32)
    enc_len = enc_lengths.reshape(blocks, group_size).astype(jnp.int32)
    params = tuple((member.astype(jnp.float32) for member in (self_query, self_key, self_value, self_output, self_gain, rel_bias, cross_query, cross_key, cross_value, cross_output, cross_gain, ffn_in, ffn_out, ffn_gain)))

    def forward(dec_all, enc_all, *weights):
        step_layer = jax.checkpoint(lambda dec_block, enc_block, dec_part, enc_part: decoder_layer(dec_block, enc_block, dec_part, enc_part, weights))

        def scan_step(carry, inputs):
            return (carry, step_layer(*inputs))
        unused, outputs = lax.scan(scan_step, jnp.float32(0.0), (dec_all.reshape(blocks, group_size, LEN, D), enc_all.reshape(blocks, group_size, ENC, D), dec_len, enc_len))
        return outputs.reshape(EXAMPLES, LEN, D)
    layer_out, pull_back = jax.vjp(forward, dec_input.astype(jnp.float32), enc_output.astype(jnp.float32), *params)
    grads = pull_back(cotangent.astype(jnp.float32))
    return (layer_out.astype(jnp.bfloat16), grads[0].astype(jnp.bfloat16), grads[1].astype(jnp.bfloat16), grads[2], grads[3], grads[4], grads[5], grads[6], grads[7], grads[8], grads[9], grads[10], grads[11], grads[12], grads[13], grads[14], grads[15])
```

```python
import jax
import jax.numpy as jnp
import numpy as np
from jax import lax
from jax.sharding import PartitionSpec as P

epsilon = 1e-06
highest = lax.Precision.HIGHEST
masked_value = -1e30


def bucket_table(seq_len, buckets):
    half_count = buckets // 2
    distance = np.maximum(np.arange(seq_len)[:, None] - np.arange(seq_len)[None, :], 0)
    bounds = np.ceil(16.0 * 8.0 ** (np.arange(1, half_count) / half_count))
    coarse = half_count + (distance[:, :, None] >= bounds[None, None, :]).sum(-1)
    chosen = np.where(distance < half_count, distance, coarse)
    return (chosen[:, :, None] == np.arange(buckets)[None, None, :]).astype(np.float32)


def smooth(values):
    return jax.nn.gelu(values, approximate=True)


def rms_scale(values):
    return lax.rsqrt(jnp.mean(values * values, axis=-1, keepdims=True) + epsilon)


def rms_back(values, inverse, gain_vector, grad_normed):
    scaled = grad_normed * gain_vector
    grad_gain = jnp.sum((grad_normed * values * inverse).reshape(-1, values.shape[-1]), axis=0)
    grad_values = inverse * scaled - values * inverse**3 * jnp.mean(
        scaled * values, axis=-1, keepdims=True
    )
    return (grad_values, grad_gain)


def matmul(left, right):
    return jnp.einsum("...k,kn->...n", left, right, preferred_element_type=jnp.float32)


def matmul_back(left, right):
    return jnp.einsum("...n,kn->...k", left, right, preferred_element_type=jnp.float32)


def outer_sum(left, right):
    return jnp.einsum(
        "rm,rn->mn",
        left.reshape(-1, left.shape[-1]),
        right.reshape(-1, right.shape[-1]),
        preferred_element_type=jnp.float32,
    )


def pair_sum(values, axis):
    return values + lax.ppermute(values, axis, [(0, 1), (1, 0)])


def swap_bit(values, bit, count):
    return lax.ppermute(values, "dp", [(k, k ^ (1 << bit)) for k in range(count)])


def half_of(values, dim, which):
    return lax.dynamic_index_in_dim(values, which, dim, keepdims=False)


def scatter_sum(blocks, order, count):
    place = lax.axis_index("dp")
    levels = len(order)
    left = list(reversed(range(levels)))
    blocks = blocks.reshape((2,) * levels + blocks.shape[1:])
    for bit in order:
        dim = left.index(bit)
        mine = (place >> bit) & 1
        moved = swap_bit(half_of(blocks, dim, 1 - mine), bit, count)
        blocks = half_of(blocks, dim, mine) + moved
        left.remove(bit)
    return blocks


def full_sum(values, count):
    for bit in range(count.bit_length() - 1):
        values = values + swap_bit(values, bit, count)
    return values


def score_block(queries, key_heads, bias_heads, allowed):
    raw_scores = jnp.einsum(
        "sqhc,skhc->shqk", queries, key_heads, preferred_element_type=jnp.float32
    )
    return jnp.where(allowed, raw_scores + bias_heads, masked_value)


def attend_forward(queries, key_heads, value_heads, bias_heads, allowed):
    logits = score_block(queries, key_heads, bias_heads, allowed)
    row_max = jnp.max(logits, axis=-1, keepdims=True)
    weights = jnp.exp(logits - row_max)
    totals = jnp.sum(weights, axis=-1, keepdims=True)
    softmax_weights = (weights / totals).astype(jnp.bfloat16)
    attended = jnp.einsum(
        "shqk,skhc->sqhc", softmax_weights, value_heads, preferred_element_type=jnp.float32
    )
    return (attended, row_max + jnp.log(totals))


def attend_backward(
    queries, key_heads, value_heads, bias_heads, allowed, log_totals, grad_attended
):
    logits = score_block(queries, key_heads, bias_heads, allowed)
    softmax_weights = jnp.exp(logits - log_totals)
    grad_weights = jnp.einsum(
        "sqhc,skhc->shqk", grad_attended, value_heads, preferred_element_type=jnp.float32
    )
    grad_scores = softmax_weights * (
        grad_weights - jnp.sum(softmax_weights * grad_weights, axis=-1, keepdims=True)
    )
    low_scores = grad_scores.astype(jnp.bfloat16)
    grad_queries = jnp.einsum(
        "shqk,skhc->sqhc", low_scores, key_heads, preferred_element_type=jnp.float32
    )
    grad_keys = jnp.einsum(
        "shqk,sqhc->skhc", low_scores, queries, preferred_element_type=jnp.float32
    )
    grad_values = jnp.einsum(
        "shqk,sqhc->skhc",
        softmax_weights.astype(jnp.bfloat16),
        grad_attended,
        preferred_element_type=jnp.float32,
    )
    return (grad_queries, grad_keys, grad_values, grad_scores)


def on_device(
    dec_input,
    enc_output,
    dec_lengths,
    enc_lengths,
    self_query,
    self_key,
    self_value,
    self_output,
    self_gain,
    rel_bias,
    cross_query,
    cross_key,
    cross_value,
    cross_output,
    cross_gain,
    ffn_in,
    ffn_out,
    ffn_gain,
    cotangent,
):
    seq_len = dec_input.shape[1]
    enc_steps = enc_output.shape[1]
    head_count = rel_bias.shape[1]
    count = lax.axis_size("dp")
    bits = list(range(count.bit_length() - 1))
    order_a, order_b = bits, bits[1::-1] + bits[2:]

    def scattered(order, *grads):
        parts = [grad.reshape(count, -1, grad.shape[1]) for grad in grads]
        widths = [part.shape[2] for part in parts]
        total = scatter_sum(jnp.concatenate(parts, axis=2), order, count)
        return jnp.split(total, np.cumsum(widths)[:-1].tolist(), axis=1)

    def split_heads(values):
        return values.reshape(values.shape[0], values.shape[1], head_count, -1)

    def merge_heads(values):
        return values.reshape(values.shape[0], values.shape[1], -1)

    places = jnp.arange(seq_len, dtype=jnp.int32)
    dec_len = dec_lengths.reshape(-1)
    enc_len = enc_lengths.reshape(-1)
    dec_valid = places[None, :] < dec_len[:, None]
    enc_valid = jnp.arange(enc_steps, dtype=jnp.int32)[None, :] < enc_len[:, None]
    self_allowed = (places[:, None] >= places[None, :])[None, None] & dec_valid[:, None, None, :]
    cross_allowed = enc_valid[:, None, None, :]
    onehot = jnp.asarray(bucket_table(seq_len, rel_bias.shape[0]))
    bias_heads = jnp.einsum("qkb,bh->hqk", onehot, rel_bias, precision=highest)[None]
    row_mask = dec_valid[:, :, None].astype(jnp.float32)
    residual = dec_input.astype(jnp.float32)
    inverse_self = rms_scale(residual)
    normed_self = (residual * inverse_self * self_gain).astype(jnp.bfloat16)
    self_queries = split_heads(matmul(normed_self, self_query).astype(jnp.bfloat16))
    self_keys = split_heads(matmul(normed_self, self_key).astype(jnp.bfloat16))
    self_values = split_heads(matmul(normed_self, self_value).astype(jnp.bfloat16))
    attended_self, totals_self = attend_forward(
        self_queries, self_keys, self_values, bias_heads, self_allowed
    )
    mixed_self = merge_heads(attended_self).astype(jnp.bfloat16)
    after_self = residual + pair_sum(matmul(mixed_self, self_output), "mp")
    inverse_cross = rms_scale(after_self)
    normed_cross = (after_self * inverse_cross * cross_gain).astype(jnp.bfloat16)
    cross_queries = split_heads(matmul(normed_cross, cross_query).astype(jnp.bfloat16))
    cross_keys = split_heads(matmul(enc_output, cross_key).astype(jnp.bfloat16))
    cross_values = split_heads(matmul(enc_output, cross_value).astype(jnp.bfloat16))
    attended_cross, totals_cross = attend_forward(
        cross_queries, cross_keys, cross_values, 0.0, cross_allowed
    )
    mixed_cross = merge_heads(attended_cross).astype(jnp.bfloat16)
    after_cross = after_self + pair_sum(matmul(mixed_cross, cross_output), "mp")
    inverse_ffn = rms_scale(after_cross)
    normed_ffn = (after_cross * inverse_ffn * ffn_gain).astype(jnp.bfloat16)
    hidden = matmul(normed_ffn, ffn_in)
    activated, smooth_pull = jax.vjp(smooth, hidden)
    activated = activated.astype(jnp.bfloat16)
    after_ffn = after_cross + pair_sum(matmul(activated, ffn_out), "mp")
    layer_out = (after_ffn * row_mask).astype(jnp.bfloat16)
    grad_ffn = cotangent.astype(jnp.float32) * row_mask
    low_ffn = grad_ffn.astype(jnp.bfloat16)
    grad_ffn_out = outer_sum(low_ffn, activated)
    grad_hidden = smooth_pull(matmul_back(low_ffn, ffn_out))[0].astype(jnp.bfloat16)
    grad_ffn_in = outer_sum(normed_ffn, grad_hidden)
    (grad_ffn_in,) = scattered(order_a, grad_ffn_in)
    (grad_ffn_out,) = scattered(order_b, grad_ffn_out)
    grad_ffn_out = grad_ffn_out.T
    grad_normed = pair_sum(matmul_back(grad_hidden, ffn_in), "mp")
    grad_norm_in, gain_ffn = rms_back(after_cross, inverse_ffn, ffn_gain, grad_normed)
    grad_cross = grad_ffn + grad_norm_in
    low_cross = grad_cross.astype(jnp.bfloat16)
    grad_cross_output = outer_sum(low_cross, mixed_cross)
    grad_mixed = split_heads(matmul_back(low_cross, cross_output).astype(jnp.bfloat16))
    grad_queries, grad_keys, grad_values, ignored = attend_backward(
        cross_queries, cross_keys, cross_values, 0.0, cross_allowed, totals_cross, grad_mixed
    )
    query_low = merge_heads(grad_queries).astype(jnp.bfloat16)
    key_low = merge_heads(grad_keys).astype(jnp.bfloat16)
    value_low = merge_heads(grad_values).astype(jnp.bfloat16)
    grad_cross_query = outer_sum(normed_cross, query_low)
    grad_cross_key = outer_sum(enc_output, key_low)
    grad_cross_value = outer_sum(enc_output, value_low)
    grad_cross_query, grad_cross_key = scattered(order_a, grad_cross_query, grad_cross_key)
    grad_cross_value, grad_cross_output = scattered(order_b, grad_cross_value, grad_cross_output)
    grad_cross_output = grad_cross_output.T
    grad_normed = pair_sum(matmul_back(query_low, cross_query), "mp")
    enc_grad = pair_sum(
        matmul_back(key_low, cross_key) + matmul_back(value_low, cross_value), "mp"
    ).astype(jnp.bfloat16)
    grad_norm_in, gain_cross = rms_back(after_self, inverse_cross, cross_gain, grad_normed)
    grad_self = grad_cross + grad_norm_in
    low_self = grad_self.astype(jnp.bfloat16)
    grad_self_output = outer_sum(low_self, mixed_self)
    grad_mixed = split_heads(matmul_back(low_self, self_output).astype(jnp.bfloat16))
    grad_queries, grad_keys, grad_values, grad_scores = attend_backward(
        self_queries, self_keys, self_values, bias_heads, self_allowed, totals_self, grad_mixed
    )
    grad_bias = jnp.einsum("hqk,qkb->bh", jnp.sum(grad_scores, axis=0), onehot, precision=highest)
    query_low = merge_heads(grad_queries).astype(jnp.bfloat16)
    key_low = merge_heads(grad_keys).astype(jnp.bfloat16)
    value_low = merge_heads(grad_values).astype(jnp.bfloat16)
    grad_self_query = outer_sum(normed_self, query_low)
    grad_self_key = outer_sum(normed_self, key_low)
    grad_self_value = outer_sum(normed_self, value_low)
    grad_self_query, grad_self_key = scattered(order_a, grad_self_query, grad_self_key)
    grad_self_value, grad_self_output = scattered(order_b, grad_self_value, grad_self_output)
    grad_self_output = grad_self_output.T
    grad_normed = pair_sum(
        matmul_back(query_low, self_query)
        + matmul_back(key_low, self_key)
        + matmul_back(value_low, self_value),
        "mp",
    )
    grad_norm_in, gain_self = rms_back(residual, inverse_self, self_gain, grad_normed)
    dec_grad = (grad_self + grad_norm_in).astype(jnp.bfloat16)
    small = full_sum(
        jnp.concatenate([gain_self, gain_cross, gain_ffn, grad_bias.reshape(-1)]), count
    )
    width = gain_self.shape[0]
    gain_self, gain_cross, gain_ffn = (small[k * width : (k + 1) * width] for k in range(3))
    grad_bias = small[3 * width :].reshape(grad_bias.shape)
    return (
        layer_out,
        dec_grad,
        enc_grad,
        grad_self_query,
        grad_self_key,
        grad_self_value,
        grad_self_output,
        gain_self,
        grad_bias,
        grad_cross_query,
        grad_cross_key,
        grad_cross_value,
        grad_cross_output,
        gain_cross,
        grad_ffn_in,
        grad_ffn_out,
        gain_ffn,
    )


def solution(mesh):
    in_specs = (
        P("dp", None, None),
        P("dp", None, None),
        P("dp", None),
        P("dp", None),
        P(None, "mp"),
        P(None, "mp"),
        P(None, "mp"),
        P("mp", None),
        P(),
        P(None, "mp"),
        P(None, "mp"),
        P(None, "mp"),
        P(None, "mp"),
        P("mp", None),
        P(),
        P(None, "mp"),
        P("mp", None),
        P(),
        P("dp", None, None),
    )
    out_specs = (
        P("dp", None, None),
        P("dp", None, None),
        P("dp", None, None),
        P("dp", "mp"),
        P("dp", "mp"),
        P("dp", "mp"),
        P("mp", "dp"),
        P(),
        P(None, "mp"),
        P("dp", "mp"),
        P("dp", "mp"),
        P("dp", "mp"),
        P("mp", "dp"),
        P(),
        P("dp", "mp"),
        P("mp", "dp"),
        P(),
    )
    return jax.shard_map(
        on_device, mesh=mesh, in_specs=in_specs, out_specs=out_specs, check_vma=False
    )
```

```python
import functools

import jax
import jax.numpy as jnp
import numpy as np
from jax import lax
from jax.experimental import pallas as pl
from jax.experimental.pallas import tpu as pltpu
from jax.sharding import PartitionSpec as P

epsilon = 1e-06
masked_value = -1e30
head_width = 64
pair_width = 2 * head_width
bf16 = jnp.bfloat16
f32 = jnp.float32
curve = 0.7978845608028654
cubic = 0.044715


def nn(left, right, precision=None):
    return lax.dot_general(
        left, right, (((1,), (0,)), ((), ())), precision=precision, preferred_element_type=f32
    )


def nt(left, right, precision=None):
    return lax.dot_general(
        left, right, (((1,), (1,)), ((), ())), precision=precision, preferred_element_type=f32
    )


def tn(left, right, precision=None):
    return lax.dot_general(
        left, right, (((0,), (0,)), ((), ())), precision=precision, preferred_element_type=f32
    )


def gain_row(gain):
    return gain[...].reshape(1, gain.shape[0])


def iota(shape, dim):
    return lax.broadcasted_iota(jnp.int32, shape, dim)


def inverse_rms(values):
    return lax.rsqrt(jnp.sum(values * values, -1, keepdims=True) / values.shape[-1] + epsilon)


def norm_back(values, gain, upstream):
    inverse = inverse_rms(values)
    scaled = upstream * gain
    mean = jnp.sum(scaled * values, -1, keepdims=True) / values.shape[-1]
    gain_grad = jnp.sum(upstream * values * inverse, 0, keepdims=True)
    return inverse * scaled - values * (inverse * inverse * inverse * mean), gain_grad


def bucket_bounds(buckets):
    half = buckets // 2
    return [int(b) for b in np.ceil(16.0 * 8.0 ** (np.arange(1, half) / half))]


def bucket_rows(buckets, width):
    distance = iota((buckets, width), 1)
    coarse = jnp.full((buckets, width), buckets // 2, jnp.int32)
    for bound in bucket_bounds(buckets):
        coarse += (distance >= bound).astype(jnp.int32)
    chosen = jnp.where(distance < buckets // 2, distance, coarse)
    return (chosen == iota((buckets, width), 0)).astype(f32)


def half_masks():
    lane = iota((1, pair_width), 1)
    low = (lane < head_width).astype(f32)
    return low.astype(bf16), (1.0 - low).astype(bf16)


def pick_rows(first, tokens, slots):
    row, col = iota((tokens, 2 * slots), 0), iota((tokens, 2 * slots), 1)
    return (col == jnp.where(row < first, row, row + (slots - first))).astype(f32).astype(bf16)


def self_bias(bias_ref, width):
    return nn(
        bias_ref[...], bucket_rows(bias_ref.shape[1], width), precision=lax.Precision.HIGHEST
    )


def self_allowed(first, tokens):
    key, query = iota((tokens, tokens), 0), iota((tokens, tokens), 1)
    return (key <= query) & ((key < first) == (query < first))


def spread_bias(base, head, tokens):
    width = base.shape[1]
    rows = jnp.broadcast_to(base[head : head + 1], (tokens, width))
    return pltpu.roll(rows, 0, 1, stride=1, stride_axis=0)[:, :tokens]


def own_half(values):
    half = values.shape[0] // 2
    return jnp.where(lax.axis_index("mp") == 0, values[:half], values[half:])


def flush(out):
    if isinstance(out, Leaving):
        out.leave()


def self_forward(
    dec_len, dec, gain, w_q, w_k, w_v, cot, bias, w_o, x_out, low_out, qkv_out, att_out, lse_out, part_out, x_half
):
    slots, width = dec.shape[1], dec.shape[2]
    tokens = x_out.shape[0]
    heads = bias.shape[0]
    first = dec_len[:, 0:1]
    picked = pick_rows(first, tokens, slots)
    x = nn(picked, dec[...].reshape(2 * slots, width))
    x_out[...] = x.astype(bf16)
    flush(x_out)
    half = tokens // 2
    x_half[:half, :] = own_half(x)
    x_half[half:, :] = jnp.broadcast_to(first.astype(f32), (8, width))
    flush(x_half)
    normed = (x * inverse_rms(x) * gain_row(gain)).astype(bf16)
    inner = w_q.shape[1]
    for k, w in enumerate((w_q, w_k, w_v)):
        qkv_out[:, k * inner : (k + 1) * inner] = nn(normed, w[...]).astype(bf16)
    flush(qkv_out)
    low_out[...] = nn(picked, cot[...].reshape(2 * slots, width)).astype(bf16)
    flush(low_out)
    base = self_bias(bias, 2 * slots)
    allowed = self_allowed(first, tokens)
    masks = half_masks()
    top = iota((pair_width, tokens), 0) < head_width
    lse_out[...] = jnp.zeros_like(lse_out)
    for pair in range(heads // 2):
        lanes = slice(pair * pair_width, (pair + 1) * pair_width)
        q = qkv_out[:, lanes]
        k = qkv_out[:, inner + pair * pair_width : inner + (pair + 1) * pair_width]
        v = qkv_out[:, 2 * inner + pair * pair_width : 2 * inner + (pair + 1) * pair_width]
        v_t = v.astype(f32).T.astype(bf16)
        mixed = []
        for side in range(2):
            head = 2 * pair + side
            scores = nt(k, q * masks[side]) + spread_bias(base, head, tokens)
            scores = jnp.where(allowed, scores, masked_value)
            top_score = jnp.max(scores, 0, keepdims=True)
            weights = jnp.exp(scores - top_score)
            total = jnp.sum(weights, 0, keepdims=True)
            lse_out[head : head + 1, :] = top_score + jnp.log(total)
            mixed.append(nn(v_t, (weights * (1.0 / total)).astype(bf16)))
        att_out[:, lanes] = jnp.where(top, mixed[0], mixed[1]).T.astype(bf16)
    flush(att_out)
    flush(lse_out)
    part_out[...] = nn(att_out[...], w_o[...])


def encoder_forward(enc, w_k, w_v, k_out, vt_out, k_far, v_far, kt_far):
    steps = enc.shape[1]
    for w, out, out_t in ((w_v, v_far, vt_out), (w_k, k_out, kt_far)):
        for e in range(enc.shape[0]):
            rows = slice(e * steps, (e + 1) * steps)
            made = nn(enc[e], w[...])
            out[rows, :] = made.astype(bf16)
            out_t[:, rows] = made.T.astype(bf16)
        if out is v_far:
            flush(v_far)
    k_far[...] = k_out[...]


def cross_rows(first, tokens, slots, e):
    row = iota((slots, 1), 0) + e * (tokens - slots)
    return row < first if e == 0 else row >= first


def cross_forward(
    dec_len, enc_len, x, part, moved, gain, w_q, w_o, k_in, vt_in, after_out, q_out, att_out, lse_out, part_out
):
    tokens = x.shape[0]
    slots = 2 * tokens // 3
    steps = k_in.shape[0] // 2
    first = dec_len[:, 0:1]
    after = x[...].astype(f32) + (part[...] + moved[...])
    after_out[...] = after
    normed = (after * inverse_rms(after) * gain_row(gain)).astype(bf16)
    q_out[...] = nn(normed, w_q[...]).astype(bf16)
    flush(q_out)
    masks = half_masks()
    top = iota((pair_width, slots), 0) < head_width
    own = iota((tokens, 1), 0) < first
    lse_out[...] = jnp.zeros_like(lse_out)
    shift = tokens - slots
    for pair in range(q_out.shape[1] // pair_width):
        lanes = slice(pair * pair_width, (pair + 1) * pair_width)
        parts = []
        for e in range(2):
            q = q_out[e * shift : e * shift + slots, lanes]
            both = jnp.concatenate([q * masks[0], q * masks[1]], 0)
            scores = nt(k_in[e * steps : (e + 1) * steps, lanes], both)
            valid = iota((steps, 1), 0) < enc_len[:, e : e + 1]
            scores = jnp.where(valid, scores, masked_value)
            top_score = jnp.max(scores, 0, keepdims=True)
            weights = jnp.exp(scores - top_score)
            total = jnp.sum(weights, 0, keepdims=True)
            lse_out[2 * pair + e : 2 * pair + e + 1, :] = top_score + jnp.log(total)
            mixed = nn(
                vt_in[lanes, e * steps : (e + 1) * steps], (weights * (1.0 / total)).astype(bf16)
            )
            parts.append(jnp.where(top, mixed[:, :slots], mixed[:, slots:]).T)
        fill = jnp.zeros((shift, pair_width), f32)
        att_out[:, lanes] = jnp.where(
            own, jnp.concatenate([parts[0], fill], 0), jnp.concatenate([fill, parts[1]], 0)
        ).astype(bf16)
    flush(lse_out)
    part_out[...] = nn(att_out[...], w_o[...])


def ffn_both(
    after, part, moved, gain, low, w_in, w_out, *outs
):
    if len(outs) > 6:
        x_half, x_moved, *outs, x_rest = outs
        stack(x_rest, x_half, x_moved)
    after_out, normed_out, halves_out, act_out, hid_out, back_out = outs
    total = after[...] + (part[...] + moved[...])
    after_out[...] = total
    normed = (total * inverse_rms(total) * gain_row(gain)).astype(bf16)
    normed_out[...] = normed
    flush(normed_out)
    low_in = low[...]
    half = low_in.shape[0] // 2
    halves_out[:half, :] = own_half(low_in.astype(f32))
    halves_out[half:, :] = own_half(normed.astype(f32))
    hidden = w_in.shape[1]
    chunk = 512 if hidden % 512 == 0 else hidden
    for start in range(0, hidden, chunk):
        cols = slice(start, start + chunk)
        u = nn(normed, w_in[:, cols])
        t = jnp.tanh(curve * (u + cubic * (u * u * u)))
        act = (0.5 * u * (1.0 + t)).astype(bf16)
        slope = 0.5 * (1.0 + t) + 0.5 * u * (1.0 - t * t) * (curve * (1.0 + 3.0 * cubic * (u * u)))
        hid = (nt(low_in, w_out[cols, :]) * slope).astype(bf16)
        act_out[:, cols] = act
        hid_out[:, cols] = hid
        backward = nt(hid, w_in[:, cols])
        if start == 0:
            back_out[...] = backward
        else:
            back_out[...] += backward


def cross_backward(
    dec_len, enc_len, after, part, moved, gain, low, w_o, w_q, q_in, k_in, v_in, kt_in, lse,
    grad_out, low_out, dq_out, dk_out, dv_out, gain_out, part_out
):
    tokens = after.shape[0]
    slots = 2 * tokens // 3
    steps = k_in.shape[0] // 2
    first = dec_len[:, 0:1]
    shift = tokens - slots
    norm_in, gain_grad = norm_back(after[...], gain_row(gain), part[...] + moved[...])
    gain_out[...] = gain_grad
    flush(gain_out)
    grad = low[...].astype(f32) + norm_in
    grad_out[...] = grad
    flush(grad_out)
    low_grad = grad.astype(bf16)
    low_out[...] = low_grad
    flush(low_out)
    g_all = nt(low_grad, w_o[...])
    masks = half_masks()
    top = iota((pair_width, slots), 0) < head_width
    for pair in range(q_in.shape[1] // pair_width):
        lanes = slice(pair * pair_width, (pair + 1) * pair_width)
        parts = []
        for e in range(2):
            keys = slice(e * steps, (e + 1) * steps)
            window = slice(e * shift, e * shift + slots)
            q = q_in[window, lanes]
            g = jnp.where(cross_rows(first, tokens, slots, e), g_all[window, lanes], 0.0)
            g = g.astype(bf16)
            q_both = jnp.concatenate([q * masks[0], q * masks[1]], 0)
            g_both = jnp.concatenate([g * masks[0], g * masks[1]], 0)
            valid = iota((steps, 1), 0) < enc_len[:, e : e + 1]
            scores = jnp.where(valid, nt(k_in[keys, lanes], q_both), masked_value)
            p = jnp.exp(scores - lse[2 * pair + e : 2 * pair + e + 1, :])
            dp = nt(v_in[keys, lanes], g_both)
            ds = (p * (dp - jnp.sum(p * dp, 0, keepdims=True))).astype(bf16)
            dk_out[keys, lanes] = nn(ds, q_both).astype(bf16)
            dv_out[keys, lanes] = nn(p.astype(bf16), g_both).astype(bf16)
            dq = nn(kt_in[lanes, keys], ds)
            parts.append(jnp.where(top, dq[:, :slots], dq[:, slots:]).T)
        fill = jnp.zeros((shift, pair_width), f32)
        dq_out[:, lanes] = (
            jnp.concatenate([parts[0], fill], 0) + jnp.concatenate([fill, parts[1]], 0)
        ).astype(bf16)
    part_out[...] = nt(dq_out[...], w_q[...])


def self_grad(after, part, moved, gain, grad_in, grad_out, low_out, half_out, gain_out):
    norm_in, gain_grad = norm_back(after[...], gain_row(gain), part[...] + moved[...])
    gain_out[...] = gain_grad
    grad = grad_in[...] + norm_in
    grad_out[...] = grad
    low = grad.astype(bf16)
    low_out[...] = low
    half_out[...] = own_half(low.astype(f32))


def back_all(
    dec_len, low, bias, w_o, w_q, w_k, w_v, qkv, lse, dk, dv, w_ck, w_cv, act, w_ffn, dqkv_out, bias_out, part_out
):
    tokens = low.shape[0]
    self_backward(
        dec_len, low, bias, w_o, w_q, w_k, w_v, qkv, lse, dqkv_out, bias_out, part_out.at[pl.ds(0, tokens), :]
    )
    part_out[tokens : 2 * tokens, :] = nn(act[...], w_ffn[...])
    steps = dk.shape[0] // 2
    for e in range(2):
        rows = slice(e * steps, (e + 1) * steps)
        part_out[2 * tokens + e * steps : 2 * tokens + (e + 1) * steps, :] = nt(dk[rows, :], w_ck[...]) + nt(
            dv[rows, :], w_cv[...]
        )


def self_backward(dec_len, low, bias, w_o, w_q, w_k, w_v, qkv, lse, dqkv_out, bias_out, part_out):
    tokens = low.shape[0]
    heads = bias.shape[0]
    first = dec_len[:, 0:1]
    inner = w_q.shape[1]
    g_all = nt(low[...], w_o[...]).astype(bf16)
    reach = 4 * tokens // 3
    base = self_bias(bias, reach)
    allowed = self_allowed(first, tokens)
    masks = half_masks()
    top = iota((pair_width, tokens), 0) < head_width
    diagonals = []
    for pair in range(heads // 2):
        lanes = slice(pair * pair_width, (pair + 1) * pair_width)
        k_lanes = slice(inner + pair * pair_width, inner + (pair + 1) * pair_width)
        v_lanes = slice(2 * inner + pair * pair_width, 2 * inner + (pair + 1) * pair_width)
        q, k, v, g = qkv[:, lanes], qkv[:, k_lanes], qkv[:, v_lanes], g_all[:, lanes]
        k_t = k.astype(f32).T.astype(bf16)
        dk, dv, dq = 0.0, 0.0, []
        for side in range(2):
            head = 2 * pair + side
            q_half, g_half = q * masks[side], g * masks[side]
            scores = nt(k, q_half) + spread_bias(base, head, tokens)
            scores = jnp.where(allowed, scores, masked_value)
            p = jnp.exp(scores - lse[head : head + 1, :])
            dp = nt(v, g_half)
            ds = p * (dp - jnp.sum(p * dp, 0, keepdims=True))
            ds_low = ds.astype(bf16)
            dk += nn(ds_low, q_half)
            dv += nn(p.astype(bf16), g_half)
            dq.append(nn(k_t, ds_low))
            wide = jnp.concatenate([ds, jnp.zeros((tokens, reach - tokens), f32)], 1)
            total = wide[:8]
            for start in range(8, tokens, 8):
                total += pltpu.roll(wide[start : start + 8], reach - start, 1)
            diagonals.append(total)
        dqkv_out[:, lanes] = jnp.where(top, dq[0], dq[1]).T.astype(bf16)
        dqkv_out[:, k_lanes] = dk.astype(bf16)
        dqkv_out[:, v_lanes] = dv.astype(bf16)
    flush(dqkv_out)
    part_out[...] = (
        nt(dqkv_out[:, :inner], w_q[...])
        + nt(dqkv_out[:, inner : 2 * inner], w_k[...])
        + nt(dqkv_out[:, 2 * inner :], w_v[...])
    )
    total = jnp.concatenate(diagonals, 0)
    row = iota(total.shape, 0) & 7
    lined = jnp.zeros_like(total)
    for s in range(8):
        lined += jnp.where(row == s, pltpu.roll(total, (reach - s) % reach, 1), 0.0)
    head_of = ((iota((8, 8 * heads), 1) >> 3) == iota((8, 8 * heads), 0)).astype(f32)
    by_head = nn(head_of, lined, precision=lax.Precision.HIGHEST)
    bias_out[...] = nt(by_head, bucket_rows(bias.shape[1], reach), precision=lax.Precision.HIGHEST)


def unpacked(values, first, slots):
    tokens = values.shape[0]
    slot, row = iota((2 * slots, tokens), 0), iota((2 * slots, tokens), 1)
    limit = jnp.where(slot < slots, first, slots + tokens - first)
    wanted = jnp.where(slot < slots, slot, slot - slots + first)
    spread = ((row == wanted) & (slot < limit)).astype(f32).astype(bf16)
    return nn(spread, values.astype(bf16)).astype(bf16)


def finish_self_norm(
    heads, x, part, moved, gain, grad_in, gain_ffn, gain_cross, bias_grad, dec_out, small_out
):
    tokens, width = x.shape
    norm_in, gain_grad = norm_back(x[...].astype(f32), gain_row(gain), part[:tokens, :] + moved[:tokens, :])
    buckets = bias_grad.shape[1]
    small_out[...] = jnp.zeros_like(small_out)
    small_out[:heads, :buckets] = bias_grad[:heads, :]
    small_out[heads : heads + 1, :width] = gain_grad
    small_out[heads : heads + 1, width : 2 * width] = gain_cross[...]
    small_out[heads + 1 : heads + 2, :width] = gain_ffn[...]
    dec_out[...] = (grad_in[...] + norm_in).astype(bf16)


def finish_outputs(dec_len, dec, part, moved, after, dec_out, layer_out, enc_out):
    tokens = dec.shape[0]
    first, slots = dec_len[:, 0:1], dec_out.shape[1]
    dec_out[...] = unpacked(dec[...], first, slots).reshape(dec_out.shape)
    total = after[...] + (part[tokens : 2 * tokens, :] + moved[tokens : 2 * tokens, :])
    layer_out[...] = unpacked(total, first, slots).reshape(layer_out.shape)
    enc_out[...] = (part[2 * tokens :, :] + moved[2 * tokens :, :]).astype(bf16).reshape(enc_out.shape)


def pause(out):
    out[...] = jnp.zeros_like(out)


def collect(low_half, low_a, halves, group_a, low_out, group_out):
    stack(low_out, low_half, low_a)
    stack(group_out, halves, group_a)


def gather_self(x_moved, x_rest, low_a, low_rest, out):
    stack(out, x_moved, x_rest, low_a, low_rest)


def relay(value, out):
    out[...] = value[...]


def gather_ffn(group_a, group_rest, out):
    stack(out, group_a, group_rest)


def place_of():
    return lax.axis_index("dp"), lax.axis_index("mp")


def own_bit(stage):
    place, core = place_of()
    shift = (core, 1 - core, 2 + core, 3 - core)[stage]
    return lax.shift_right_logical(place, shift) & 1


def entry(stage, step, bit):
    if stage % 2:
        return 2 * step + bit
    core = lax.axis_index("mp")
    return jnp.where(core == 0, 2 * step + bit, (step // 2) * 4 + 2 * bit + step % 2)


def pick_chunks(chunks, rows, width):
    gap = iota((rows, width), 1) - iota((rows, width), 0)
    return jnp.concatenate([(gap == chunk * rows).astype(f32) for chunk in chunks], 0).astype(bf16)


def half_pick(other, width):
    bit = own_bit(0)
    bit = 1 - bit if other else bit
    return pick_chunks([entry(0, step, bit) for step in range(8)], width // 16, width)


def fold_lanes(values):
    half = values.shape[0] // 2
    return jnp.concatenate([values[:half], values[half:]], 1)


def unfold_lanes(values):
    half = values.shape[1] // 2
    return jnp.concatenate([values[:, :half], values[:, half:]], 0)


def split_entries(stage, source, send_out, keep_out, rows):
    bit = own_bit(stage)
    for step in range(keep_out.shape[0] // rows):
        here = slice(step * rows, (step + 1) * rows)
        send_out[here, :] = source(entry(stage, step, 1 - bit))
        keep_out[here, :] = source(entry(stage, step, bit))


def pack_early(after, gain, att, early_out, own):
    width = after.shape[1]
    inner = att.shape[1]
    v = after[...]
    normed = (v * inverse_rms(v) * gain_row(gain)).astype(bf16)
    own[...] = nt(half_pick(0, width), normed).astype(bf16)
    early_out[:, :inner] = fold_lanes(nt(half_pick(1, width), normed))
    early_out[:, inner:] = att[...].astype(f32)


def stack(out, *parts):
    at = 0
    for part in parts:
        out[at : at + part.shape[0], :] = part[...]
        at += part.shape[0]


def cross_weights(enc, dk, dv, dq, low, late_out, keep_out):
    steps, width = enc.shape[1:]
    inner = dk.shape[1]
    half = keep_out.shape[0]
    flat = enc[...].reshape(2 * steps, width)
    for other, out in ((0, keep_out), (1, late_out)):
        left = nt(half_pick(other, width), flat).astype(bf16)
        out[:half, :inner] = nn(left, dk[...])
        out[:half, inner:] = nn(left, dv[...])
        flush(out)
    late_out[half:, :inner] = dq[...].astype(f32)
    late_out[half:, inner:] = fold_lanes(nt(half_pick(1, width), low[...]))


def cross_fold(keep, moved, early, own, dq, low, att, send_out, keep_out, total):
    width = low.shape[1]
    half, inner = own.shape[0], dq.shape[1]
    rows = width // 16
    total[:, :inner] = nn(own[...], dq[...]) + nn(
        unfold_lanes(early[:, :inner]).astype(bf16), moved[half:, :inner].astype(bf16)
    )
    total[:, 3 * inner :] = nn(nt(half_pick(0, width), low[...]).astype(bf16), att[...]) + nn(
        unfold_lanes(moved[half:, inner:]).astype(bf16), early[:, inner:].astype(bf16)
    )
    total[:, inner : 3 * inner] = keep[...] + moved[:half, :]
    split_entries(1, lambda i: total[pl.ds(pl.multiple_of(i * rows, 8), rows), :], send_out, keep_out, rows)


def self_group(
    x, dqkv, low, att, here, there, gain, bias, w_q, w_k, w_v, w_o, small,
    send_out, keep_out, made, grads, total
):
    tokens, width = x.shape
    inner = att.shape[1]
    heads = bias.shape[0]
    half = tokens // 2
    place, core = place_of()
    rows = width // 16
    base = self_bias(bias, 4 * tokens // 3)
    masks = half_masks()
    top = iota((pair_width, tokens), 0) < head_width
    biases = [spread_bias(base, head, tokens) for head in range(heads)]
    tall = half + 8
    x_at, low_at = (0, tall, 2 * tall), (3 * tall, 3 * tall + half, 3 * tall + 2 * half)
    orders = ((0, 1), (1, 0), (2, 2))

    def joined(starts, mine, other):
        a, b = here[starts[mine] : starts[mine] + half, :], there[starts[other] : starts[other] + half, :]
        return [jnp.where(core == 0, a, b), jnp.where(core == 0, b, a)]

    v = jnp.concatenate([part for order in orders for part in joined(x_at, *order)], 0)
    normed = (v * inverse_rms(v) * gain_row(gain)).astype(bf16)
    low_all = jnp.concatenate([part for order in orders for part in joined(low_at, *order)], 0).astype(bf16)
    for k, w in enumerate((w_q, w_k, w_v)):
        made[:, k * inner : (k + 1) * inner] = nn(normed, w[...]).astype(bf16)
    made[:, 3 * inner :] = nt(low_all, w_o[...]).astype(bf16)
    grads[:tokens, : 3 * inner] = dqkv[...]
    grads[:tokens, 3 * inner :] = att[...]
    for k, (mine, _) in enumerate(orders):
        first = here[x_at[mine] + half : x_at[mine] + half + 1, 0:1].astype(jnp.int32)
        allowed = self_allowed(first, tokens)
        source, target = slice(k * tokens, (k + 1) * tokens), slice((k + 1) * tokens, (k + 2) * tokens)
        every = range(heads)
        lanes = [slice(pair * pair_width, (pair + 1) * pair_width) for pair in range(heads // 2)]
        q, key, value, g = (
            [made[source, n * inner + lane.start : n * inner + lane.stop] for lane in lanes] for n in range(4)
        )
        k_t = [part.astype(f32).T.astype(bf16) for part in key]
        v_t = [part.astype(f32).T.astype(bf16) for part in value]
        q_half = [q[h // 2] * masks[h % 2] for h in every]
        g_half = [g[h // 2] * masks[h % 2] for h in every]
        scores = [jnp.where(allowed, nt(key[h // 2], q_half[h]) + biases[h], masked_value) for h in every]
        weights = [jnp.exp(score - jnp.max(score, 0, keepdims=True)) for score in scores]
        p = [weight * (1.0 / jnp.sum(weight, 0, keepdims=True)) for weight in weights]
        dp = [nt(value[h // 2], g_half[h]) for h in every]
        ds = [(p[h] * (dp[h] - jnp.sum(p[h] * dp[h], 0, keepdims=True))).astype(bf16) for h in every]
        p = [part.astype(bf16) for part in p]
        dk = [nn(ds[h], q_half[h]) for h in every]
        dv = [nn(p[h], g_half[h]) for h in every]
        dq = [nn(k_t[h // 2], ds[h]) for h in every]
        mixed = [nn(v_t[h // 2], p[h]) for h in every]
        for pair, lane in enumerate(lanes):
            a, b = 2 * pair, 2 * pair + 1
            for n, part in enumerate(
                (jnp.where(top, dq[a], dq[b]).T, dk[a] + dk[b], dv[a] + dv[b], jnp.where(top, mixed[a], mixed[b]).T)
            ):
                grads[target, n * inner + lane.start : n * inner + lane.stop] = part.astype(bf16)
    picked = pick_chunks([4 * z + (place & 3) for z in range(4)], rows, width)
    v = x[...].astype(f32)
    own = (v * inverse_rms(v) * gain_row(gain)).astype(bf16)
    left = jnp.concatenate([nt(picked, own), nt(picked, normed)], 1).astype(bf16)
    total[:, : 3 * inner] = nn(left, grads[:, : 3 * inner])
    left = jnp.concatenate([nt(picked, low[...]), nt(picked, low_all)], 1).astype(bf16)
    total[:, 3 * inner :] = nn(left, grads[:, 3 * inner :])
    split_entries(2, lambda i: total[pl.ds(pl.multiple_of(i * rows, 8), rows), :], send_out, keep_out, rows)
    send_out[keep_out.shape[0] :, :] = small[...]


def chunk_of(ref, index, rows):
    return ref[pl.ds(pl.multiple_of(index * rows, 8), rows), :]


def entry_here(step):
    core, bit = lax.axis_index("mp"), own_bit(2)
    return jnp.where(core == 0, 2 * step + bit, 2 * bit + step)


def fold_z(rows, keep, first, out):
    for step in range(2):
        index = entry(2, step, 1 - own_bit(2))
        out[step * rows : (step + 1) * rows, :] = chunk_of(keep, index, rows) + chunk_of(first, index, rows)


def three_sum(rows, step, keep, first, second):
    index = entry_here(step)
    return chunk_of(keep, index, rows) + chunk_of(first, index, rows) + chunk_of(second, step, rows)


def fold_last(rows, keep, first, second, out):
    out[:rows, :] = three_sum(rows, 1 - own_bit(3), keep, first, second)


def four_sum(mine, first, second):
    core = lax.axis_index("mp")
    near = mine + jnp.where(core == 0, first, second[:8])
    return near + (jnp.where(core == 0, second[:8], first) + second[8:])


def finish_cross(rows, keep, first, second, third, q_out, k_out, v_out, o_out):
    inner = q_out.shape[1]
    total = three_sum(rows, own_bit(3), keep, first, second) + third[...]
    for k, out in enumerate((q_out, k_out, v_out, o_out)):
        out[...] = total[:, k * inner : (k + 1) * inner]


def self_fold(rows, keep, sent, first, out):
    step = 1 - own_bit(3)
    out[:rows, :] = chunk_of(keep, step, rows) + chunk_of(first, step, rows)
    out[rows : rows + 8, :] = sent[2 * rows :, :]
    out[rows + 8 :, :] = first[2 * rows :, :]


def small_sum(rows, sent, second, out):
    out[...] = four_sum(sent[rows : rows + 8, :], sent[rows + 8 :, :], second[rows:, :])


def small_pair(mine, first, out):
    stack(out, mine, first)


def finish_self(
    keep, first, second, sent, small, q_out, k_out, v_out, o_out, gain_s, gain_c, gain_f, bias_out
):
    rows, inner = q_out.shape
    step = own_bit(3)
    total = chunk_of(keep, step, rows) + chunk_of(first, step, rows) + second[:rows, :]
    for k, out in enumerate((q_out, k_out, v_out, o_out)):
        out[...] = total[:, k * inner : (k + 1) * inner]
    width = gain_s.shape[0]
    heads, buckets = bias_out.shape
    small = four_sum(sent[:8, :], sent[8:, :], small[...])
    gain_s[...] = small[heads : heads + 1, :width].reshape(width)
    gain_c[...] = small[heads : heads + 1, width : 2 * width].reshape(width)
    gain_f[...] = small[heads + 1 : heads + 2, :width].reshape(width)
    bias_out[...] = small[:heads, :buckets]


def ffn_fold(rows, keep, first, out):
    step = 1 - own_bit(1)
    out[...] = chunk_of(keep, step, rows) + chunk_of(first, step, rows)


def finish_ffn(rows, keep, first, second, in_out, out_out):
    step = own_bit(1)
    total = chunk_of(keep, step, rows) + chunk_of(first, step, rows) + second[...]
    hidden = in_out.shape[1]
    in_out[...] = total[:, :hidden]
    out_out[...] = total[:, hidden:]


def ffn_group(normed, low, act, hid, here, there, w_in, w_out, send_out, keep_out, normed_all, low_all, total):
    tokens, width = normed.shape
    hidden = w_in.shape[1]
    half = tokens // 2
    rows = width // 16
    normed_all[:tokens, :] = normed[...]
    low_all[:tokens, :] = low[...]
    at = tokens
    for source in (here, there):
        for k in range(3):
            low_all[at : at + half, :] = source[2 * k * half : (2 * k + 1) * half, :].astype(bf16)
            normed_all[at : at + half, :] = source[(2 * k + 1) * half : (2 * k + 2) * half, :].astype(bf16)
            at += half
    place, core = place_of()
    first = lax.shift_right_logical(place, 2) * 4
    picked = pick_chunks([first + k for k in range(4)], rows, width)
    left_in = nt(picked, normed_all[...]).astype(bf16)
    left_out = nt(picked, low_all[...]).astype(bf16)
    others_normed, others_low = normed_all[tokens:, :], low_all[tokens:, :]
    chunk = 512 if hidden % 512 == 0 else hidden
    for start in range(0, hidden, chunk):
        cols = slice(start, start + chunk)
        u = nn(others_normed, w_in[:, cols])
        t = jnp.tanh(curve * (u + cubic * (u * u * u)))
        other_act = (0.5 * u * (1.0 + t)).astype(bf16)
        slope = 0.5 * (1.0 + t) + 0.5 * u * (1.0 - t * t) * (curve * (1.0 + 3.0 * cubic * (u * u)))
        other_hid = (nt(others_low, w_out[cols, :]) * slope).astype(bf16)
        total[:, cols] = nn(left_in[:, :tokens], hid[:, cols]) + nn(left_in[:, tokens:], other_hid)
        total[:, hidden + start : hidden + start + chunk] = nn(left_out[:, :tokens], act[:, cols]) + nn(
            left_out[:, tokens:], other_act
        )
    split_entries(0, lambda i: total[pl.ds(pl.multiple_of(i * rows, 8), rows), :], send_out, keep_out, rows)


class Fetched:
    def __init__(self, ref, copy):
        self.ref, self.copy, self.shape, self.dtype = ref, copy, ref.shape, ref.dtype

    def arrive(self):
        if self.copy is not None:
            self.copy.wait()
            self.copy = None

    def __getitem__(self, place):
        self.arrive()
        return self.ref[place]


class Leaving:
    def __init__(self, ref, copy):
        self.ref, self.copy, self.shape, self.dtype = ref, copy, ref.shape, ref.dtype
        self.left = False

    def leave(self):
        if not self.left:
            self.copy.start()
            self.left = True

    def __getitem__(self, place):
        return self.ref[place]

    def __setitem__(self, place, value):
        self.ref[place] = value


SPACES = {"v": pltpu.VMEM, "h": pltpu.HBM, "a": pl.ANY}


def call(kernel, outs, args, scratch=(), after=(), limit=20, cost=1):
    kinds = [kind for _, kind, *_ in args]
    fetched = [k for k, kind in enumerate(kinds) if kind != "v"]
    written = [k for k, (_, _, kind) in enumerate(outs) if kind != "v"]

    def body(*refs):
        ins, rest = list(refs[: len(args)]), refs[len(args) + len(after) :]
        results, rest = list(rest[: len(outs)]), rest[len(outs) :]
        in_bufs, rest = rest[: len(fetched)], rest[len(fetched) :]
        out_bufs, rest = rest[: len(written)], rest[len(written) :]
        extra, rest = rest[: len(scratch)], rest[len(scratch) :]
        sems = rest[0] if rest else None
        waits = []
        for n, (k, buf) in enumerate(zip(fetched, in_bufs)):
            source = ins[k]
            if len(args[k]) > 2:
                source = source.at[pl.ds(args[k][2], buf.shape[0])]
            copy = pltpu.make_async_copy(source, buf, sems.at[n])
            copy.start()
            ins[k] = Fetched(buf, copy)
            waits.append(ins[k])
        leaving = []
        for n, (k, buf) in enumerate(zip(written, out_bufs)):
            results[k] = Leaving(buf, pltpu.make_async_copy(buf, results[k], sems.at[len(fetched) + n]))
            leaving.append(results[k])
        kernel(*ins, *results, *extra)
        for out in leaving:
            out.leave()
        for wait in waits:
            wait.arrive()
        for out in leaving:
            out.copy.wait()

    places = {kind: pl.BlockSpec(memory_space=space) for kind, space in SPACES.items()}
    shapes = [
        pltpu.VMEM((args[k][3:] or args[k][0].shape[:1]) + args[k][0].shape[1:], args[k][0].dtype) for k in fetched
    ]
    shapes += [pltpu.VMEM(outs[k][0], outs[k][1]) for k in written]
    shapes += [pltpu.VMEM(shape, kind) for shape, kind in scratch]
    if fetched or written:
        shapes.append(pltpu.SemaphoreType.DMA((len(fetched) + len(written),)))
    name = getattr(kernel, "__name__", None) or kernel.func.__name__
    return pl.pallas_call(
        body,
        out_shape=[
            pltpu.HBM(shape, kind) if place == "h" else jax.ShapeDtypeStruct(shape, kind) for shape, kind, place in outs
        ],
        in_specs=[places[kind] for kind in kinds] + [places["a"]] * len(after),
        out_specs=[places[kind] for _, _, kind in outs],
        scratch_shapes=shapes,
        compiler_params=pltpu.CompilerParams(vmem_limit_bytes=limit * 1024 * 1024),
        cost_estimate=pl.CostEstimate(flops=cost * 35 * 10**9, transcendentals=0, bytes_accessed=1000),
        name=name,
    )(
        *[
            pltpu.with_memory_space_constraint(value, pltpu.HBM) if kind == "h" else value
            for value, kind, *_ in args
        ],
        *after,
    )


def pair_swap(values):
    return lax.ppermute(values, "mp", [(0, 1), (1, 0)])


def swap_bit(values, bit, count):
    return lax.ppermute(values, "dp", [(k, k ^ (1 << bit)) for k in range(count)])


def stage_swap(values, stage, count):
    bits = ((0, 1), (1, 0), (2, 3), (3, 2))[stage]
    pairs = [(2 * k + core, 2 * (k ^ (1 << bits[core])) + core) for k in range(count) for core in range(2)]
    return lax.ppermute(values, ("dp", "mp"), pairs)


def half_of(values, dim, which):
    return lax.dynamic_index_in_dim(values, which, dim, keepdims=False)


def scatter_sum(blocks, order, count):
    place = lax.axis_index("dp")
    levels = len(order)
    left = list(reversed(range(levels)))
    blocks = blocks.reshape((2,) * levels + blocks.shape[1:])
    for bit in order:
        dim = left.index(bit)
        mine = (place >> bit) & 1
        moved = swap_bit(half_of(blocks, dim, 1 - mine), bit, count)
        blocks = half_of(blocks, dim, mine) + moved
        left.remove(bit)
    return blocks


def full_sum(values, count):
    for bit in range(count.bit_length() - 1):
        values = values + swap_bit(values, bit, count)
    return values


def on_device(
    dec_input, enc_output, dec_lengths, enc_lengths, self_query, self_key, self_value, self_output, self_gain,
    rel_bias, cross_query, cross_key, cross_value, cross_output, cross_gain, ffn_in, ffn_out, ffn_gain, cotangent
):
    slots, width = dec_input.shape[1:]
    steps = enc_output.shape[1]
    inner = self_query.shape[1]
    hidden = ffn_in.shape[1]
    tokens = 3 * slots // 2
    count = lax.axis_size("dp")
    quick = count == 16
    row, half_row = (tokens, width), (tokens // 2, width)
    part_of = (tokens, inner)
    wide = 4 * inner
    share = width // count

    bias_rows = rel_bias.T
    tall = tokens // 2 + 8
    x, low_ffn, qkv, att_self, lse_self, part_self, x_half = call(
        self_forward,
        [(row, bf16, "h"), (row, bf16, "h"), ((tokens, 3 * inner), bf16, "h"), (part_of, bf16, "v"),
         ((8, tokens), f32, "v"), (row, f32, "v"), ((tall, width), f32, "h")],
        [(dec_lengths, "h"), (dec_input, "h"), (self_gain, "h"), (self_query, "h"), (self_key, "h"), (self_value, "h"),
         (cotangent, "h"), (bias_rows, "h"), (self_output, "h")],
    )
    moved_self = pair_swap(part_self)
    if quick:
        x_moved = stage_swap(x_half, 0, count)
    keys, values_t, keys_far, values, keys_t = call(
        encoder_forward,
        [((2 * steps, inner), bf16, "v"), ((inner, 2 * steps), bf16, "v")] + [((2 * steps, inner), bf16, "h")] * 2
        + [((inner, 2 * steps), bf16, "h")],
        [(enc_output, "v"), (cross_key, "v"), (cross_value, "v")],
        after=(part_self,),
    )
    after_self, cross_q, att_cross, lse_cross, part_cross = call(
        cross_forward,
        [(row, f32, "v"), (part_of, bf16, "h"), (part_of, bf16, "v"), ((8, 2 * slots), f32, "v"), (row, f32, "v")],
        [(dec_lengths, "v"), (enc_lengths, "v"), (x, "v"), (part_self, "v"), (moved_self, "v"), (cross_gain, "v"),
         (cross_query, "v"), (cross_output, "v"), (keys, "v"), (values_t, "v")],
    )
    moved_cross = pair_swap(part_cross)
    after = (part_cross,)
    if quick:
        early, own_cross = call(
            pack_early,
            [(row, f32, "v"), ((width // 2, tokens), bf16, "v")],
            [(after_self, "v"), (cross_gain, "v"), (att_cross, "v")],
            after=after,
        )
        early_moved = stage_swap(early, 0, count)
        after = (early,)
    after_cross, normed_ffn, halves, act, hid, back, *x_two = call(
        ffn_both,
        [(row, f32, "v"), (row, bf16, "h"), (row, f32, "v"), ((tokens, hidden), bf16, "v"), ((tokens, hidden), bf16, "v"),
         (row, f32, "v")] + [((2 * tall, width), f32, "v")] * quick,
        [(after_self, "v"), (part_cross, "v"), (moved_cross, "v"), (ffn_gain, "v"), (low_ffn, "v"), (ffn_in, "v"),
         (ffn_out, "v")] + ([(x_half, "v"), (x_moved, "v")] if quick else []),
        after=after,
    )
    moved_back = pair_swap(back)
    if quick:
        group_a = stage_swap(halves, 2, count)
        x_rest = stage_swap(x_two[0], 1, count)
    grad_cross, low_cross, dq, dk, dv, gain_ffn_grad, part_dq = call(
        cross_backward,
        [(row, f32, "h"), (row, bf16, "v"), (part_of, bf16, "v")] + [((2 * steps, inner), bf16, "v")] * 2
        + [((1, width), f32, "v"), (row, f32, "v")],
        [(dec_lengths, "v"), (enc_lengths, "v"), (after_cross, "v"), (back, "v"), (moved_back, "v"), (ffn_gain, "v"),
         (low_ffn, "v"), (cross_output, "v"), (cross_query, "v"), (cross_q, "v"), (keys_far, "v"), (values, "v"),
         (keys_t, "v"), (lse_cross, "v")],
        after=(rest(back),),
    )
    moved_dq = pair_swap(part_dq)
    after = (rest(part_dq), early_moved) if quick else (rest(part_dq),)
    grad_self, low_self, self_half, gain_cross_grad = call(
        self_grad,
        [(row, f32, "v"), (row, bf16, "v"), ((tokens // 2, width), f32, "v"), ((1, width), f32, "v")],
        [(after_self, "v"), (part_dq, "v"), (moved_dq, "v"), (cross_gain, "v"), (grad_cross, "v")],
        after=after,
    )
    after = (low_self,)
    half = width // 2
    if quick:
        self_a = stage_swap(self_half, 0, count)
    dqkv, bias_grad, parts = call(
        back_all,
        [((tokens, 3 * inner), bf16, "v"), ((8, rel_bias.shape[0]), f32, "v"), ((2 * tokens + 2 * steps, width), f32, "v")],
        [(dec_lengths, "v"), (low_self, "v"), (bias_rows, "v"), (self_output, "v"), (self_query, "v"), (self_key, "v"),
         (self_value, "v"), (qkv, "v"), (lse_self, "v"), (dk, "v"), (dv, "v"), (cross_key, "v"), (cross_value, "v"),
         (act, "v"), (ffn_out, "v")],
        after=after,
    )
    parts_moved = pair_swap(parts)
    after = (rest(parts),)
    if quick:
        self_two, halves_two = call(
            collect,
            [(row, f32, "v"), ((2 * tokens, width), f32, "v")],
            [(self_half, "v"), (self_a, "v"), (halves, "v"), (group_a, "v")],
            after=(parts, x_rest),
        )
        self_rest = stage_swap(self_two, 1, count)
        group_rest = stage_swap(halves_two, 3, count)
        late_cross, keep_cross = call(
            cross_weights,
            [((half + tokens, 2 * inner), f32, "v"), ((half, 2 * inner), f32, "h")],
            [(enc_output, "v"), (dk, "v"), (dv, "v"), (dq, "v"), (low_cross, "v")],
            after=(self_two,),
        )
        late_cross_moved = stage_swap(late_cross, 0, count)
        (self_here,) = call(
            gather_self,
            [((3 * tall + 3 * tokens // 2, width), f32, "v")],
            [(x_moved, "v"), (x_rest, "v"), (self_a, "v"), (self_rest, "v")],
            after=(late_cross,),
        )
        self_there = pair_swap(self_here)
        after = (rest(self_here),)
    dec_packed, small = call(
        named(finish_self_norm, rel_bias.shape[1]),
        [(row, bf16, "v"), ((8, wide), f32, "v")],
        [(x, "v"), (parts, "v"), (parts_moved, "v"), (self_gain, "v"), (grad_self, "v"),
         (gain_ffn_grad, "v"), (gain_cross_grad, "v"), (bias_grad, "v")],
        after=after,
    )
    after = (small,)
    if quick:
        send_self, keep_self = call(
            self_group,
            [((2 * share + 8, wide), f32, "v"), ((2 * share, wide), f32, "v")],
            [(x, "v"), (dqkv, "v"), (low_self, "v"), (att_self, "v"), (self_here, "v"), (self_there, "v"),
             (self_gain, "v"), (bias_rows, "v"), (self_query, "v"), (self_key, "v"), (self_value, "v"), (self_output, "v"),
             (small, "v")],
            scratch=[((3 * tokens, wide), bf16), ((4 * tokens, wide), bf16), ((4 * share, wide), f32)],
            after=after,
        )
        self_first = stage_swap(send_self, 2, count)
        after = (send_self,)
    dec_grad, layer_out, enc_grad = call(
        finish_outputs,
        [(dec_input.shape, bf16, "v"), (dec_input.shape, bf16, "v"), (enc_output.shape, bf16, "v")],
        [(dec_lengths, "v"), (dec_packed, "v"), (parts, "v"), (parts_moved, "v"), (after_cross, "v")],
        after=after,
    )
    if not quick:
        return slow_sums(
            locals(), x, after_self, self_gain, cross_gain, rel_bias, enc_output, count
        )
    send_cross, keep_cross = call(
        cross_fold,
        [((half // 2, wide), f32, "v")] * 2,
        [(keep_cross, "h"), (late_cross_moved, "v"), (early_moved, "v"), (own_cross, "v"), (dq, "v"),
         (low_cross, "v"), (att_cross, "v")],
        scratch=[((half, wide), f32)],
        after=(enc_grad,),
    )
    cross_first = stage_swap(send_cross, 1, count)
    (ffn_here,) = call(
        gather_ffn, [((3 * tokens, width), f32, "v")], [(group_a, "v"), (group_rest, "v")], after=(send_cross,)
    )
    ffn_there = pair_swap(ffn_here)
    (send_self2,) = call(
        named(self_fold, share),
        [((share + 16, wide), f32, "v")],
        [(keep_self, "v"), (send_self, "v"), (self_first, "v")],
        after=(ffn_here,),
    )
    self_second = stage_swap(send_self2, 3, count)
    made_ffn, keep_ffn = call(
        ffn_group,
        [((2 * share, 2 * hidden), f32, "v")] * 2,
        [(normed_ffn, "v"), (low_ffn, "v"), (act, "v"), (hid, "v"), (ffn_here, "v"), (ffn_there, "v"), (ffn_in, "v"),
         (ffn_out, "v")],
        scratch=[((4 * tokens, width), bf16), ((4 * tokens, width), bf16), ((4 * share, 2 * hidden), f32)],
        after=(send_self2,),
    )
    (send_cross2,) = call(
        named(fold_z, share),
        [((half // 4, wide), f32, "v")],
        [(keep_cross, "v"), (cross_first, "v")],
        after=(made_ffn,),
    )
    cross_second = stage_swap(send_cross2, 2, count)
    (send_ffn,) = call(relay, [((2 * share, 2 * hidden), f32, "v")], [(made_ffn, "v")], after=(send_cross2,))
    ffn_first = stage_swap(send_ffn, 0, count)
    (small,) = call(
        named(small_sum, share), [((8, wide), f32, "v")], [(send_self2, "v"), (self_second, "v")], after=(send_ffn,)
    )
    small_moved = stage_swap(small, 0, count)
    (send_cross3,) = call(
        named(fold_last, share),
        [((share, wide), f32, "v")],
        [(keep_cross, "v"), (cross_first, "v"), (cross_second, "v")],
        after=(small,),
    )
    cross_third = stage_swap(send_cross3, 3, count)
    (send_ffn,) = call(
        named(ffn_fold, share), [((share, 2 * hidden), f32, "v")], [(keep_ffn, "v"), (ffn_first, "v")], after=(send_cross3,)
    )
    ffn_second = stage_swap(send_ffn, 1, count)
    (send_small,) = call(
        small_pair, [((16, wide), f32, "v")], [(small, "v"), (small_moved, "v")], after=(send_ffn,)
    )
    small_moved = stage_swap(send_small, 1, count)
    *cross_grads, cross_out_grad = call(
        named(finish_cross, share),
        [((share, inner), f32, "h")] * 4,
        [(keep_cross, "v"), (cross_first, "v"), (cross_second, "v"), (cross_third, "v")],
        after=(rest(send_small),),
    )
    *self_grads, self_out_grad, gain_self_sum, gain_cross_sum, gain_ffn_sum, bias_sum = call(
        finish_self,
        [((share, inner), f32, "v")] * 4 + [((width,), f32, "v")] * 3 + [(rel_bias.shape[::-1], f32, "v")],
        [(keep_self, "v"), (self_first, "v"), (self_second, "v"), (send_small, "v"), (small_moved, "v")],
        after=(cross_out_grad,),
    )
    grad_ffn_in, grad_ffn_out = call(
        named(finish_ffn, share),
        [((share, hidden), f32, "h")] * 2,
        [(keep_ffn, "v"), (ffn_first, "v"), (ffn_second, "v")],
        after=(bias_sum,),
    )
    return (
        layer_out,
        dec_grad,
        enc_grad,
        *self_grads,
        self_out_grad.T,
        gain_self_sum,
        bias_sum.T,
        *cross_grads,
        cross_out_grad.T,
        gain_cross_sum,
        grad_ffn_in,
        grad_ffn_out.T,
        gain_ffn_sum,
    )


def rest(made):
    (out,) = call(pause, [((8, 128), f32, "v")], [], after=(made,))
    return out


def named(kernel, *given):
    def run(*refs):
        return kernel(*given, *refs)

    run.__name__ = kernel.__name__
    return run


def slow_sums(made, x, after_self, self_gain, cross_gain, rel_bias, enc_output, count):
    width = x.shape[1]
    heads, buckets = rel_bias.shape[1], rel_bias.shape[0]
    inner = made["dq"].shape[1]
    bits = list(range(count.bit_length() - 1))
    order_a, order_b = bits, bits[1::-1] + bits[2:]

    def scattered(order, *grads):
        parts = [grad.reshape(count, -1, grad.shape[1]) for grad in grads]
        widths = [part.shape[2] for part in parts]
        total = scatter_sum(jnp.concatenate(parts, axis=2), order, count)
        return jnp.split(total, np.cumsum(widths)[:-1].tolist(), axis=1)

    def outer(left, right):
        return jnp.einsum("rm,rn->mn", left, right, preferred_element_type=f32)

    def normed(values, gain):
        return (values * inverse_rms(values) * gain).astype(bf16)

    normed_self = normed(x.astype(f32), self_gain)
    normed_cross = normed(after_self, cross_gain)
    enc_flat = enc_output.reshape(-1, width)
    dqkv = made["dqkv"]
    (grad_ffn_in,) = scattered(order_a, outer(made["normed_ffn"], made["hid"]))
    (grad_ffn_out,) = scattered(order_b, outer(made["low_ffn"], made["act"]))
    cross_query, cross_key = scattered(order_a, outer(normed_cross, made["dq"]), outer(enc_flat, made["dk"]))
    cross_value, cross_output = scattered(
        order_b, outer(enc_flat, made["dv"]), outer(made["low_cross"], made["att_cross"])
    )
    self_query, self_key = scattered(
        order_a, outer(normed_self, dqkv[:, :inner]), outer(normed_self, dqkv[:, inner : 2 * inner])
    )
    self_value, self_output = scattered(
        order_b, outer(normed_self, dqkv[:, 2 * inner :]), outer(made["low_self"], made["att_self"])
    )
    small = full_sum(made["small"], count)
    return (
        made["layer_out"],
        made["dec_grad"],
        made["enc_grad"],
        self_query,
        self_key,
        self_value,
        self_output.T,
        small[heads, :width],
        small[:heads, :buckets].T,
        cross_query,
        cross_key,
        cross_value,
        cross_output.T,
        small[heads, width : 2 * width],
        grad_ffn_in,
        grad_ffn_out.T,
        small[heads + 1, :width],
    )


def solution(mesh):
    in_specs = (
        P("dp", None, None),
        P("dp", None, None),
        P("dp", None),
        P("dp", None),
        P(None, "mp"),
        P(None, "mp"),
        P(None, "mp"),
        P("mp", None),
        P(),
        P(None, "mp"),
        P(None, "mp"),
        P(None, "mp"),
        P(None, "mp"),
        P("mp", None),
        P(),
        P(None, "mp"),
        P("mp", None),
        P(),
        P("dp", None, None),
    )
    out_specs = (
        P("dp", None, None),
        P("dp", None, None),
        P("dp", None, None),
        P("dp", "mp"),
        P("dp", "mp"),
        P("dp", "mp"),
        P("mp", "dp"),
        P(),
        P(None, "mp"),
        P("dp", "mp"),
        P("dp", "mp"),
        P("dp", "mp"),
        P("mp", "dp"),
        P(),
        P("dp", "mp"),
        P("mp", "dp"),
        P(),
    )
    return jax.shard_map(
        on_device, mesh=mesh, in_specs=in_specs, out_specs=out_specs, check_vma=False
    )
```

```python
import functools

import jax
import jax.numpy as jnp
import numpy as np
from jax import lax
from jax.experimental import pallas as pl
from jax.experimental.pallas import tpu as pltpu
from jax.sharding import PartitionSpec as P

epsilon = 1e-06
masked_value = -1e30
head_width = 64
pair_width = 2 * head_width
bf16 = jnp.bfloat16
f32 = jnp.float32
curve = 0.7978845608028654
cubic = 0.044715


def nn(left, right, precision=None):
    return lax.dot_general(
        left, right, (((1,), (0,)), ((), ())), precision=precision, preferred_element_type=f32
    )


def nt(left, right, precision=None):
    return lax.dot_general(
        left, right, (((1,), (1,)), ((), ())), precision=precision, preferred_element_type=f32
    )


def tn(left, right, precision=None):
    return lax.dot_general(
        left, right, (((0,), (0,)), ((), ())), precision=precision, preferred_element_type=f32
    )


def gain_row(gain):
    return gain[...].reshape(1, gain.shape[0])


def iota(shape, dim):
    return lax.broadcasted_iota(jnp.int32, shape, dim)


def inverse_rms(values):
    return lax.rsqrt(jnp.sum(values * values, -1, keepdims=True) / values.shape[-1] + epsilon)


def norm_back(values, gain, upstream):
    inverse = inverse_rms(values)
    scaled = upstream * gain
    mean = jnp.sum(scaled * values, -1, keepdims=True) / values.shape[-1]
    gain_grad = jnp.sum(upstream * values * inverse, 0, keepdims=True)
    return inverse * scaled - values * (inverse * inverse * inverse * mean), gain_grad


def bucket_bounds(buckets):
    half = buckets // 2
    return [int(b) for b in np.ceil(16.0 * 8.0 ** (np.arange(1, half) / half))]


def bucket_rows(buckets, width):
    distance = iota((buckets, width), 1)
    coarse = jnp.full((buckets, width), buckets // 2, jnp.int32)
    for bound in bucket_bounds(buckets):
        coarse += (distance >= bound).astype(jnp.int32)
    chosen = jnp.where(distance < buckets // 2, distance, coarse)
    return (chosen == iota((buckets, width), 0)).astype(f32)


def half_masks():
    lane = iota((1, pair_width), 1)
    low = (lane < head_width).astype(f32)
    return low.astype(bf16), (1.0 - low).astype(bf16)


def pick_rows(first, tokens, slots):
    row, col = iota((tokens, 2 * slots), 0), iota((tokens, 2 * slots), 1)
    return (col == jnp.where(row < first, row, row + (slots - first))).astype(f32).astype(bf16)


def self_bias(bias_ref, width):
    return nn(
        bias_ref[...], bucket_rows(bias_ref.shape[1], width), precision=lax.Precision.HIGHEST
    )


def self_allowed(first, tokens):
    key, query = iota((tokens, tokens), 0), iota((tokens, tokens), 1)
    return (key <= query) & ((key < first) == (query < first))


def spread_bias(base, head, tokens):
    width = base.shape[1]
    rows = jnp.broadcast_to(base[head : head + 1], (tokens, width))
    return pltpu.roll(rows, 0, 1, stride=1, stride_axis=0)[:, :tokens]


def own_half(values):
    half = values.shape[0] // 2
    return jnp.where(lax.axis_index("mp") == 0, values[:half], values[half:])


def flush(out):
    if isinstance(out, Leaving):
        out.leave()


def self_forward(
    dec_len, dec, gain, w_q, w_k, w_v, cot, bias, w_o, x_out, low_out, qkv_out, att_out, lse_out, part_out, x_half
):
    slots, width = dec.shape[1], dec.shape[2]
    tokens = x_out.shape[0]
    heads = bias.shape[0]
    first = dec_len[:, 0:1]
    picked = pick_rows(first, tokens, slots)
    x = nn(picked, dec[...].reshape(2 * slots, width))
    x_out[...] = x.astype(bf16)
    flush(x_out)
    half = tokens // 2
    x_half[:half, :] = own_half(x)
    x_half[half:, :] = jnp.broadcast_to(first.astype(f32), (8, width))
    flush(x_half)
    normed = (x * inverse_rms(x) * gain_row(gain)).astype(bf16)
    inner = w_q.shape[1]
    for k, w in enumerate((w_q, w_k, w_v)):
        qkv_out[:, k * inner : (k + 1) * inner] = nn(normed, w[...]).astype(bf16)
    flush(qkv_out)
    low_out[...] = nn(picked, cot[...].reshape(2 * slots, width)).astype(bf16)
    flush(low_out)
    base = self_bias(bias, 2 * slots)
    allowed = self_allowed(first, tokens)
    masks = half_masks()
    top = iota((pair_width, tokens), 0) < head_width
    lse_out[...] = jnp.zeros_like(lse_out)
    for pair in range(heads // 2):
        lanes = slice(pair * pair_width, (pair + 1) * pair_width)
        q = qkv_out[:, lanes]
        k = qkv_out[:, inner + pair * pair_width : inner + (pair + 1) * pair_width]
        v = qkv_out[:, 2 * inner + pair * pair_width : 2 * inner + (pair + 1) * pair_width]
        v_t = v.astype(f32).T.astype(bf16)
        mixed = []
        for side in range(2):
            head = 2 * pair + side
            scores = nt(k, q * masks[side]) + spread_bias(base, head, tokens)
            scores = jnp.where(allowed, scores, masked_value)
            top_score = jnp.max(scores, 0, keepdims=True)
            weights = jnp.exp(scores - top_score)
            total = jnp.sum(weights, 0, keepdims=True)
            lse_out[head : head + 1, :] = top_score + jnp.log(total)
            mixed.append(nn(v_t, (weights * (1.0 / total)).astype(bf16)))
        att_out[:, lanes] = jnp.where(top, mixed[0], mixed[1]).T.astype(bf16)
    flush(att_out)
    flush(lse_out)
    part_out[...] = nn(att_out[...], w_o[...])


def encoder_forward(enc, w_k, w_v, k_out, vt_out, k_far, v_far, kt_far):
    steps = enc.shape[1]
    for w, out, out_t in ((w_v, v_far, vt_out), (w_k, k_out, kt_far)):
        for e in range(enc.shape[0]):
            rows = slice(e * steps, (e + 1) * steps)
            made = nn(enc[e], w[...])
            out[rows, :] = made.astype(bf16)
            out_t[:, rows] = made.T.astype(bf16)
        if out is v_far:
            flush(v_far)
    k_far[...] = k_out[...]


def cross_rows(first, tokens, slots, e):
    row = iota((slots, 1), 0) + e * (tokens - slots)
    return row < first if e == 0 else row >= first


def cross_forward(
    dec_len, enc_len, x, part, moved, gain, w_q, w_o, k_in, vt_in, after_out, q_out, att_out, lse_out, part_out
):
    tokens = x.shape[0]
    slots = 2 * tokens // 3
    steps = k_in.shape[0] // 2
    first = dec_len[:, 0:1]
    after = x[...].astype(f32) + (part[...] + moved[...])
    after_out[...] = after
    normed = (after * inverse_rms(after) * gain_row(gain)).astype(bf16)
    q_out[...] = nn(normed, w_q[...]).astype(bf16)
    flush(q_out)
    masks = half_masks()
    top = iota((pair_width, slots), 0) < head_width
    own = iota((tokens, 1), 0) < first
    lse_out[...] = jnp.zeros_like(lse_out)
    shift = tokens - slots
    for pair in range(q_out.shape[1] // pair_width):
        lanes = slice(pair * pair_width, (pair + 1) * pair_width)
        parts = []
        for e in range(2):
            q = q_out[e * shift : e * shift + slots, lanes]
            both = jnp.concatenate([q * masks[0], q * masks[1]], 0)
            scores = nt(k_in[e * steps : (e + 1) * steps, lanes], both)
            valid = iota((steps, 1), 0) < enc_len[:, e : e + 1]
            scores = jnp.where(valid, scores, masked_value)
            top_score = jnp.max(scores, 0, keepdims=True)
            weights = jnp.exp(scores - top_score)
            total = jnp.sum(weights, 0, keepdims=True)
            lse_out[2 * pair + e : 2 * pair + e + 1, :] = top_score + jnp.log(total)
            mixed = nn(
                vt_in[lanes, e * steps : (e + 1) * steps], (weights * (1.0 / total)).astype(bf16)
            )
            parts.append(jnp.where(top, mixed[:, :slots], mixed[:, slots:]).T)
        fill = jnp.zeros((shift, pair_width), f32)
        att_out[:, lanes] = jnp.where(
            own, jnp.concatenate([parts[0], fill], 0), jnp.concatenate([fill, parts[1]], 0)
        ).astype(bf16)
    flush(lse_out)
    part_out[...] = nn(att_out[...], w_o[...])


def ffn_both(
    after, part, moved, gain, low, w_in, w_out, *outs
):
    if len(outs) > 6:
        x_half, x_moved, *outs, x_rest = outs
        stack(x_rest, x_half, x_moved)
    after_out, normed_out, halves_out, act_out, hid_out, back_out = outs
    total = after[...] + (part[...] + moved[...])
    after_out[...] = total
    normed = (total * inverse_rms(total) * gain_row(gain)).astype(bf16)
    normed_out[...] = normed
    flush(normed_out)
    low_in = low[...]
    half = low_in.shape[0] // 2
    halves_out[:half, :] = own_half(low_in.astype(f32))
    halves_out[half:, :] = own_half(normed.astype(f32))
    hidden = w_in.shape[1]
    chunk = 512 if hidden % 512 == 0 else hidden
    for start in range(0, hidden, chunk):
        cols = slice(start, start + chunk)
        u = nn(normed, w_in[:, cols])
        t = jnp.tanh(curve * (u + cubic * (u * u * u)))
        act = (0.5 * u * (1.0 + t)).astype(bf16)
        slope = 0.5 * (1.0 + t) + 0.5 * u * (1.0 - t * t) * (curve * (1.0 + 3.0 * cubic * (u * u)))
        hid = (nt(low_in, w_out[cols, :]) * slope).astype(bf16)
        act_out[:, cols] = act
        hid_out[:, cols] = hid
        backward = nt(hid, w_in[:, cols])
        if start == 0:
            back_out[...] = backward
        else:
            back_out[...] += backward


def cross_backward(
    dec_len, enc_len, after, part, moved, gain, low, w_o, w_q, q_in, k_in, v_in, kt_in, lse,
    grad_out, low_out, dq_out, dk_out, dv_out, gain_out, part_out
):
    tokens = after.shape[0]
    slots = 2 * tokens // 3
    steps = k_in.shape[0] // 2
    first = dec_len[:, 0:1]
    shift = tokens - slots
    norm_in, gain_grad = norm_back(after[...], gain_row(gain), part[...] + moved[...])
    gain_out[...] = gain_grad
    flush(gain_out)
    grad = low[...].astype(f32) + norm_in
    grad_out[...] = grad
    flush(grad_out)
    low_grad = grad.astype(bf16)
    low_out[...] = low_grad
    flush(low_out)
    g_all = nt(low_grad, w_o[...])
    masks = half_masks()
    top = iota((pair_width, slots), 0) < head_width
    for pair in range(q_in.shape[1] // pair_width):
        lanes = slice(pair * pair_width, (pair + 1) * pair_width)
        parts = []
        for e in range(2):
            keys = slice(e * steps, (e + 1) * steps)
            window = slice(e * shift, e * shift + slots)
            q = q_in[window, lanes]
            g = jnp.where(cross_rows(first, tokens, slots, e), g_all[window, lanes], 0.0)
            g = g.astype(bf16)
            q_both = jnp.concatenate([q * masks[0], q * masks[1]], 0)
            g_both = jnp.concatenate([g * masks[0], g * masks[1]], 0)
            valid = iota((steps, 1), 0) < enc_len[:, e : e + 1]
            scores = jnp.where(valid, nt(k_in[keys, lanes], q_both), masked_value)
            p = jnp.exp(scores - lse[2 * pair + e : 2 * pair + e + 1, :])
            dp = nt(v_in[keys, lanes], g_both)
            ds = (p * (dp - jnp.sum(p * dp, 0, keepdims=True))).astype(bf16)
            dk_out[keys, lanes] = nn(ds, q_both).astype(bf16)
            dv_out[keys, lanes] = nn(p.astype(bf16), g_both).astype(bf16)
            dq = nn(kt_in[lanes, keys], ds)
            parts.append(jnp.where(top, dq[:, :slots], dq[:, slots:]).T)
        fill = jnp.zeros((shift, pair_width), f32)
        dq_out[:, lanes] = (
            jnp.concatenate([parts[0], fill], 0) + jnp.concatenate([fill, parts[1]], 0)
        ).astype(bf16)
    part_out[...] = nt(dq_out[...], w_q[...])


def self_grad(after, part, moved, gain, grad_in, grad_out, low_out, half_out, gain_out):
    norm_in, gain_grad = norm_back(after[...], gain_row(gain), part[...] + moved[...])
    gain_out[...] = gain_grad
    grad = grad_in[...] + norm_in
    grad_out[...] = grad
    low = grad.astype(bf16)
    low_out[...] = low
    half_out[...] = own_half(low.astype(f32))


def back_all(
    dec_len, low, bias, w_o, w_q, w_k, w_v, qkv, lse, dk, dv, w_ck, w_cv, act, w_ffn, dqkv_out, bias_out, part_out
):
    tokens = low.shape[0]
    self_backward(
        dec_len, low, bias, w_o, w_q, w_k, w_v, qkv, lse, dqkv_out, bias_out, part_out.at[pl.ds(0, tokens), :]
    )
    part_out[tokens : 2 * tokens, :] = nn(act[...], w_ffn[...])
    steps = dk.shape[0] // 2
    for e in range(2):
        rows = slice(e * steps, (e + 1) * steps)
        part_out[2 * tokens + e * steps : 2 * tokens + (e + 1) * steps, :] = nt(dk[rows, :], w_ck[...]) + nt(
            dv[rows, :], w_cv[...]
        )


def self_backward(dec_len, low, bias, w_o, w_q, w_k, w_v, qkv, lse, dqkv_out, bias_out, part_out):
    tokens = low.shape[0]
    heads = bias.shape[0]
    first = dec_len[:, 0:1]
    inner = w_q.shape[1]
    g_all = nt(low[...], w_o[...]).astype(bf16)
    reach = 4 * tokens // 3
    base = self_bias(bias, reach)
    allowed = self_allowed(first, tokens)
    masks = half_masks()
    top = iota((pair_width, tokens), 0) < head_width
    diagonals = []
    for pair in range(heads // 2):
        lanes = slice(pair * pair_width, (pair + 1) * pair_width)
        k_lanes = slice(inner + pair * pair_width, inner + (pair + 1) * pair_width)
        v_lanes = slice(2 * inner + pair * pair_width, 2 * inner + (pair + 1) * pair_width)
        q, k, v, g = qkv[:, lanes], qkv[:, k_lanes], qkv[:, v_lanes], g_all[:, lanes]
        k_t = k.astype(f32).T.astype(bf16)
        dk, dv, dq = 0.0, 0.0, []
        for side in range(2):
            head = 2 * pair + side
            q_half, g_half = q * masks[side], g * masks[side]
            scores = nt(k, q_half) + spread_bias(base, head, tokens)
            scores = jnp.where(allowed, scores, masked_value)
            p = jnp.exp(scores - lse[head : head + 1, :])
            dp = nt(v, g_half)
            ds = p * (dp - jnp.sum(p * dp, 0, keepdims=True))
            ds_low = ds.astype(bf16)
            dk += nn(ds_low, q_half)
            dv += nn(p.astype(bf16), g_half)
            dq.append(nn(k_t, ds_low))
            wide = jnp.concatenate([ds, jnp.zeros((tokens, reach - tokens), f32)], 1)
            total = wide[:8]
            for start in range(8, tokens, 8):
                total += pltpu.roll(wide[start : start + 8], reach - start, 1)
            diagonals.append(total)
        dqkv_out[:, lanes] = jnp.where(top, dq[0], dq[1]).T.astype(bf16)
        dqkv_out[:, k_lanes] = dk.astype(bf16)
        dqkv_out[:, v_lanes] = dv.astype(bf16)
    flush(dqkv_out)
    part_out[...] = (
        nt(dqkv_out[:, :inner], w_q[...])
        + nt(dqkv_out[:, inner : 2 * inner], w_k[...])
        + nt(dqkv_out[:, 2 * inner :], w_v[...])
    )
    total = jnp.concatenate(diagonals, 0)
    row = iota(total.shape, 0) & 7
    lined = jnp.zeros_like(total)
    for s in range(8):
        lined += jnp.where(row == s, pltpu.roll(total, (reach - s) % reach, 1), 0.0)
    head_of = ((iota((8, 8 * heads), 1) >> 3) == iota((8, 8 * heads), 0)).astype(f32)
    by_head = nn(head_of, lined, precision=lax.Precision.HIGHEST)
    bias_out[...] = nt(by_head, bucket_rows(bias.shape[1], reach), precision=lax.Precision.HIGHEST)


def unpacked(values, first, slots):
    tokens = values.shape[0]
    slot, row = iota((2 * slots, tokens), 0), iota((2 * slots, tokens), 1)
    limit = jnp.where(slot < slots, first, slots + tokens - first)
    wanted = jnp.where(slot < slots, slot, slot - slots + first)
    spread = ((row == wanted) & (slot < limit)).astype(f32).astype(bf16)
    return nn(spread, values.astype(bf16)).astype(bf16)


def finish_self_norm(
    heads, x, part, moved, gain, grad_in, gain_ffn, gain_cross, bias_grad, dec_out, small_out
):
    tokens, width = x.shape
    norm_in, gain_grad = norm_back(x[...].astype(f32), gain_row(gain), part[:tokens, :] + moved[:tokens, :])
    half, buckets = small_out.shape[1], bias_grad.shape[1]
    small_out[...] = jnp.zeros_like(small_out)
    for k, value in enumerate((gain_grad, gain_cross[...], gain_ffn[...])):
        small_out[2 * k : 2 * k + 1, :] = value[:, :half]
        small_out[2 * k + 1 : 2 * k + 2, :] = value[:, half:]
    small_out[6:7, : heads * buckets] = jnp.concatenate([bias_grad[h : h + 1, :] for h in range(heads)], 1)
    dec_out[...] = (grad_in[...] + norm_in).astype(bf16)


def finish_outputs(dec_len, dec, part, moved, after, dec_out, layer_out, enc_out, token):
    token[...] = jnp.zeros_like(token)
    tokens = dec.shape[0]
    first, slots = dec_len[:, 0:1], dec_out.shape[1]
    dec_out[...] = unpacked(dec[...], first, slots).reshape(dec_out.shape)
    total = after[...] + (part[tokens : 2 * tokens, :] + moved[tokens : 2 * tokens, :])
    layer_out[...] = unpacked(total, first, slots).reshape(layer_out.shape)
    enc_out[...] = (part[2 * tokens :, :] + moved[2 * tokens :, :]).astype(bf16).reshape(enc_out.shape)


def pause(out):
    out[...] = jnp.zeros_like(out)


def collect(low_half, low_a, halves, group_a, low_out, group_out):
    stack(low_out, low_half, low_a)
    stack(group_out, halves, group_a)


def gather_self(x_moved, x_rest, low_a, low_rest, out):
    stack(out, x_moved, x_rest, low_a, low_rest)


def relay(value, out):
    out[...] = value[...]


def gather_ffn(group_a, group_rest, out):
    stack(out, group_a, group_rest)


def place_of():
    return lax.axis_index("dp"), lax.axis_index("mp")


def own_bit(stage):
    place, core = place_of()
    shift = (core, 1 - core, 2 + core, 3 - core)[stage]
    return lax.shift_right_logical(place, shift) & 1


def entry(stage, step, bit):
    if stage % 2:
        return 2 * step + bit
    core = lax.axis_index("mp")
    return jnp.where(core == 0, 2 * step + bit, (step // 2) * 4 + 2 * bit + step % 2)


def pick_chunks(chunks, rows, width):
    gap = iota((rows, width), 1) - iota((rows, width), 0)
    return jnp.concatenate([(gap == chunk * rows).astype(f32) for chunk in chunks], 0).astype(bf16)


def half_pick(other, width):
    bit = own_bit(0)
    bit = 1 - bit if other else bit
    return pick_chunks([entry(0, step, bit) for step in range(8)], width // 16, width)


def fold_lanes(values):
    half = values.shape[0] // 2
    return jnp.concatenate([values[:half], values[half:]], 1)


def unfold_lanes(values):
    half = values.shape[1] // 2
    return jnp.concatenate([values[:, :half], values[:, half:]], 0)


def split_entries(stage, source, send_out, keep_out, rows):
    bit = own_bit(stage)
    for step in range(keep_out.shape[0] // rows):
        here = slice(step * rows, (step + 1) * rows)
        send_out[here, :] = source(entry(stage, step, 1 - bit))
        keep_out[here, :] = source(entry(stage, step, bit))


def pack_early(after, gain, att, early_out, own):
    width = after.shape[1]
    inner = att.shape[1]
    v = after[...]
    normed = (v * inverse_rms(v) * gain_row(gain)).astype(bf16)
    own[...] = nt(half_pick(0, width), normed).astype(bf16)
    early_out[:, :inner] = fold_lanes(nt(half_pick(1, width), normed))
    early_out[:, inner:] = att[...].astype(f32)


def stack(out, *parts):
    at = 0
    for part in parts:
        out[at : at + part.shape[0], :] = part[...]
        at += part.shape[0]


def cross_weights(enc, dk, dv, dq, low, late_out):
    steps, width = enc.shape[1:]
    inner = dk.shape[1]
    half = width // 2
    left = nt(half_pick(1, width), enc[...].reshape(2 * steps, width)).astype(bf16)
    late_out[:half, :inner] = nn(left, dk[...])
    late_out[:half, inner:] = nn(left, dv[...])
    late_out[half:, :inner] = dq[...].astype(f32)
    late_out[half:, inner:] = fold_lanes(nt(half_pick(1, width), low[...]))


def cross_keep(enc, dk, dv, keep_out):
    steps, width = enc.shape[1:]
    inner = dk.shape[1]
    left = nt(half_pick(0, width), enc[...].reshape(2 * steps, width)).astype(bf16)
    keep_out[:, :inner] = nn(left, dk[...])
    keep_out[:, inner:] = nn(left, dv[...])


def side_by_side(out, at, small):
    n = small.shape[1]
    out[at:, :n] = small[:8, :]
    out[at:, n : 2 * n] = small[8:, :]
    out[at:, 2 * n :] = jnp.zeros_like(out[at:, 2 * n :])


def above(rows, n):
    return jnp.concatenate([rows[:, :n], rows[:, n : 2 * n]], 0)


def cross_fold(keep, moved, early, own, dq, low, att, small, small_moved, send_out, keep_out, small_out, total):
    width = low.shape[1]
    half, inner = own.shape[0], dq.shape[1]
    rows = width // 16
    total[:, :inner] = nn(own[...], dq[...]) + nn(
        unfold_lanes(early[:, :inner]).astype(bf16), moved[half:, :inner].astype(bf16)
    )
    total[:, 3 * inner :] = nn(nt(half_pick(0, width), low[...]).astype(bf16), att[...]) + nn(
        unfold_lanes(moved[half:, inner:]).astype(bf16), early[:, inner:].astype(bf16)
    )
    total[:, inner : 3 * inner] = keep[...] + moved[:half, :]
    split_entries(1, lambda i: total[pl.ds(pl.multiple_of(i * rows, 8), rows), :], send_out, keep_out, rows)
    stack(small_out, small, small_moved)
    side_by_side(send_out, keep_out.shape[0], small_out)


def self_group(
    x, dqkv, low, att, here, there, gain, bias, w_q, w_k, w_v, w_o,
    send_out, keep_out, made, grads, total
):
    tokens, width = x.shape
    inner = att.shape[1]
    heads = bias.shape[0]
    half = tokens // 2
    place, core = place_of()
    rows = width // 16
    base = self_bias(bias, 4 * tokens // 3)
    masks = half_masks()
    top = iota((pair_width, tokens), 0) < head_width
    biases = [spread_bias(base, head, tokens) for head in range(heads)]
    tall = half + 8
    x_at, low_at = (0, tall, 2 * tall), (3 * tall, 3 * tall + half, 3 * tall + 2 * half)
    orders = ((0, 1), (1, 0), (2, 2))

    def joined(starts, mine, other):
        a, b = here[starts[mine] : starts[mine] + half, :], there[starts[other] : starts[other] + half, :]
        return [jnp.where(core == 0, a, b), jnp.where(core == 0, b, a)]

    v = jnp.concatenate([part for order in orders for part in joined(x_at, *order)], 0)
    normed = (v * inverse_rms(v) * gain_row(gain)).astype(bf16)
    low_all = jnp.concatenate([part for order in orders for part in joined(low_at, *order)], 0).astype(bf16)
    for k, w in enumerate((w_q, w_k, w_v)):
        made[:, k * inner : (k + 1) * inner] = nn(normed, w[...]).astype(bf16)
    made[:, 3 * inner :] = nt(low_all, w_o[...]).astype(bf16)
    grads[:tokens, : 3 * inner] = dqkv[...]
    grads[:tokens, 3 * inner :] = att[...]
    def one_chip(k, carry):
        first = here[pl.ds(pl.multiple_of(k * tall + half, 8), 8), :][0:1, 0:1].astype(jnp.int32)
        allowed = self_allowed(first, tokens)
        source = pl.ds(pl.multiple_of(k * tokens, 16), tokens)
        target = pl.ds(pl.multiple_of((k + 1) * tokens, 16), tokens)
        every = range(heads)
        lanes = [slice(pair * pair_width, (pair + 1) * pair_width) for pair in range(heads // 2)]
        q, key, value, g = (
            [made[source, n * inner + lane.start : n * inner + lane.stop] for lane in lanes] for n in range(4)
        )
        k_t = [part.astype(f32).T.astype(bf16) for part in key]
        v_t = [part.astype(f32).T.astype(bf16) for part in value]
        q_half = [q[h // 2] * masks[h % 2] for h in every]
        g_half = [g[h // 2] * masks[h % 2] for h in every]
        scores = [jnp.where(allowed, nt(key[h // 2], q_half[h]) + biases[h], masked_value) for h in every]
        weights = [jnp.exp(score - jnp.max(score, 0, keepdims=True)) for score in scores]
        p = [weight * (1.0 / jnp.sum(weight, 0, keepdims=True)) for weight in weights]
        dp = [nt(value[h // 2], g_half[h]) for h in every]
        ds = [(p[h] * (dp[h] - jnp.sum(p[h] * dp[h], 0, keepdims=True))).astype(bf16) for h in every]
        p = [part.astype(bf16) for part in p]
        dk = [nn(ds[h], q_half[h]) for h in every]
        dv = [nn(p[h], g_half[h]) for h in every]
        dq = [nn(k_t[h // 2], ds[h]) for h in every]
        mixed = [nn(v_t[h // 2], p[h]) for h in every]
        for pair, lane in enumerate(lanes):
            a, b = 2 * pair, 2 * pair + 1
            for n, part in enumerate(
                (jnp.where(top, dq[a], dq[b]).T, dk[a] + dk[b], dv[a] + dv[b], jnp.where(top, mixed[a], mixed[b]).T)
            ):
                grads[target, n * inner + lane.start : n * inner + lane.stop] = part.astype(bf16)
        return carry

    lax.fori_loop(0, 3, one_chip, 0)
    picked = pick_chunks([4 * z + (place & 3) for z in range(4)], rows, width)
    v = x[...].astype(f32)
    own = (v * inverse_rms(v) * gain_row(gain)).astype(bf16)
    left = jnp.concatenate([nt(picked, own), nt(picked, normed)], 1).astype(bf16)
    total[:, : 3 * inner] = nn(left, grads[:, : 3 * inner])
    left = jnp.concatenate([nt(picked, low[...]), nt(picked, low_all)], 1).astype(bf16)
    total[:, 3 * inner :] = nn(left, grads[:, 3 * inner :])
    split_entries(2, lambda i: total[pl.ds(pl.multiple_of(i * rows, 8), rows), :], send_out, keep_out, rows)


def chunk_of(ref, index, rows):
    return ref[pl.ds(pl.multiple_of(index * rows, 8), rows), :]


def entry_here(step):
    core, bit = lax.axis_index("mp"), own_bit(2)
    return jnp.where(core == 0, 2 * step + bit, 2 * bit + step)


def fold_z(rows, keep, small, first, out, small_out):
    for step in range(2):
        index = entry(2, step, 1 - own_bit(2))
        out[step * rows : (step + 1) * rows, :] = chunk_of(keep, index, rows) + chunk_of(first, index, rows)
    n = small.shape[1]
    total = four_sum(small[:8, :], small[8:, :], above(first[keep.shape[0] :, : 2 * n], n))
    small_out[...] = total
    out[2 * rows :, :n] = total
    out[2 * rows :, n:] = jnp.zeros_like(out[2 * rows :, n:])


def three_sum(rows, step, keep, first, second):
    index = entry_here(step)
    return chunk_of(keep, index, rows) + chunk_of(first, index, rows) + chunk_of(second, step, rows)


def fold_last(rows, keep, small, first, second, out, small_out):
    out[:rows, :] = three_sum(rows, 1 - own_bit(3), keep, first, second)
    small_out[:8, :] = small[...]
    small_out[8:, :] = second[2 * rows :, : small.shape[1]]
    side_by_side(out, rows, small_out)


def four_sum(mine, first, second):
    core = lax.axis_index("mp")
    near = mine + jnp.where(core == 0, first, second[:8])
    return near + (jnp.where(core == 0, second[:8], first) + second[8:])


def finish_cross(
    heads, rows, keep, first, second, sums, third, q_out, k_out, v_out, o_out, gain_s, gain_c, gain_f, bias_out, token
):
    token[...] = jnp.zeros_like(token)
    inner = q_out.shape[1]
    total = three_sum(rows, own_bit(3), keep, first, second) + third[:rows, :]
    for k, out in enumerate((q_out, k_out, v_out, o_out)):
        out[...] = total[:, k * inner : (k + 1) * inner]
    width, buckets, n = gain_s.shape[0], bias_out.shape[1], sums.shape[1]
    small = four_sum(sums[:8, :], sums[8:, :], above(third[rows:, : 2 * n], n))
    for k, out in enumerate((gain_s, gain_c, gain_f)):
        out[...] = jnp.concatenate([small[2 * k : 2 * k + 1, :], small[2 * k + 1 : 2 * k + 2, :]], 1).reshape(width)
    bias_out[...] = jnp.concatenate([small[6:7, h * buckets : (h + 1) * buckets] for h in range(heads)], 0)


def self_fold(rows, keep, first, out):
    step = 1 - own_bit(3)
    out[...] = chunk_of(keep, step, rows) + chunk_of(first, step, rows)


def finish_self(rows, keep, first, second, q_out, k_out, v_out, o_out, token):
    token[...] = jnp.zeros_like(token)
    inner = q_out.shape[1]
    step = own_bit(3)
    total = chunk_of(keep, step, rows) + chunk_of(first, step, rows) + second[...]
    for k, out in enumerate((q_out, k_out, v_out, o_out)):
        out[...] = total[:, k * inner : (k + 1) * inner]


def ffn_fold(rows, keep, first, out):
    step = 1 - own_bit(1)
    out[...] = chunk_of(keep, step, rows) + chunk_of(first, step, rows)


def finish_ffn(rows, keep, first, second, in_out, out_out):
    step = own_bit(1)
    total = chunk_of(keep, step, rows) + chunk_of(first, step, rows) + second[...]
    hidden = in_out.shape[1]
    in_out[...] = total[:, :hidden]
    out_out[...] = total[:, hidden:]


def ffn_group(normed, low, act, hid, here, there, w_in, w_out, send_out, keep_out, normed_all, low_all, total):
    tokens, width = normed.shape
    hidden = w_in.shape[1]
    half = tokens // 2
    rows = width // 16
    normed_all[:tokens, :] = normed[...]
    low_all[:tokens, :] = low[...]
    at = tokens
    for source in (here, there):
        for k in range(3):
            low_all[at : at + half, :] = source[2 * k * half : (2 * k + 1) * half, :].astype(bf16)
            normed_all[at : at + half, :] = source[(2 * k + 1) * half : (2 * k + 2) * half, :].astype(bf16)
            at += half
    place, core = place_of()
    first = lax.shift_right_logical(place, 2) * 4
    picked = pick_chunks([first + k for k in range(4)], rows, width)
    left_in = nt(picked, normed_all[...]).astype(bf16)
    left_out = nt(picked, low_all[...]).astype(bf16)
    chunk = 512 if hidden % 512 == 0 else hidden

    def one_chunk(k, carry):
        cols = pl.ds(pl.multiple_of(k * chunk, 128), chunk)
        u = nn(normed_all[tokens:, :], w_in[:, cols])
        t = jnp.tanh(curve * (u + cubic * (u * u * u)))
        other_act = (0.5 * u * (1.0 + t)).astype(bf16)
        slope = 0.5 * (1.0 + t) + 0.5 * u * (1.0 - t * t) * (curve * (1.0 + 3.0 * cubic * (u * u)))
        other_hid = (nt(low_all[tokens:, :], w_out[cols, :]) * slope).astype(bf16)
        total[:, cols] = nn(left_in[:, :tokens], hid[:, cols]) + nn(left_in[:, tokens:], other_hid)
        total[:, pl.ds(pl.multiple_of(hidden + k * chunk, 128), chunk)] = nn(
            left_out[:, :tokens], act[:, cols]
        ) + nn(left_out[:, tokens:], other_act)
        return carry

    lax.fori_loop(0, hidden // chunk, one_chunk, 0)
    split_entries(0, lambda i: total[pl.ds(pl.multiple_of(i * rows, 8), rows), :], send_out, keep_out, rows)


class Fetched:
    def __init__(self, ref, copy):
        self.ref, self.copy, self.shape, self.dtype = ref, copy, ref.shape, ref.dtype

    def arrive(self):
        if self.copy is not None:
            self.copy.wait()
            self.copy = None

    def __getitem__(self, place):
        self.arrive()
        return self.ref[place]


class Leaving:
    def __init__(self, ref, copy):
        self.ref, self.copy, self.shape, self.dtype = ref, copy, ref.shape, ref.dtype
        self.left = False

    def leave(self):
        if not self.left:
            self.copy.start()
            self.left = True

    def __getitem__(self, place):
        return self.ref[place]

    def __setitem__(self, place, value):
        self.ref[place] = value


SPACES = {"v": pltpu.VMEM, "h": pltpu.HBM, "a": pl.ANY}


def call(kernel, outs, args, scratch=(), after=(), limit=20, cost=1):
    kinds = [kind for _, kind, *_ in args]
    fetched = [k for k, kind in enumerate(kinds) if kind != "v"]
    written = [k for k, (_, _, kind) in enumerate(outs) if kind != "v"]

    def body(*refs):
        ins, rest = list(refs[: len(args)]), refs[len(args) + len(after) :]
        results, rest = list(rest[: len(outs)]), rest[len(outs) :]
        in_bufs, rest = rest[: len(fetched)], rest[len(fetched) :]
        out_bufs, rest = rest[: len(written)], rest[len(written) :]
        extra, rest = rest[: len(scratch)], rest[len(scratch) :]
        sems = rest[0] if rest else None
        waits = []
        for n, (k, buf) in enumerate(zip(fetched, in_bufs)):
            source = ins[k]
            if len(args[k]) > 2:
                source = source.at[pl.ds(args[k][2], buf.shape[0])]
            copy = pltpu.make_async_copy(source, buf, sems.at[n])
            copy.start()
            ins[k] = Fetched(buf, copy)
            waits.append(ins[k])
        leaving = []
        for n, (k, buf) in enumerate(zip(written, out_bufs)):
            results[k] = Leaving(buf, pltpu.make_async_copy(buf, results[k], sems.at[len(fetched) + n]))
            leaving.append(results[k])
        kernel(*ins, *results, *extra)
        for out in leaving:
            out.leave()
        for wait in waits:
            wait.arrive()
        for out in leaving:
            out.copy.wait()

    places = {kind: pl.BlockSpec(memory_space=space) for kind, space in SPACES.items()}
    shapes = [
        pltpu.VMEM((args[k][3:] or args[k][0].shape[:1]) + args[k][0].shape[1:], args[k][0].dtype) for k in fetched
    ]
    shapes += [pltpu.VMEM(outs[k][0], outs[k][1]) for k in written]
    shapes += [pltpu.VMEM(shape, kind) for shape, kind in scratch]
    if fetched or written:
        shapes.append(pltpu.SemaphoreType.DMA((len(fetched) + len(written),)))
    name = getattr(kernel, "__name__", None) or kernel.func.__name__
    return pl.pallas_call(
        body,
        out_shape=[
            pltpu.HBM(shape, kind) if place == "h" else jax.ShapeDtypeStruct(shape, kind) for shape, kind, place in outs
        ],
        in_specs=[places[kind] for kind in kinds] + [places["a"]] * len(after),
        out_specs=[places[kind] for _, _, kind in outs],
        scratch_shapes=shapes,
        compiler_params=pltpu.CompilerParams(vmem_limit_bytes=limit * 1024 * 1024),
        cost_estimate=pl.CostEstimate(flops=cost * 35 * 10**9, transcendentals=0, bytes_accessed=1000),
        name=name,
    )(
        *[
            pltpu.with_memory_space_constraint(value, pltpu.HBM) if kind == "h" else value
            for value, kind, *_ in args
        ],
        *after,
    )


def pair_swap(values):
    return lax.ppermute(values, "mp", [(0, 1), (1, 0)])


def swap_bit(values, bit, count):
    return lax.ppermute(values, "dp", [(k, k ^ (1 << bit)) for k in range(count)])


def stage_swap(values, stage, count):
    bits = ((0, 1), (1, 0), (2, 3), (3, 2))[stage]
    pairs = [(2 * k + core, 2 * (k ^ (1 << bits[core])) + core) for k in range(count) for core in range(2)]
    return lax.ppermute(values, ("dp", "mp"), pairs)


def half_of(values, dim, which):
    return lax.dynamic_index_in_dim(values, which, dim, keepdims=False)


def scatter_sum(blocks, order, count):
    place = lax.axis_index("dp")
    levels = len(order)
    left = list(reversed(range(levels)))
    blocks = blocks.reshape((2,) * levels + blocks.shape[1:])
    for bit in order:
        dim = left.index(bit)
        mine = (place >> bit) & 1
        moved = swap_bit(half_of(blocks, dim, 1 - mine), bit, count)
        blocks = half_of(blocks, dim, mine) + moved
        left.remove(bit)
    return blocks


def full_sum(values, count):
    for bit in range(count.bit_length() - 1):
        values = values + swap_bit(values, bit, count)
    return values


def on_device(
    dec_input, enc_output, dec_lengths, enc_lengths, self_query, self_key, self_value, self_output, self_gain,
    rel_bias, cross_query, cross_key, cross_value, cross_output, cross_gain, ffn_in, ffn_out, ffn_gain, cotangent
):
    slots, width = dec_input.shape[1:]
    steps = enc_output.shape[1]
    inner = self_query.shape[1]
    hidden = ffn_in.shape[1]
    tokens = 3 * slots // 2
    count = lax.axis_size("dp")
    quick = count == 16
    row, half_row = (tokens, width), (tokens // 2, width)
    part_of = (tokens, inner)
    wide = 4 * inner
    share = width // count

    bias_rows = rel_bias.T
    tall = tokens // 2 + 8
    x, low_ffn, qkv, att_self, lse_self, part_self, x_half = call(
        self_forward,
        [(row, bf16, "h"), (row, bf16, "h"), ((tokens, 3 * inner), bf16, "h"), (part_of, bf16, "v"),
         ((8, tokens), f32, "v"), (row, f32, "v"), ((tall, width), f32, "h")],
        [(dec_lengths, "h"), (dec_input, "h"), (self_gain, "h"), (self_query, "h"), (self_key, "h"), (self_value, "h"),
         (cotangent, "h"), (bias_rows, "h"), (self_output, "h")],
    )
    moved_self = pair_swap(part_self)
    if quick:
        x_moved = stage_swap(x_half, 0, count)
    keys, values_t, keys_far, values, keys_t = call(
        encoder_forward,
        [((2 * steps, inner), bf16, "v"), ((inner, 2 * steps), bf16, "v")] + [((2 * steps, inner), bf16, "h")] * 2
        + [((inner, 2 * steps), bf16, "h")],
        [(enc_output, "v"), (cross_key, "v"), (cross_value, "v")],
        after=(part_self,),
    )
    after_self, cross_q, att_cross, lse_cross, part_cross = call(
        cross_forward,
        [(row, f32, "v"), (part_of, bf16, "h"), (part_of, bf16, "v"), ((8, 2 * slots), f32, "v"), (row, f32, "v")],
        [(dec_lengths, "v"), (enc_lengths, "v"), (x, "v"), (part_self, "v"), (moved_self, "v"), (cross_gain, "v"),
         (cross_query, "v"), (cross_output, "v"), (keys, "v"), (values_t, "v")],
    )
    moved_cross = pair_swap(part_cross)
    after = (part_cross,)
    if quick:
        early, own_cross = call(
            pack_early,
            [(row, f32, "v"), ((width // 2, tokens), bf16, "v")],
            [(after_self, "v"), (cross_gain, "v"), (att_cross, "v")],
            after=after,
        )
        early_moved = stage_swap(early, 0, count)
        after = (early,)
    after_cross, normed_ffn, halves, act, hid, back, *x_two = call(
        ffn_both,
        [(row, f32, "v"), (row, bf16, "h"), (row, f32, "v"), ((tokens, hidden), bf16, "v"), ((tokens, hidden), bf16, "v"),
         (row, f32, "v")] + [((2 * tall, width), f32, "v")] * quick,
        [(after_self, "v"), (part_cross, "v"), (moved_cross, "v"), (ffn_gain, "v"), (low_ffn, "v"), (ffn_in, "v"),
         (ffn_out, "v")] + ([(x_half, "v"), (x_moved, "v")] if quick else []),
        after=after,
    )
    moved_back = pair_swap(back)
    if quick:
        group_a = stage_swap(halves, 2, count)
        x_rest = stage_swap(x_two[0], 1, count)
    grad_cross, low_cross, dq, dk, dv, gain_ffn_grad, part_dq = call(
        cross_backward,
        [(row, f32, "h"), (row, bf16, "v"), (part_of, bf16, "v")] + [((2 * steps, inner), bf16, "v")] * 2
        + [((1, width), f32, "v"), (row, f32, "v")],
        [(dec_lengths, "v"), (enc_lengths, "v"), (after_cross, "v"), (back, "v"), (moved_back, "v"), (ffn_gain, "v"),
         (low_ffn, "v"), (cross_output, "v"), (cross_query, "v"), (cross_q, "v"), (keys_far, "v"), (values, "v"),
         (keys_t, "v"), (lse_cross, "v")],
        after=(rest(back),),
    )
    moved_dq = pair_swap(part_dq)
    after = (rest(part_dq), early_moved) if quick else (rest(part_dq),)
    grad_self, low_self, self_half, gain_cross_grad = call(
        self_grad,
        [(row, f32, "v"), (row, bf16, "v"), ((tokens // 2, width), f32, "v"), ((1, width), f32, "v")],
        [(after_self, "v"), (part_dq, "v"), (moved_dq, "v"), (cross_gain, "v"), (grad_cross, "v")],
        after=after,
    )
    after = (low_self,)
    half = width // 2
    if quick:
        self_a = stage_swap(self_half, 0, count)
    dqkv, bias_grad, parts = call(
        back_all,
        [((tokens, 3 * inner), bf16, "v"), ((8, rel_bias.shape[0]), f32, "v"), ((2 * tokens + 2 * steps, width), f32, "v")],
        [(dec_lengths, "v"), (low_self, "v"), (bias_rows, "v"), (self_output, "v"), (self_query, "v"), (self_key, "v"),
         (self_value, "v"), (qkv, "v"), (lse_self, "v"), (dk, "v"), (dv, "v"), (cross_key, "v"), (cross_value, "v"),
         (act, "v"), (ffn_out, "v")],
        after=after,
    )
    parts_moved = pair_swap(parts)
    after = (rest(parts),)
    if quick:
        self_two, halves_two = call(
            collect,
            [(row, f32, "v"), ((2 * tokens, width), f32, "v")],
            [(self_half, "v"), (self_a, "v"), (halves, "v"), (group_a, "v")],
            after=(parts, x_rest),
        )
        self_rest = stage_swap(self_two, 1, count)
        group_rest = stage_swap(halves_two, 3, count)
        (late_cross,) = call(
            cross_weights,
            [((half + tokens, 2 * inner), f32, "v")],
            [(enc_output, "v"), (dk, "v"), (dv, "v"), (dq, "v"), (low_cross, "v")],
            after=(self_two,),
        )
        late_cross_moved = stage_swap(late_cross, 0, count)
        (self_here,) = call(
            gather_self,
            [((3 * tall + 3 * tokens // 2, width), f32, "v")],
            [(x_moved, "v"), (x_rest, "v"), (self_a, "v"), (self_rest, "v")],
            after=(late_cross,),
        )
        self_there = pair_swap(self_here)
        after = (rest(self_here),)
    dec_packed, small = call(
        named(finish_self_norm, rel_bias.shape[1]),
        [(row, bf16, "v"), ((8, half), f32, "v")],
        [(x, "v"), (parts, "v"), (parts_moved, "v"), (self_gain, "v"), (grad_self, "v"),
         (gain_ffn_grad, "v"), (gain_cross_grad, "v"), (bias_grad, "v")],
        after=after,
    )
    if quick:
        small_moved = stage_swap(small, 0, count)
    after = (small,)
    if quick:
        send_self, keep_self = call(
            self_group,
            [((2 * share, wide), f32, "v")] * 2,
            [(x, "v"), (dqkv, "v"), (low_self, "v"), (att_self, "v"), (self_here, "v"), (self_there, "v"),
             (self_gain, "v"), (bias_rows, "v"), (self_query, "v"), (self_key, "v"), (self_value, "v"), (self_output, "v")],
            scratch=[((3 * tokens, wide), bf16), ((4 * tokens, wide), bf16), ((4 * share, wide), f32)],
            after=after,
        )
        self_first = stage_swap(send_self, 2, count)
        after = (send_self,)
    mark = ((8, 128), f32, "v")
    dec_grad, layer_out, enc_grad, done = call(
        finish_outputs,
        [(dec_input.shape, bf16, "v"), (dec_input.shape, bf16, "v"), (enc_output.shape, bf16, "v"), mark],
        [(dec_lengths, "v"), (dec_packed, "v"), (parts, "v"), (parts_moved, "v"), (after_cross, "v")],
        after=after,
    )
    if not quick:
        return slow_sums(
            locals(), x, after_self, self_gain, cross_gain, rel_bias, enc_output, count
        )
    (keep_cross,) = call(
        cross_keep, [((half, 2 * inner), f32, "v")], [(enc_output, "v"), (dk, "v"), (dv, "v")], after=(done,)
    )
    send_cross, keep_cross, small_two = call(
        cross_fold,
        [((half // 2 + 8, wide), f32, "v"), ((half // 2, wide), f32, "v"), ((16, half), f32, "v")],
        [(keep_cross, "v"), (late_cross_moved, "v"), (early_moved, "v"), (own_cross, "v"), (dq, "v"),
         (low_cross, "v"), (att_cross, "v"), (small, "v"), (small_moved, "v")],
        scratch=[((half, wide), f32)],
        after=(keep_cross,),
    )
    cross_first = stage_swap(send_cross, 1, count)
    (ffn_here,) = call(
        gather_ffn, [((3 * tokens, width), f32, "v")], [(group_a, "v"), (group_rest, "v")], after=(send_cross,)
    )
    ffn_there = pair_swap(ffn_here)
    (send_self2,) = call(
        named(self_fold, share), [((share, wide), f32, "v")], [(keep_self, "v"), (self_first, "v")], after=(ffn_here,)
    )
    self_second = stage_swap(send_self2, 3, count)
    made_ffn, keep_ffn = call(
        ffn_group,
        [((2 * share, 2 * hidden), f32, "v")] * 2,
        [(normed_ffn, "v"), (low_ffn, "v"), (act, "v"), (hid, "v"), (ffn_here, "v"), (ffn_there, "v"), (ffn_in, "v"),
         (ffn_out, "v")],
        scratch=[((4 * tokens, width), bf16), ((4 * tokens, width), bf16), ((4 * share, 2 * hidden), f32)],
        after=(send_self2,),
    )
    send_cross2, small_four = call(
        named(fold_z, share),
        [((half // 4 + 8, wide), f32, "v"), ((8, half), f32, "v")],
        [(keep_cross, "v"), (small_two, "v"), (cross_first, "v")],
        after=(made_ffn,),
    )
    cross_second = stage_swap(send_cross2, 2, count)
    (send_ffn,) = call(relay, [((2 * share, 2 * hidden), f32, "v")], [(made_ffn, "v")], after=(send_cross2,))
    ffn_first = stage_swap(send_ffn, 0, count)
    send_cross3, small_last = call(
        named(fold_last, share),
        [((share + 8, wide), f32, "v"), ((16, half), f32, "v")],
        [(keep_cross, "v"), (small_four, "v"), (cross_first, "v"), (cross_second, "v")],
        after=(send_ffn,),
    )
    cross_third = stage_swap(send_cross3, 3, count)
    (send_ffn2,) = call(
        named(ffn_fold, share), [((share, 2 * hidden), f32, "v")], [(keep_ffn, "v"), (ffn_first, "v")], after=(send_cross3,)
    )
    ffn_second = stage_swap(send_ffn2, 1, count)
    *self_grads, self_out_grad, done = call(
        named(finish_self, share),
        [((share, inner), f32, "v")] * 4 + [mark],
        [(keep_self, "v"), (self_first, "v"), (self_second, "v")],
        after=(rest(send_ffn2),),
    )
    *cross_grads, cross_out_grad, gain_self_sum, gain_cross_sum, gain_ffn_sum, bias_sum, done = call(
        named(finish_cross, rel_bias.shape[1], share),
        [((share, inner), f32, "v")] * 4 + [((width,), f32, "v")] * 3 + [(rel_bias.shape[::-1], f32, "v"), mark],
        [(keep_cross, "v"), (cross_first, "v"), (cross_second, "v"), (small_last, "v"), (cross_third, "v")],
        after=(done,),
    )
    grad_ffn_in, grad_ffn_out = call(
        named(finish_ffn, share),
        [((share, hidden), f32, "h")] * 2,
        [(keep_ffn, "v"), (ffn_first, "v"), (ffn_second, "v")],
        after=(done,),
    )
    return (
        layer_out,
        dec_grad,
        enc_grad,
        *self_grads,
        self_out_grad.T,
        gain_self_sum,
        bias_sum.T,
        *cross_grads,
        cross_out_grad.T,
        gain_cross_sum,
        grad_ffn_in,
        grad_ffn_out.T,
        gain_ffn_sum,
    )


def rest(made):
    (out,) = call(pause, [((8, 128), f32, "v")], [], after=(made,))
    return out


def named(kernel, *given):
    def run(*refs):
        return kernel(*given, *refs)

    run.__name__ = kernel.__name__
    return run


def slow_sums(made, x, after_self, self_gain, cross_gain, rel_bias, enc_output, count):
    width = x.shape[1]
    heads, buckets = rel_bias.shape[1], rel_bias.shape[0]
    inner = made["dq"].shape[1]
    bits = list(range(count.bit_length() - 1))
    order_a, order_b = bits, bits[1::-1] + bits[2:]

    def scattered(order, *grads):
        parts = [grad.reshape(count, -1, grad.shape[1]) for grad in grads]
        widths = [part.shape[2] for part in parts]
        total = scatter_sum(jnp.concatenate(parts, axis=2), order, count)
        return jnp.split(total, np.cumsum(widths)[:-1].tolist(), axis=1)

    def outer(left, right):
        return jnp.einsum("rm,rn->mn", left, right, preferred_element_type=f32)

    def normed(values, gain):
        return (values * inverse_rms(values) * gain).astype(bf16)

    normed_self = normed(x.astype(f32), self_gain)
    normed_cross = normed(after_self, cross_gain)
    enc_flat = enc_output.reshape(-1, width)
    dqkv = made["dqkv"]
    (grad_ffn_in,) = scattered(order_a, outer(made["normed_ffn"], made["hid"]))
    (grad_ffn_out,) = scattered(order_b, outer(made["low_ffn"], made["act"]))
    cross_query, cross_key = scattered(order_a, outer(normed_cross, made["dq"]), outer(enc_flat, made["dk"]))
    cross_value, cross_output = scattered(
        order_b, outer(enc_flat, made["dv"]), outer(made["low_cross"], made["att_cross"])
    )
    self_query, self_key = scattered(
        order_a, outer(normed_self, dqkv[:, :inner]), outer(normed_self, dqkv[:, inner : 2 * inner])
    )
    self_value, self_output = scattered(
        order_b, outer(normed_self, dqkv[:, 2 * inner :]), outer(made["low_self"], made["att_self"])
    )
    small = full_sum(made["small"], count)
    return (
        made["layer_out"],
        made["dec_grad"],
        made["enc_grad"],
        self_query,
        self_key,
        self_value,
        self_output.T,
        small[0:2].reshape(-1),
        small[6, : heads * buckets].reshape(heads, buckets).T,
        cross_query,
        cross_key,
        cross_value,
        cross_output.T,
        small[2:4].reshape(-1),
        grad_ffn_in,
        grad_ffn_out.T,
        small[4:6].reshape(-1),
    )


def solution(mesh):
    in_specs = (
        P("dp", None, None),
        P("dp", None, None),
        P("dp", None),
        P("dp", None),
        P(None, "mp"),
        P(None, "mp"),
        P(None, "mp"),
        P("mp", None),
        P(),
        P(None, "mp"),
        P(None, "mp"),
        P(None, "mp"),
        P(None, "mp"),
        P("mp", None),
        P(),
        P(None, "mp"),
        P("mp", None),
        P(),
        P("dp", None, None),
    )
    out_specs = (
        P("dp", None, None),
        P("dp", None, None),
        P("dp", None, None),
        P("dp", "mp"),
        P("dp", "mp"),
        P("dp", "mp"),
        P("mp", "dp"),
        P(),
        P(None, "mp"),
        P("dp", "mp"),
        P("dp", "mp"),
        P("dp", "mp"),
        P("mp", "dp"),
        P(),
        P("dp", "mp"),
        P("mp", "dp"),
        P(),
    )
    return jax.shard_map(
        on_device, mesh=mesh, in_specs=in_specs, out_specs=out_specs, check_vma=False
    )
```

```python
import functools

import jax
import jax.numpy as jnp
import numpy as np
from jax import lax
from jax.experimental import pallas as pl
from jax.experimental.pallas import tpu as pltpu
from jax.sharding import PartitionSpec as P

epsilon = 1e-06
masked_value = -1e30
head_width = 64
pair_width = 2 * head_width
bf16 = jnp.bfloat16
f32 = jnp.float32
curve = 0.7978845608028654
cubic = 0.044715


def nn(left, right, precision=None):
    return lax.dot_general(
        left, right, (((1,), (0,)), ((), ())), precision=precision, preferred_element_type=f32
    )


def nt(left, right, precision=None):
    return lax.dot_general(
        left, right, (((1,), (1,)), ((), ())), precision=precision, preferred_element_type=f32
    )


def tn(left, right, precision=None):
    return lax.dot_general(
        left, right, (((0,), (0,)), ((), ())), precision=precision, preferred_element_type=f32
    )


def gain_row(gain):
    return gain[...].reshape(1, gain.shape[0])


def iota(shape, dim):
    return lax.broadcasted_iota(jnp.int32, shape, dim)


def inverse_rms(values):
    return lax.rsqrt(jnp.sum(values * values, -1, keepdims=True) / values.shape[-1] + epsilon)


def norm_back(values, gain, upstream):
    inverse = inverse_rms(values)
    scaled = upstream * gain
    mean = jnp.sum(scaled * values, -1, keepdims=True) / values.shape[-1]
    gain_grad = jnp.sum(upstream * values * inverse, 0, keepdims=True)
    return inverse * scaled - values * (inverse * inverse * inverse * mean), gain_grad


def bucket_bounds(buckets):
    half = buckets // 2
    return [int(b) for b in np.ceil(16.0 * 8.0 ** (np.arange(1, half) / half))]


def bucket_rows(buckets, width):
    distance = iota((buckets, width), 1)
    coarse = jnp.full((buckets, width), buckets // 2, jnp.int32)
    for bound in bucket_bounds(buckets):
        coarse += (distance >= bound).astype(jnp.int32)
    chosen = jnp.where(distance < buckets // 2, distance, coarse)
    return (chosen == iota((buckets, width), 0)).astype(f32)


def half_masks():
    lane = iota((1, pair_width), 1)
    low = (lane < head_width).astype(f32)
    return low.astype(bf16), (1.0 - low).astype(bf16)


def pick_rows(first, tokens, slots):
    row, col = iota((tokens, 2 * slots), 0), iota((tokens, 2 * slots), 1)
    return (col == jnp.where(row < first, row, row + (slots - first))).astype(f32).astype(bf16)


def self_bias(bias_ref, width):
    return nn(
        bias_ref[...], bucket_rows(bias_ref.shape[1], width), precision=lax.Precision.HIGHEST
    )


def self_allowed(first, tokens):
    key, query = iota((tokens, tokens), 0), iota((tokens, tokens), 1)
    return (key <= query) & ((key < first) == (query < first))


def spread_bias(base, head, tokens):
    width = base.shape[1]
    rows = jnp.broadcast_to(base[head : head + 1], (tokens, width))
    return pltpu.roll(rows, 0, 1, stride=1, stride_axis=0)[:, :tokens]


def own_half(values):
    half = values.shape[0] // 2
    return jnp.where(lax.axis_index("mp") == 0, values[:half], values[half:])


def flush(out):
    if isinstance(out, Leaving):
        out.leave()


def self_forward(
    dec_len, dec, gain, w_q, w_k, w_v, cot, bias, w_o, x_out, low_out, qkv_out, att_out, lse_out, part_out, x_half
):
    slots, width = dec.shape[1], dec.shape[2]
    tokens = x_out.shape[0]
    heads = bias.shape[0]
    first = dec_len[:, 0:1]
    picked = pick_rows(first, tokens, slots)
    x = nn(picked, dec[...].reshape(2 * slots, width))
    x_out[...] = x.astype(bf16)
    flush(x_out)
    half = tokens // 2
    x_half[:half, :] = own_half(x)
    x_half[half:, :] = jnp.broadcast_to(first.astype(f32), (8, width))
    flush(x_half)
    normed = (x * inverse_rms(x) * gain_row(gain)).astype(bf16)
    inner = w_q.shape[1]
    for k, w in enumerate((w_q, w_k, w_v)):
        qkv_out[:, k * inner : (k + 1) * inner] = nn(normed, w[...]).astype(bf16)
    flush(qkv_out)
    low_out[...] = nn(picked, cot[...].reshape(2 * slots, width)).astype(bf16)
    flush(low_out)
    base = self_bias(bias, 2 * slots)
    allowed = self_allowed(first, tokens)
    masks = half_masks()
    top = iota((pair_width, tokens), 0) < head_width
    lse_out[...] = jnp.zeros_like(lse_out)
    for pair in range(heads // 2):
        lanes = slice(pair * pair_width, (pair + 1) * pair_width)
        q = qkv_out[:, lanes]
        k = qkv_out[:, inner + pair * pair_width : inner + (pair + 1) * pair_width]
        v = qkv_out[:, 2 * inner + pair * pair_width : 2 * inner + (pair + 1) * pair_width]
        v_t = v.astype(f32).T.astype(bf16)
        mixed = []
        for side in range(2):
            head = 2 * pair + side
            scores = nt(k, q * masks[side]) + spread_bias(base, head, tokens)
            scores = jnp.where(allowed, scores, masked_value)
            top_score = jnp.max(scores, 0, keepdims=True)
            weights = jnp.exp(scores - top_score)
            total = jnp.sum(weights, 0, keepdims=True)
            lse_out[head : head + 1, :] = top_score + jnp.log(total)
            mixed.append(nn(v_t, (weights * (1.0 / total)).astype(bf16)))
        att_out[:, lanes] = jnp.where(top, mixed[0], mixed[1]).T.astype(bf16)
    flush(att_out)
    flush(lse_out)
    part_out[...] = nn(att_out[...], w_o[...])


def encoder_forward(enc, w_k, w_v, k_out, vt_out, k_far, v_far, kt_far):
    steps = enc.shape[1]
    for w, out, out_t in ((w_v, v_far, vt_out), (w_k, k_out, kt_far)):
        for e in range(enc.shape[0]):
            rows = slice(e * steps, (e + 1) * steps)
            made = nn(enc[e], w[...])
            out[rows, :] = made.astype(bf16)
            out_t[:, rows] = made.T.astype(bf16)
        if out is v_far:
            flush(v_far)
    k_far[...] = k_out[...]


def cross_rows(first, tokens, slots, e):
    row = iota((slots, 1), 0) + e * (tokens - slots)
    return row < first if e == 0 else row >= first


def cross_forward(
    dec_len, enc_len, x, part, moved, gain, w_q, w_o, k_in, vt_in, after_out, q_out, att_out, lse_out, part_out
):
    tokens = x.shape[0]
    slots = 2 * tokens // 3
    steps = k_in.shape[0] // 2
    first = dec_len[:, 0:1]
    after = x[...].astype(f32) + (part[...] + moved[...])
    after_out[...] = after
    normed = (after * inverse_rms(after) * gain_row(gain)).astype(bf16)
    q_out[...] = nn(normed, w_q[...]).astype(bf16)
    flush(q_out)
    masks = half_masks()
    top = iota((pair_width, slots), 0) < head_width
    own = iota((tokens, 1), 0) < first
    lse_out[...] = jnp.zeros_like(lse_out)
    shift = tokens - slots
    for pair in range(q_out.shape[1] // pair_width):
        lanes = slice(pair * pair_width, (pair + 1) * pair_width)
        parts = []
        for e in range(2):
            q = q_out[e * shift : e * shift + slots, lanes]
            both = jnp.concatenate([q * masks[0], q * masks[1]], 0)
            scores = nt(k_in[e * steps : (e + 1) * steps, lanes], both)
            valid = iota((steps, 1), 0) < enc_len[:, e : e + 1]
            scores = jnp.where(valid, scores, masked_value)
            top_score = jnp.max(scores, 0, keepdims=True)
            weights = jnp.exp(scores - top_score)
            total = jnp.sum(weights, 0, keepdims=True)
            lse_out[2 * pair + e : 2 * pair + e + 1, :] = top_score + jnp.log(total)
            mixed = nn(
                vt_in[lanes, e * steps : (e + 1) * steps], (weights * (1.0 / total)).astype(bf16)
            )
            parts.append(jnp.where(top, mixed[:, :slots], mixed[:, slots:]).T)
        fill = jnp.zeros((shift, pair_width), f32)
        att_out[:, lanes] = jnp.where(
            own, jnp.concatenate([parts[0], fill], 0), jnp.concatenate([fill, parts[1]], 0)
        ).astype(bf16)
    flush(lse_out)
    part_out[...] = nn(att_out[...], w_o[...])


def ffn_both(
    after, part, moved, gain, low, w_in, w_out, *outs
):
    if len(outs) > 6:
        x_half, x_moved, *outs, x_rest = outs
        stack(x_rest, x_half, x_moved)
    after_out, normed_out, halves_out, act_out, hid_out, back_out = outs
    total = after[...] + (part[...] + moved[...])
    after_out[...] = total
    normed = (total * inverse_rms(total) * gain_row(gain)).astype(bf16)
    normed_out[...] = normed
    flush(normed_out)
    low_in = low[...]
    half = low_in.shape[0] // 2
    halves_out[:half, :] = own_half(low_in.astype(f32))
    halves_out[half:, :] = own_half(normed.astype(f32))
    hidden = w_in.shape[1]
    chunk = 512 if hidden % 512 == 0 else hidden
    for start in range(0, hidden, chunk):
        cols = slice(start, start + chunk)
        u = nn(normed, w_in[:, cols])
        t = jnp.tanh(curve * (u + cubic * (u * u * u)))
        act = (0.5 * u * (1.0 + t)).astype(bf16)
        slope = 0.5 * (1.0 + t) + 0.5 * u * (1.0 - t * t) * (curve * (1.0 + 3.0 * cubic * (u * u)))
        hid = (nt(low_in, w_out[cols, :]) * slope).astype(bf16)
        act_out[:, cols] = act
        hid_out[:, cols] = hid
        backward = nt(hid, w_in[:, cols])
        if start == 0:
            back_out[...] = backward
        else:
            back_out[...] += backward


def cross_backward(
    dec_len, enc_len, after, part, moved, gain, low, w_o, w_q, q_in, k_in, v_in, kt_in, lse,
    grad_out, low_out, dq_out, dk_out, dv_out, gain_out, part_out
):
    tokens = after.shape[0]
    slots = 2 * tokens // 3
    steps = k_in.shape[0] // 2
    first = dec_len[:, 0:1]
    shift = tokens - slots
    norm_in, gain_grad = norm_back(after[...], gain_row(gain), part[...] + moved[...])
    gain_out[...] = gain_grad
    flush(gain_out)
    grad = low[...].astype(f32) + norm_in
    grad_out[...] = grad
    flush(grad_out)
    low_grad = grad.astype(bf16)
    low_out[...] = low_grad
    flush(low_out)
    g_all = nt(low_grad, w_o[...])
    masks = half_masks()
    top = iota((pair_width, slots), 0) < head_width
    for pair in range(q_in.shape[1] // pair_width):
        lanes = slice(pair * pair_width, (pair + 1) * pair_width)
        parts = []
        for e in range(2):
            keys = slice(e * steps, (e + 1) * steps)
            window = slice(e * shift, e * shift + slots)
            q = q_in[window, lanes]
            g = jnp.where(cross_rows(first, tokens, slots, e), g_all[window, lanes], 0.0)
            g = g.astype(bf16)
            q_both = jnp.concatenate([q * masks[0], q * masks[1]], 0)
            g_both = jnp.concatenate([g * masks[0], g * masks[1]], 0)
            valid = iota((steps, 1), 0) < enc_len[:, e : e + 1]
            scores = jnp.where(valid, nt(k_in[keys, lanes], q_both), masked_value)
            p = jnp.exp(scores - lse[2 * pair + e : 2 * pair + e + 1, :])
            dp = nt(v_in[keys, lanes], g_both)
            ds = (p * (dp - jnp.sum(p * dp, 0, keepdims=True))).astype(bf16)
            dk_out[keys, lanes] = nn(ds, q_both).astype(bf16)
            dv_out[keys, lanes] = nn(p.astype(bf16), g_both).astype(bf16)
            dq = nn(kt_in[lanes, keys], ds)
            parts.append(jnp.where(top, dq[:, :slots], dq[:, slots:]).T)
        fill = jnp.zeros((shift, pair_width), f32)
        dq_out[:, lanes] = (
            jnp.concatenate([parts[0], fill], 0) + jnp.concatenate([fill, parts[1]], 0)
        ).astype(bf16)
    part_out[...] = nt(dq_out[...], w_q[...])


def self_grad(after, part, moved, gain, grad_in, grad_out, low_out, half_out, gain_out):
    norm_in, gain_grad = norm_back(after[...], gain_row(gain), part[...] + moved[...])
    gain_out[...] = gain_grad
    grad = grad_in[...] + norm_in
    grad_out[...] = grad
    low = grad.astype(bf16)
    low_out[...] = low
    half_out[...] = own_half(low.astype(f32))


def back_all(
    dec_len, low, bias, w_o, w_q, w_k, w_v, qkv, lse, dk, dv, w_ck, w_cv, act, w_ffn, dqkv_out, bias_out, part_out
):
    tokens = low.shape[0]
    self_backward(
        dec_len, low, bias, w_o, w_q, w_k, w_v, qkv, lse, dqkv_out, bias_out, part_out.at[pl.ds(0, tokens), :]
    )
    part_out[tokens : 2 * tokens, :] = nn(act[...], w_ffn[...])
    steps = dk.shape[0] // 2
    for e in range(2):
        rows = slice(e * steps, (e + 1) * steps)
        part_out[2 * tokens + e * steps : 2 * tokens + (e + 1) * steps, :] = nt(dk[rows, :], w_ck[...]) + nt(
            dv[rows, :], w_cv[...]
        )


def self_backward(dec_len, low, bias, w_o, w_q, w_k, w_v, qkv, lse, dqkv_out, bias_out, part_out):
    tokens = low.shape[0]
    heads = bias.shape[0]
    first = dec_len[:, 0:1]
    inner = w_q.shape[1]
    g_all = nt(low[...], w_o[...]).astype(bf16)
    reach = 4 * tokens // 3
    base = self_bias(bias, reach)
    allowed = self_allowed(first, tokens)
    masks = half_masks()
    top = iota((pair_width, tokens), 0) < head_width
    diagonals = []
    for pair in range(heads // 2):
        lanes = slice(pair * pair_width, (pair + 1) * pair_width)
        k_lanes = slice(inner + pair * pair_width, inner + (pair + 1) * pair_width)
        v_lanes = slice(2 * inner + pair * pair_width, 2 * inner + (pair + 1) * pair_width)
        q, k, v, g = qkv[:, lanes], qkv[:, k_lanes], qkv[:, v_lanes], g_all[:, lanes]
        k_t = k.astype(f32).T.astype(bf16)
        dk, dv, dq = 0.0, 0.0, []
        for side in range(2):
            head = 2 * pair + side
            q_half, g_half = q * masks[side], g * masks[side]
            scores = nt(k, q_half) + spread_bias(base, head, tokens)
            scores = jnp.where(allowed, scores, masked_value)
            p = jnp.exp(scores - lse[head : head + 1, :])
            dp = nt(v, g_half)
            ds = p * (dp - jnp.sum(p * dp, 0, keepdims=True))
            ds_low = ds.astype(bf16)
            dk += nn(ds_low, q_half)
            dv += nn(p.astype(bf16), g_half)
            dq.append(nn(k_t, ds_low))
            wide = jnp.concatenate([ds, jnp.zeros((tokens, reach - tokens), f32)], 1)
            total = wide[:8]
            for start in range(8, tokens, 8):
                total += pltpu.roll(wide[start : start + 8], reach - start, 1)
            diagonals.append(total)
        dqkv_out[:, lanes] = jnp.where(top, dq[0], dq[1]).T.astype(bf16)
        dqkv_out[:, k_lanes] = dk.astype(bf16)
        dqkv_out[:, v_lanes] = dv.astype(bf16)
    flush(dqkv_out)
    part_out[...] = (
        nt(dqkv_out[:, :inner], w_q[...])
        + nt(dqkv_out[:, inner : 2 * inner], w_k[...])
        + nt(dqkv_out[:, 2 * inner :], w_v[...])
    )
    total = jnp.concatenate(diagonals, 0)
    row = iota(total.shape, 0) & 7
    lined = jnp.zeros_like(total)
    for s in range(8):
        lined += jnp.where(row == s, pltpu.roll(total, (reach - s) % reach, 1), 0.0)
    head_of = ((iota((8, 8 * heads), 1) >> 3) == iota((8, 8 * heads), 0)).astype(f32)
    by_head = nn(head_of, lined, precision=lax.Precision.HIGHEST)
    bias_out[...] = nt(by_head, bucket_rows(bias.shape[1], reach), precision=lax.Precision.HIGHEST)


def unpacked(values, first, slots):
    tokens = values.shape[0]
    slot, row = iota((2 * slots, tokens), 0), iota((2 * slots, tokens), 1)
    limit = jnp.where(slot < slots, first, slots + tokens - first)
    wanted = jnp.where(slot < slots, slot, slot - slots + first)
    spread = ((row == wanted) & (slot < limit)).astype(f32).astype(bf16)
    return nn(spread, values.astype(bf16)).astype(bf16)


def finish_self_norm(
    heads, x, part, moved, gain, grad_in, gain_ffn, gain_cross, bias_grad, dec_out, small_out
):
    tokens, width = x.shape
    norm_in, gain_grad = norm_back(x[...].astype(f32), gain_row(gain), part[:tokens, :] + moved[:tokens, :])
    half, buckets = small_out.shape[1], bias_grad.shape[1]
    small_out[...] = jnp.zeros_like(small_out)
    for k, value in enumerate((gain_grad, gain_cross[...], gain_ffn[...])):
        small_out[2 * k : 2 * k + 1, :] = value[:, :half]
        small_out[2 * k + 1 : 2 * k + 2, :] = value[:, half:]
    small_out[6:7, : heads * buckets] = jnp.concatenate([bias_grad[h : h + 1, :] for h in range(heads)], 1)
    dec_out[...] = (grad_in[...] + norm_in).astype(bf16)


def finish_outputs(dec_len, dec, part, moved, after, dec_out, layer_out, enc_out, token):
    token[...] = jnp.zeros_like(token)
    tokens = dec.shape[0]
    first, slots = dec_len[:, 0:1], dec_out.shape[1]
    dec_out[...] = unpacked(dec[...], first, slots).reshape(dec_out.shape)
    total = after[...] + (part[tokens : 2 * tokens, :] + moved[tokens : 2 * tokens, :])
    layer_out[...] = unpacked(total, first, slots).reshape(layer_out.shape)
    enc_out[...] = (part[2 * tokens :, :] + moved[2 * tokens :, :]).astype(bf16).reshape(enc_out.shape)


def pause(out):
    out[...] = jnp.zeros_like(out)


def collect(low_half, low_a, halves, group_a, low_out, group_out):
    stack(low_out, low_half, low_a)
    stack(group_out, halves, group_a)


def gather_self(x_moved, x_rest, low_a, low_rest, out):
    stack(out, x_moved, x_rest, low_a, low_rest)


def relay(value, out):
    out[...] = value[...]


def gather_ffn(group_a, group_rest, out):
    stack(out, group_a, group_rest)


def place_of():
    return lax.axis_index("dp"), lax.axis_index("mp")


def own_bit(stage):
    place, core = place_of()
    shift = (core, 1 - core, 2 + core, 3 - core)[stage]
    return lax.shift_right_logical(place, shift) & 1


def entry(stage, step, bit):
    if stage % 2:
        return 2 * step + bit
    core = lax.axis_index("mp")
    return jnp.where(core == 0, 2 * step + bit, (step // 2) * 4 + 2 * bit + step % 2)


def pick_chunks(chunks, rows, width):
    gap = iota((rows, width), 1) - iota((rows, width), 0)
    return jnp.concatenate([(gap == chunk * rows).astype(f32) for chunk in chunks], 0).astype(bf16)


def half_pick(other, width):
    bit = own_bit(0)
    bit = 1 - bit if other else bit
    return pick_chunks([entry(0, step, bit) for step in range(8)], width // 16, width)


def fold_lanes(values):
    half = values.shape[0] // 2
    return jnp.concatenate([values[:half], values[half:]], 1)


def unfold_lanes(values):
    half = values.shape[1] // 2
    return jnp.concatenate([values[:, :half], values[:, half:]], 0)


def split_entries(stage, source, send_out, keep_out, rows):
    bit = own_bit(stage)
    for step in range(keep_out.shape[0] // rows):
        here = slice(step * rows, (step + 1) * rows)
        send_out[here, :] = source(entry(stage, step, 1 - bit))
        keep_out[here, :] = source(entry(stage, step, bit))


def pack_early(after, gain, att, early_out, own):
    width = after.shape[1]
    inner = att.shape[1]
    v = after[...]
    normed = (v * inverse_rms(v) * gain_row(gain)).astype(bf16)
    own[...] = nt(half_pick(0, width), normed).astype(bf16)
    early_out[:, :inner] = fold_lanes(nt(half_pick(1, width), normed))
    early_out[:, inner:] = att[...].astype(f32)


def stack(out, *parts):
    at = 0
    for part in parts:
        out[at : at + part.shape[0], :] = part[...]
        at += part.shape[0]


def cross_weights(enc, dk, dv, dq, low, late_out):
    steps, width = enc.shape[1:]
    inner = dk.shape[1]
    half = width // 2
    left = nt(half_pick(1, width), enc[...].reshape(2 * steps, width)).astype(bf16)
    late_out[:half, :inner] = nn(left, dk[...])
    late_out[:half, inner:] = nn(left, dv[...])
    late_out[half:, :inner] = dq[...].astype(f32)
    late_out[half:, inner:] = fold_lanes(nt(half_pick(1, width), low[...]))


def cross_keep(enc, dk, dv, keep_out):
    steps, width = enc.shape[1:]
    inner = dk.shape[1]
    left = nt(half_pick(0, width), enc[...].reshape(2 * steps, width)).astype(bf16)
    keep_out[:, :inner] = nn(left, dk[...])
    keep_out[:, inner:] = nn(left, dv[...])


def side_by_side(out, at, small):
    n = small.shape[1]
    out[at:, :n] = small[:8, :]
    out[at:, n : 2 * n] = small[8:, :]
    out[at:, 2 * n :] = jnp.zeros_like(out[at:, 2 * n :])


def above(rows, n):
    return jnp.concatenate([rows[:, :n], rows[:, n : 2 * n]], 0)


def cross_fold(keep, moved, early, own, dq, low, att, small, small_moved, send_out, keep_out, small_out, total):
    width = low.shape[1]
    half, inner = own.shape[0], dq.shape[1]
    rows = width // 16
    total[:, :inner] = nn(own[...], dq[...]) + nn(
        unfold_lanes(early[:, :inner]).astype(bf16), moved[half:, :inner].astype(bf16)
    )
    total[:, 3 * inner :] = nn(nt(half_pick(0, width), low[...]).astype(bf16), att[...]) + nn(
        unfold_lanes(moved[half:, inner:]).astype(bf16), early[:, inner:].astype(bf16)
    )
    total[:, inner : 3 * inner] = keep[...] + moved[:half, :]
    split_entries(1, lambda i: total[pl.ds(pl.multiple_of(i * rows, 8), rows), :], send_out, keep_out, rows)
    stack(small_out, small, small_moved)
    side_by_side(send_out, keep_out.shape[0], small_out)


def self_group(
    x, dqkv, low, att, here, there, gain, bias, w_q, w_k, w_v, w_o,
    send_out, keep_out, made, grads, total
):
    tokens, width = x.shape
    inner = att.shape[1]
    heads = bias.shape[0]
    half = tokens // 2
    place, core = place_of()
    rows = width // 16
    base = self_bias(bias, 4 * tokens // 3)
    masks = half_masks()
    top = iota((pair_width, tokens), 0) < head_width
    biases = [spread_bias(base, head, tokens) for head in range(heads)]
    tall = half + 8
    x_at, low_at = (0, tall, 2 * tall), (3 * tall, 3 * tall + half, 3 * tall + 2 * half)
    orders = ((0, 1), (1, 0), (2, 2))

    def joined(starts, mine, other):
        a, b = here[starts[mine] : starts[mine] + half, :], there[starts[other] : starts[other] + half, :]
        return [jnp.where(core == 0, a, b), jnp.where(core == 0, b, a)]

    v = jnp.concatenate([part for order in orders for part in joined(x_at, *order)], 0)
    normed = (v * inverse_rms(v) * gain_row(gain)).astype(bf16)
    low_all = jnp.concatenate([part for order in orders for part in joined(low_at, *order)], 0).astype(bf16)
    for k, w in enumerate((w_q, w_k, w_v)):
        made[:, k * inner : (k + 1) * inner] = nn(normed, w[...]).astype(bf16)
    made[:, 3 * inner :] = nt(low_all, w_o[...]).astype(bf16)
    grads[:tokens, : 3 * inner] = dqkv[...]
    grads[:tokens, 3 * inner :] = att[...]
    def one_chip(k, carry):
        first = here[pl.ds(pl.multiple_of(k * tall + half, 8), 8), :][0:1, 0:1].astype(jnp.int32)
        allowed = self_allowed(first, tokens)
        source = pl.ds(pl.multiple_of(k * tokens, 16), tokens)
        target = pl.ds(pl.multiple_of((k + 1) * tokens, 16), tokens)
        every = range(heads)
        lanes = [slice(pair * pair_width, (pair + 1) * pair_width) for pair in range(heads // 2)]
        q, key, value, g = (
            [made[source, n * inner + lane.start : n * inner + lane.stop] for lane in lanes] for n in range(4)
        )
        k_t = [part.astype(f32).T.astype(bf16) for part in key]
        v_t = [part.astype(f32).T.astype(bf16) for part in value]
        q_half = [q[h // 2] * masks[h % 2] for h in every]
        g_half = [g[h // 2] * masks[h % 2] for h in every]
        scores = [jnp.where(allowed, nt(key[h // 2], q_half[h]) + biases[h], masked_value) for h in every]
        weights = [jnp.exp(score - jnp.max(score, 0, keepdims=True)) for score in scores]
        p = [weight * (1.0 / jnp.sum(weight, 0, keepdims=True)) for weight in weights]
        dp = [nt(value[h // 2], g_half[h]) for h in every]
        ds = [(p[h] * (dp[h] - jnp.sum(p[h] * dp[h], 0, keepdims=True))).astype(bf16) for h in every]
        p = [part.astype(bf16) for part in p]
        dk = [nn(ds[h], q_half[h]) for h in every]
        dv = [nn(p[h], g_half[h]) for h in every]
        dq = [nn(k_t[h // 2], ds[h]) for h in every]
        mixed = [nn(v_t[h // 2], p[h]) for h in every]
        for pair, lane in enumerate(lanes):
            a, b = 2 * pair, 2 * pair + 1
            for n, part in enumerate(
                (jnp.where(top, dq[a], dq[b]).T, dk[a] + dk[b], dv[a] + dv[b], jnp.where(top, mixed[a], mixed[b]).T)
            ):
                grads[target, n * inner + lane.start : n * inner + lane.stop] = part.astype(bf16)
        return carry

    lax.fori_loop(0, 3, one_chip, 0)
    picked = pick_chunks([4 * z + (place & 3) for z in range(4)], rows, width)
    v = x[...].astype(f32)
    own = (v * inverse_rms(v) * gain_row(gain)).astype(bf16)
    left = jnp.concatenate([nt(picked, own), nt(picked, normed)], 1).astype(bf16)
    total[:, : 3 * inner] = nn(left, grads[:, : 3 * inner])
    left = jnp.concatenate([nt(picked, low[...]), nt(picked, low_all)], 1).astype(bf16)
    total[:, 3 * inner :] = nn(left, grads[:, 3 * inner :])
    split_entries(2, lambda i: total[pl.ds(pl.multiple_of(i * rows, 8), rows), :], send_out, keep_out, rows)


def chunk_of(ref, index, rows):
    return ref[pl.ds(pl.multiple_of(index * rows, 8), rows), :]


def entry_here(step):
    core, bit = lax.axis_index("mp"), own_bit(2)
    return jnp.where(core == 0, 2 * step + bit, 2 * bit + step)


def fold_z(rows, keep, small, first, out, small_out):
    for step in range(2):
        index = entry(2, step, 1 - own_bit(2))
        out[step * rows : (step + 1) * rows, :] = chunk_of(keep, index, rows) + chunk_of(first, index, rows)
    n = small.shape[1]
    total = four_sum(small[:8, :], small[8:, :], above(first[keep.shape[0] :, : 2 * n], n))
    small_out[...] = total
    out[2 * rows :, :n] = total
    out[2 * rows :, n:] = jnp.zeros_like(out[2 * rows :, n:])


def three_sum(rows, step, keep, first, second):
    index = entry_here(step)
    return chunk_of(keep, index, rows) + chunk_of(first, index, rows) + chunk_of(second, step, rows)


def fold_last(rows, keep, small, first, second, out, small_out):
    out[:rows, :] = three_sum(rows, 1 - own_bit(3), keep, first, second)
    small_out[:8, :] = small[...]
    small_out[8:, :] = second[2 * rows :, : small.shape[1]]
    side_by_side(out, rows, small_out)


def four_sum(mine, first, second):
    core = lax.axis_index("mp")
    near = mine + jnp.where(core == 0, first, second[:8])
    return near + (jnp.where(core == 0, second[:8], first) + second[8:])


def finish_cross(
    heads, rows, keep, first, second, sums, third, q_out, k_out, v_out, o_out, gain_s, gain_c, gain_f, bias_out
):
    inner = q_out.shape[1]
    total = three_sum(rows, own_bit(3), keep, first, second) + third[:rows, :]
    for k, out in enumerate((q_out, k_out, v_out, o_out)):
        out[...] = total[:, k * inner : (k + 1) * inner]
    width, buckets, n = gain_s.shape[0], bias_out.shape[1], sums.shape[1]
    small = four_sum(sums[:8, :], sums[8:, :], above(third[rows:, : 2 * n], n))
    for k, out in enumerate((gain_s, gain_c, gain_f)):
        out[...] = jnp.concatenate([small[2 * k : 2 * k + 1, :], small[2 * k + 1 : 2 * k + 2, :]], 1).reshape(width)
    bias_out[...] = jnp.concatenate([small[6:7, h * buckets : (h + 1) * buckets] for h in range(heads)], 0)


def self_fold(rows, keep, first, out):
    step = 1 - own_bit(3)
    out[...] = chunk_of(keep, step, rows) + chunk_of(first, step, rows)


def finish_self(rows, keep, first, second, q_out, k_out, v_out, o_out, token):
    token[...] = jnp.zeros_like(token)
    inner = q_out.shape[1]
    step = own_bit(3)
    total = chunk_of(keep, step, rows) + chunk_of(first, step, rows) + second[...]
    for k, out in enumerate((q_out, k_out, v_out, o_out)):
        out[...] = total[:, k * inner : (k + 1) * inner]


def ffn_fold(rows, keep, first, out):
    step = 1 - own_bit(1)
    out[...] = chunk_of(keep, step, rows) + chunk_of(first, step, rows)


def finish_ffn(rows, keep, first, second, in_out, out_out, token):
    token[...] = jnp.zeros_like(token)
    step = own_bit(1)
    total = chunk_of(keep, step, rows) + chunk_of(first, step, rows) + second[...]
    hidden = in_out.shape[1]
    in_out[...] = total[:, :hidden]
    out_out[...] = total[:, hidden:]


def ffn_group(normed, low, act, hid, here, there, w_in, w_out, send_out, keep_out, normed_all, low_all, total):
    tokens, width = normed.shape
    hidden = w_in.shape[1]
    half = tokens // 2
    rows = width // 16
    normed_all[:tokens, :] = normed[...]
    low_all[:tokens, :] = low[...]
    at = tokens
    for source in (here, there):
        for k in range(3):
            low_all[at : at + half, :] = source[2 * k * half : (2 * k + 1) * half, :].astype(bf16)
            normed_all[at : at + half, :] = source[(2 * k + 1) * half : (2 * k + 2) * half, :].astype(bf16)
            at += half
    place, core = place_of()
    first = lax.shift_right_logical(place, 2) * 4
    picked = pick_chunks([first + k for k in range(4)], rows, width)
    left_in = nt(picked, normed_all[...]).astype(bf16)
    left_out = nt(picked, low_all[...]).astype(bf16)
    chunk = 512 if hidden % 512 == 0 else hidden

    def one_chunk(k, carry):
        cols = pl.ds(pl.multiple_of(k * chunk, 128), chunk)
        u = nn(normed_all[tokens:, :], w_in[:, cols])
        t = jnp.tanh(curve * (u + cubic * (u * u * u)))
        other_act = (0.5 * u * (1.0 + t)).astype(bf16)
        slope = 0.5 * (1.0 + t) + 0.5 * u * (1.0 - t * t) * (curve * (1.0 + 3.0 * cubic * (u * u)))
        other_hid = (nt(low_all[tokens:, :], w_out[cols, :]) * slope).astype(bf16)
        total[:, cols] = nn(left_in[:, :tokens], hid[:, cols]) + nn(left_in[:, tokens:], other_hid)
        total[:, pl.ds(pl.multiple_of(hidden + k * chunk, 128), chunk)] = nn(
            left_out[:, :tokens], act[:, cols]
        ) + nn(left_out[:, tokens:], other_act)
        return carry

    lax.fori_loop(0, hidden // chunk, one_chunk, 0)
    split_entries(0, lambda i: total[pl.ds(pl.multiple_of(i * rows, 8), rows), :], send_out, keep_out, rows)


class Fetched:
    def __init__(self, ref, copy):
        self.ref, self.copy, self.shape, self.dtype = ref, copy, ref.shape, ref.dtype

    def arrive(self):
        if self.copy is not None:
            self.copy.wait()
            self.copy = None

    def __getitem__(self, place):
        self.arrive()
        return self.ref[place]


class Leaving:
    def __init__(self, ref, copy):
        self.ref, self.copy, self.shape, self.dtype = ref, copy, ref.shape, ref.dtype
        self.left = False

    def leave(self):
        if not self.left:
            self.copy.start()
            self.left = True

    def __getitem__(self, place):
        return self.ref[place]

    def __setitem__(self, place, value):
        self.ref[place] = value


SPACES = {"v": pltpu.VMEM, "h": pltpu.HBM, "a": pl.ANY}


def call(kernel, outs, args, scratch=(), after=(), limit=20, cost=1):
    kinds = [kind for _, kind, *_ in args]
    fetched = [k for k, kind in enumerate(kinds) if kind != "v"]
    written = [k for k, (_, _, kind) in enumerate(outs) if kind != "v"]

    def body(*refs):
        ins, rest = list(refs[: len(args)]), refs[len(args) + len(after) :]
        results, rest = list(rest[: len(outs)]), rest[len(outs) :]
        in_bufs, rest = rest[: len(fetched)], rest[len(fetched) :]
        out_bufs, rest = rest[: len(written)], rest[len(written) :]
        extra, rest = rest[: len(scratch)], rest[len(scratch) :]
        sems = rest[0] if rest else None
        waits = []
        for n, (k, buf) in enumerate(zip(fetched, in_bufs)):
            source = ins[k]
            if len(args[k]) > 2:
                source = source.at[pl.ds(args[k][2], buf.shape[0])]
            copy = pltpu.make_async_copy(source, buf, sems.at[n])
            copy.start()
            ins[k] = Fetched(buf, copy)
            waits.append(ins[k])
        leaving = []
        for n, (k, buf) in enumerate(zip(written, out_bufs)):
            results[k] = Leaving(buf, pltpu.make_async_copy(buf, results[k], sems.at[len(fetched) + n]))
            leaving.append(results[k])
        kernel(*ins, *results, *extra)
        for out in leaving:
            out.leave()
        for wait in waits:
            wait.arrive()
        for out in leaving:
            out.copy.wait()

    places = {kind: pl.BlockSpec(memory_space=space) for kind, space in SPACES.items()}
    shapes = [
        pltpu.VMEM((args[k][3:] or args[k][0].shape[:1]) + args[k][0].shape[1:], args[k][0].dtype) for k in fetched
    ]
    shapes += [pltpu.VMEM(outs[k][0], outs[k][1]) for k in written]
    shapes += [pltpu.VMEM(shape, kind) for shape, kind in scratch]
    if fetched or written:
        shapes.append(pltpu.SemaphoreType.DMA((len(fetched) + len(written),)))
    name = getattr(kernel, "__name__", None) or kernel.func.__name__
    return pl.pallas_call(
        body,
        out_shape=[
            pltpu.HBM(shape, kind) if place == "h" else jax.ShapeDtypeStruct(shape, kind) for shape, kind, place in outs
        ],
        in_specs=[places[kind] for kind in kinds] + [places["a"]] * len(after),
        out_specs=[places[kind] for _, _, kind in outs],
        scratch_shapes=shapes,
        compiler_params=pltpu.CompilerParams(vmem_limit_bytes=limit * 1024 * 1024),
        cost_estimate=pl.CostEstimate(flops=cost * 35 * 10**9, transcendentals=0, bytes_accessed=1000),
        name=name,
    )(
        *[
            pltpu.with_memory_space_constraint(value, pltpu.HBM) if kind == "h" else value
            for value, kind, *_ in args
        ],
        *after,
    )


def pair_swap(values):
    return lax.ppermute(values, "mp", [(0, 1), (1, 0)])


def swap_bit(values, bit, count):
    return lax.ppermute(values, "dp", [(k, k ^ (1 << bit)) for k in range(count)])


def stage_swap(values, stage, count):
    bits = ((0, 1), (1, 0), (2, 3), (3, 2))[stage]
    pairs = [(2 * k + core, 2 * (k ^ (1 << bits[core])) + core) for k in range(count) for core in range(2)]
    return lax.ppermute(values, ("dp", "mp"), pairs)


def half_of(values, dim, which):
    return lax.dynamic_index_in_dim(values, which, dim, keepdims=False)


def scatter_sum(blocks, order, count):
    place = lax.axis_index("dp")
    levels = len(order)
    left = list(reversed(range(levels)))
    blocks = blocks.reshape((2,) * levels + blocks.shape[1:])
    for bit in order:
        dim = left.index(bit)
        mine = (place >> bit) & 1
        moved = swap_bit(half_of(blocks, dim, 1 - mine), bit, count)
        blocks = half_of(blocks, dim, mine) + moved
        left.remove(bit)
    return blocks


def full_sum(values, count):
    for bit in range(count.bit_length() - 1):
        values = values + swap_bit(values, bit, count)
    return values


def on_device(
    dec_input, enc_output, dec_lengths, enc_lengths, self_query, self_key, self_value, self_output, self_gain,
    rel_bias, cross_query, cross_key, cross_value, cross_output, cross_gain, ffn_in, ffn_out, ffn_gain, cotangent
):
    slots, width = dec_input.shape[1:]
    steps = enc_output.shape[1]
    inner = self_query.shape[1]
    hidden = ffn_in.shape[1]
    tokens = 3 * slots // 2
    count = lax.axis_size("dp")
    quick = count == 16
    row, half_row = (tokens, width), (tokens // 2, width)
    part_of = (tokens, inner)
    wide = 4 * inner
    share = width // count

    bias_rows = rel_bias.T
    tall = tokens // 2 + 8
    x, low_ffn, qkv, att_self, lse_self, part_self, x_half = call(
        self_forward,
        [(row, bf16, "h"), (row, bf16, "h"), ((tokens, 3 * inner), bf16, "h"), (part_of, bf16, "v"),
         ((8, tokens), f32, "v"), (row, f32, "v"), ((tall, width), f32, "h")],
        [(dec_lengths, "h"), (dec_input, "h"), (self_gain, "h"), (self_query, "h"), (self_key, "h"), (self_value, "h"),
         (cotangent, "h"), (bias_rows, "h"), (self_output, "h")],
    )
    moved_self = pair_swap(part_self)
    if quick:
        x_moved = stage_swap(x_half, 0, count)
    keys, values_t, keys_far, values, keys_t = call(
        encoder_forward,
        [((2 * steps, inner), bf16, "v"), ((inner, 2 * steps), bf16, "v")] + [((2 * steps, inner), bf16, "h")] * 2
        + [((inner, 2 * steps), bf16, "h")],
        [(enc_output, "v"), (cross_key, "v"), (cross_value, "v")],
        after=(part_self,),
    )
    after_self, cross_q, att_cross, lse_cross, part_cross = call(
        cross_forward,
        [(row, f32, "v"), (part_of, bf16, "h"), (part_of, bf16, "v"), ((8, 2 * slots), f32, "v"), (row, f32, "v")],
        [(dec_lengths, "v"), (enc_lengths, "v"), (x, "v"), (part_self, "v"), (moved_self, "v"), (cross_gain, "v"),
         (cross_query, "v"), (cross_output, "v"), (keys, "v"), (values_t, "v")],
    )
    moved_cross = pair_swap(part_cross)
    after = (part_cross,)
    if quick:
        early, own_cross = call(
            pack_early,
            [(row, f32, "v"), ((width // 2, tokens), bf16, "v")],
            [(after_self, "v"), (cross_gain, "v"), (att_cross, "v")],
            after=after,
        )
        early_moved = stage_swap(early, 0, count)
        after = (early,)
    after_cross, normed_ffn, halves, act, hid, back, *x_two = call(
        ffn_both,
        [(row, f32, "v"), (row, bf16, "h"), (row, f32, "v"), ((tokens, hidden), bf16, "v"), ((tokens, hidden), bf16, "v"),
         (row, f32, "v")] + [((2 * tall, width), f32, "v")] * quick,
        [(after_self, "v"), (part_cross, "v"), (moved_cross, "v"), (ffn_gain, "v"), (low_ffn, "v"), (ffn_in, "v"),
         (ffn_out, "v")] + ([(x_half, "v"), (x_moved, "v")] if quick else []),
        after=after,
    )
    moved_back = pair_swap(back)
    if quick:
        group_a = stage_swap(halves, 2, count)
        x_rest = stage_swap(x_two[0], 1, count)
    grad_cross, low_cross, dq, dk, dv, gain_ffn_grad, part_dq = call(
        cross_backward,
        [(row, f32, "h"), (row, bf16, "v"), (part_of, bf16, "v")] + [((2 * steps, inner), bf16, "v")] * 2
        + [((1, width), f32, "v"), (row, f32, "v")],
        [(dec_lengths, "v"), (enc_lengths, "v"), (after_cross, "v"), (back, "v"), (moved_back, "v"), (ffn_gain, "v"),
         (low_ffn, "v"), (cross_output, "v"), (cross_query, "v"), (cross_q, "v"), (keys_far, "v"), (values, "v"),
         (keys_t, "v"), (lse_cross, "v")],
        after=(rest(back),),
    )
    moved_dq = pair_swap(part_dq)
    after = (rest(part_dq), early_moved) if quick else (rest(part_dq),)
    grad_self, low_self, self_half, gain_cross_grad = call(
        self_grad,
        [(row, f32, "v"), (row, bf16, "v"), ((tokens // 2, width), f32, "v"), ((1, width), f32, "v")],
        [(after_self, "v"), (part_dq, "v"), (moved_dq, "v"), (cross_gain, "v"), (grad_cross, "v")],
        after=after,
    )
    after = (low_self,)
    half = width // 2
    if quick:
        self_a = stage_swap(self_half, 0, count)
    dqkv, bias_grad, parts = call(
        back_all,
        [((tokens, 3 * inner), bf16, "v"), ((8, rel_bias.shape[0]), f32, "v"), ((2 * tokens + 2 * steps, width), f32, "v")],
        [(dec_lengths, "v"), (low_self, "v"), (bias_rows, "v"), (self_output, "v"), (self_query, "v"), (self_key, "v"),
         (self_value, "v"), (qkv, "v"), (lse_self, "v"), (dk, "v"), (dv, "v"), (cross_key, "v"), (cross_value, "v"),
         (act, "v"), (ffn_out, "v")],
        after=after,
    )
    parts_moved = pair_swap(parts)
    after = (rest(parts),)
    if quick:
        self_two, halves_two = call(
            collect,
            [(row, f32, "v"), ((2 * tokens, width), f32, "v")],
            [(self_half, "v"), (self_a, "v"), (halves, "v"), (group_a, "v")],
            after=(parts, x_rest),
        )
        self_rest = stage_swap(self_two, 1, count)
        group_rest = stage_swap(halves_two, 3, count)
        (late_cross,) = call(
            cross_weights,
            [((half + tokens, 2 * inner), f32, "v")],
            [(enc_output, "v"), (dk, "v"), (dv, "v"), (dq, "v"), (low_cross, "v")],
            after=(self_two,),
        )
        late_cross_moved = stage_swap(late_cross, 0, count)
        (self_here,) = call(
            gather_self,
            [((3 * tall + 3 * tokens // 2, width), f32, "v")],
            [(x_moved, "v"), (x_rest, "v"), (self_a, "v"), (self_rest, "v")],
            after=(late_cross,),
        )
        self_there = pair_swap(self_here)
        after = (rest(self_here),)
    dec_packed, small = call(
        named(finish_self_norm, rel_bias.shape[1]),
        [(row, bf16, "v"), ((8, half), f32, "v")],
        [(x, "v"), (parts, "v"), (parts_moved, "v"), (self_gain, "v"), (grad_self, "v"),
         (gain_ffn_grad, "v"), (gain_cross_grad, "v"), (bias_grad, "v")],
        after=after,
    )
    if quick:
        small_moved = stage_swap(small, 0, count)
    after = (small,)
    if quick:
        send_self, keep_self = call(
            self_group,
            [((2 * share, wide), f32, "v")] * 2,
            [(x, "v"), (dqkv, "v"), (low_self, "v"), (att_self, "v"), (self_here, "v"), (self_there, "v"),
             (self_gain, "v"), (bias_rows, "v"), (self_query, "v"), (self_key, "v"), (self_value, "v"), (self_output, "v")],
            scratch=[((3 * tokens, wide), bf16), ((4 * tokens, wide), bf16), ((4 * share, wide), f32)],
            after=after,
        )
        self_first = stage_swap(send_self, 2, count)
        after = (send_self,)
    mark = ((8, 128), f32, "v")

    def outputs(after):
        return call(
            finish_outputs,
            [(dec_input.shape, bf16, "v"), (dec_input.shape, bf16, "v"), (enc_output.shape, bf16, "v"), mark],
            [(dec_lengths, "v"), (dec_packed, "v"), (parts, "v"), (parts_moved, "v"), (after_cross, "v")],
            after=after,
        )

    if not quick:
        dec_grad, layer_out, enc_grad, done = outputs(after)
        return slow_sums(
            locals(), x, after_self, self_gain, cross_gain, rel_bias, enc_output, count
        )
    (keep_cross,) = call(
        cross_keep, [((half, 2 * inner), f32, "v")], [(enc_output, "v"), (dk, "v"), (dv, "v")], after=(send_self,)
    )
    send_cross, keep_cross, small_two = call(
        cross_fold,
        [((half // 2 + 8, wide), f32, "v"), ((half // 2, wide), f32, "v"), ((16, half), f32, "v")],
        [(keep_cross, "v"), (late_cross_moved, "v"), (early_moved, "v"), (own_cross, "v"), (dq, "v"),
         (low_cross, "v"), (att_cross, "v"), (small, "v"), (small_moved, "v")],
        scratch=[((half, wide), f32)],
        after=(keep_cross,),
    )
    cross_first = stage_swap(send_cross, 1, count)
    (ffn_here,) = call(
        gather_ffn, [((3 * tokens, width), f32, "v")], [(group_a, "v"), (group_rest, "v")], after=(send_cross,)
    )
    ffn_there = pair_swap(ffn_here)
    dec_grad, layer_out, enc_grad, done = outputs((ffn_here,))
    made_ffn, keep_ffn = call(
        ffn_group,
        [((2 * share, 2 * hidden), f32, "v")] * 2,
        [(normed_ffn, "v"), (low_ffn, "v"), (act, "v"), (hid, "v"), (ffn_here, "v"), (ffn_there, "v"), (ffn_in, "v"),
         (ffn_out, "v")],
        scratch=[((4 * tokens, width), bf16), ((4 * tokens, width), bf16), ((4 * share, 2 * hidden), f32)],
        after=(done,),
    )
    (send_self2,) = call(
        named(self_fold, share), [((share, wide), f32, "v")], [(keep_self, "v"), (self_first, "v")], after=(made_ffn,)
    )
    self_second = stage_swap(send_self2, 3, count)
    send_cross2, small_four = call(
        named(fold_z, share),
        [((half // 4 + 8, wide), f32, "v"), ((8, half), f32, "v")],
        [(keep_cross, "v"), (small_two, "v"), (cross_first, "v")],
        after=(send_self2,),
    )
    cross_second = stage_swap(send_cross2, 2, count)
    (send_ffn,) = call(relay, [((2 * share, 2 * hidden), f32, "v")], [(made_ffn, "v")], after=(send_cross2,))
    ffn_first = stage_swap(send_ffn, 0, count)
    *self_grads, self_out_grad, done = call(
        named(finish_self, share),
        [((share, inner), f32, "v")] * 4 + [mark],
        [(keep_self, "v"), (self_first, "v"), (self_second, "v")],
        after=(send_ffn,),
    )
    (send_ffn2,) = call(
        named(ffn_fold, share), [((share, 2 * hidden), f32, "v")], [(keep_ffn, "v"), (ffn_first, "v")], after=(done,)
    )
    ffn_second = stage_swap(send_ffn2, 1, count)
    send_cross3, small_last = call(
        named(fold_last, share),
        [((share + 8, wide), f32, "v"), ((16, half), f32, "v")],
        [(keep_cross, "v"), (small_four, "v"), (cross_first, "v"), (cross_second, "v")],
        after=(send_ffn2,),
    )
    cross_third = stage_swap(send_cross3, 3, count)
    grad_ffn_in, grad_ffn_out, done = call(
        named(finish_ffn, share),
        [((share, hidden), f32, "h")] * 2 + [mark],
        [(keep_ffn, "v"), (ffn_first, "v"), (ffn_second, "v")],
        after=(rest(send_cross3),),
    )
    *cross_grads, cross_out_grad, gain_self_sum, gain_cross_sum, gain_ffn_sum, bias_sum = call(
        named(finish_cross, rel_bias.shape[1], share),
        [((share, inner), f32, "h")] * 4 + [((width,), f32, "h")] * 3 + [(rel_bias.shape[::-1], f32, "h")],
        [(keep_cross, "v"), (cross_first, "v"), (cross_second, "v"), (small_last, "v"), (cross_third, "v")],
        after=(done,),
    )
    return (
        layer_out,
        dec_grad,
        enc_grad,
        *self_grads,
        self_out_grad.T,
        gain_self_sum,
        bias_sum.T,
        *cross_grads,
        cross_out_grad.T,
        gain_cross_sum,
        grad_ffn_in,
        grad_ffn_out.T,
        gain_ffn_sum,
    )


def rest(made):
    (out,) = call(pause, [((8, 128), f32, "v")], [], after=(made,))
    return out


def named(kernel, *given):
    def run(*refs):
        return kernel(*given, *refs)

    run.__name__ = kernel.__name__
    return run


def slow_sums(made, x, after_self, self_gain, cross_gain, rel_bias, enc_output, count):
    width = x.shape[1]
    heads, buckets = rel_bias.shape[1], rel_bias.shape[0]
    inner = made["dq"].shape[1]
    bits = list(range(count.bit_length() - 1))
    order_a, order_b = bits, bits[1::-1] + bits[2:]

    def scattered(order, *grads):
        parts = [grad.reshape(count, -1, grad.shape[1]) for grad in grads]
        widths = [part.shape[2] for part in parts]
        total = scatter_sum(jnp.concatenate(parts, axis=2), order, count)
        return jnp.split(total, np.cumsum(widths)[:-1].tolist(), axis=1)

    def outer(left, right):
        return jnp.einsum("rm,rn->mn", left, right, preferred_element_type=f32)

    def normed(values, gain):
        return (values * inverse_rms(values) * gain).astype(bf16)

    normed_self = normed(x.astype(f32), self_gain)
    normed_cross = normed(after_self, cross_gain)
    enc_flat = enc_output.reshape(-1, width)
    dqkv = made["dqkv"]
    (grad_ffn_in,) = scattered(order_a, outer(made["normed_ffn"], made["hid"]))
    (grad_ffn_out,) = scattered(order_b, outer(made["low_ffn"], made["act"]))
    cross_query, cross_key = scattered(order_a, outer(normed_cross, made["dq"]), outer(enc_flat, made["dk"]))
    cross_value, cross_output = scattered(
        order_b, outer(enc_flat, made["dv"]), outer(made["low_cross"], made["att_cross"])
    )
    self_query, self_key = scattered(
        order_a, outer(normed_self, dqkv[:, :inner]), outer(normed_self, dqkv[:, inner : 2 * inner])
    )
    self_value, self_output = scattered(
        order_b, outer(normed_self, dqkv[:, 2 * inner :]), outer(made["low_self"], made["att_self"])
    )
    small = full_sum(made["small"], count)
    return (
        made["layer_out"],
        made["dec_grad"],
        made["enc_grad"],
        self_query,
        self_key,
        self_value,
        self_output.T,
        small[0:2].reshape(-1),
        small[6, : heads * buckets].reshape(heads, buckets).T,
        cross_query,
        cross_key,
        cross_value,
        cross_output.T,
        small[2:4].reshape(-1),
        grad_ffn_in,
        grad_ffn_out.T,
        small[4:6].reshape(-1),
    )


def solution(mesh):
    in_specs = (
        P("dp", None, None),
        P("dp", None, None),
        P("dp", None),
        P("dp", None),
        P(None, "mp"),
        P(None, "mp"),
        P(None, "mp"),
        P("mp", None),
        P(),
        P(None, "mp"),
        P(None, "mp"),
        P(None, "mp"),
        P(None, "mp"),
        P("mp", None),
        P(),
        P(None, "mp"),
        P("mp", None),
        P(),
        P("dp", None, None),
    )
    out_specs = (
        P("dp", None, None),
        P("dp", None, None),
        P("dp", None, None),
        P("dp", "mp"),
        P("dp", "mp"),
        P("dp", "mp"),
        P("mp", "dp"),
        P(),
        P(None, "mp"),
        P("dp", "mp"),
        P("dp", "mp"),
        P("dp", "mp"),
        P("mp", "dp"),
        P(),
        P("dp", "mp"),
        P("mp", "dp"),
        P(),
    )
    return jax.shard_map(
        on_device, mesh=mesh, in_specs=in_specs, out_specs=out_specs, check_vma=False
    )
```

```python
import functools

import jax
import jax.numpy as jnp
import numpy as np
from jax import lax
from jax.experimental import pallas as pl
from jax.experimental.pallas import tpu as pltpu
from jax.sharding import PartitionSpec as P

epsilon = 1e-06
masked_value = -1e30
head_width = 64
pair_width = 2 * head_width
bf16 = jnp.bfloat16
f32 = jnp.float32
curve = 0.7978845608028654
cubic = 0.044715


def nn(left, right, precision=None):
    return lax.dot_general(
        left, right, (((1,), (0,)), ((), ())), precision=precision, preferred_element_type=f32
    )


def nt(left, right, precision=None):
    return lax.dot_general(
        left, right, (((1,), (1,)), ((), ())), precision=precision, preferred_element_type=f32
    )


def tn(left, right, precision=None):
    return lax.dot_general(
        left, right, (((0,), (0,)), ((), ())), precision=precision, preferred_element_type=f32
    )


def gain_row(gain):
    return gain[...].reshape(1, gain.shape[0])


def iota(shape, dim):
    return lax.broadcasted_iota(jnp.int32, shape, dim)


def inverse_rms(values):
    return lax.rsqrt(jnp.sum(values * values, -1, keepdims=True) / values.shape[-1] + epsilon)


def norm_back(values, gain, upstream):
    inverse = inverse_rms(values)
    scaled = upstream * gain
    mean = jnp.sum(scaled * values, -1, keepdims=True) / values.shape[-1]
    gain_grad = jnp.sum(upstream * values * inverse, 0, keepdims=True)
    return inverse * scaled - values * (inverse * inverse * inverse * mean), gain_grad


def bucket_bounds(buckets):
    half = buckets // 2
    return [int(b) for b in np.ceil(16.0 * 8.0 ** (np.arange(1, half) / half))]


def bucket_rows(buckets, width):
    distance = iota((buckets, width), 1)
    coarse = jnp.full((buckets, width), buckets // 2, jnp.int32)
    for bound in bucket_bounds(buckets):
        coarse += (distance >= bound).astype(jnp.int32)
    chosen = jnp.where(distance < buckets // 2, distance, coarse)
    return (chosen == iota((buckets, width), 0)).astype(f32)


def half_masks():
    lane = iota((1, pair_width), 1)
    low = (lane < head_width).astype(f32)
    return low.astype(bf16), (1.0 - low).astype(bf16)


def pick_rows(first, tokens, slots):
    row, col = iota((tokens, 2 * slots), 0), iota((tokens, 2 * slots), 1)
    return (col == jnp.where(row < first, row, row + (slots - first))).astype(f32).astype(bf16)


def self_bias(bias_ref, width):
    return nn(
        bias_ref[...], bucket_rows(bias_ref.shape[1], width), precision=lax.Precision.HIGHEST
    )


def self_allowed(first, tokens):
    key, query = iota((tokens, tokens), 0), iota((tokens, tokens), 1)
    return (key <= query) & ((key < first) == (query < first))


def spread_bias(base, head, tokens):
    width = base.shape[1]
    rows = jnp.broadcast_to(base[head : head + 1], (tokens, width))
    return pltpu.roll(rows, 0, 1, stride=1, stride_axis=0)[:, :tokens]


def own_half(values):
    half = values.shape[0] // 2
    return jnp.where(lax.axis_index("mp") == 0, values[:half], values[half:])


def flush(out):
    if isinstance(out, Leaving):
        out.leave()


def self_forward(
    dec_len, dec, gain, w_q, w_k, w_v, cot, bias, w_o, x_out, low_out, qkv_out, att_out, lse_out, part_out, x_half
):
    slots, width = dec.shape[1], dec.shape[2]
    tokens = x_out.shape[0]
    heads = bias.shape[0]
    first = dec_len[:, 0:1]
    picked = pick_rows(first, tokens, slots)
    x = nn(picked, dec[...].reshape(2 * slots, width))
    x_out[...] = x.astype(bf16)
    flush(x_out)
    half = tokens // 2
    x_half[:half, :] = own_half(x)
    x_half[half:, :] = jnp.broadcast_to(first.astype(f32), (8, width))
    flush(x_half)
    normed = (x * inverse_rms(x) * gain_row(gain)).astype(bf16)
    inner = w_q.shape[1]
    for k, w in enumerate((w_q, w_k, w_v)):
        qkv_out[:, k * inner : (k + 1) * inner] = nn(normed, w[...]).astype(bf16)
    flush(qkv_out)
    low_out[...] = nn(picked, cot[...].reshape(2 * slots, width)).astype(bf16)
    flush(low_out)
    base = self_bias(bias, 2 * slots)
    allowed = self_allowed(first, tokens)
    masks = half_masks()
    top = iota((pair_width, tokens), 0) < head_width
    lse_out[...] = jnp.zeros_like(lse_out)
    for pair in range(heads // 2):
        lanes = slice(pair * pair_width, (pair + 1) * pair_width)
        q = qkv_out[:, lanes]
        k = qkv_out[:, inner + pair * pair_width : inner + (pair + 1) * pair_width]
        v = qkv_out[:, 2 * inner + pair * pair_width : 2 * inner + (pair + 1) * pair_width]
        v_t = v.astype(f32).T.astype(bf16)
        mixed = []
        for side in range(2):
            head = 2 * pair + side
            scores = nt(k, q * masks[side]) + spread_bias(base, head, tokens)
            scores = jnp.where(allowed, scores, masked_value)
            top_score = jnp.max(scores, 0, keepdims=True)
            weights = jnp.exp(scores - top_score)
            total = jnp.sum(weights, 0, keepdims=True)
            lse_out[head : head + 1, :] = top_score + jnp.log(total)
            mixed.append(nn(v_t, (weights * (1.0 / total)).astype(bf16)))
        att_out[:, lanes] = jnp.where(top, mixed[0], mixed[1]).T.astype(bf16)
    flush(att_out)
    flush(lse_out)
    part_out[...] = nn(att_out[...], w_o[...])


def encoder_forward(enc, w_k, w_v, k_out, vt_out, k_far, v_far, kt_far):
    steps = enc.shape[1]
    for w, out, out_t in ((w_v, v_far, vt_out), (w_k, k_out, kt_far)):
        for e in range(enc.shape[0]):
            rows = slice(e * steps, (e + 1) * steps)
            made = nn(enc[e], w[...])
            out[rows, :] = made.astype(bf16)
            out_t[:, rows] = made.T.astype(bf16)
        if out is v_far:
            flush(v_far)
    k_far[...] = k_out[...]


def cross_rows(first, tokens, slots, e):
    row = iota((slots, 1), 0) + e * (tokens - slots)
    return row < first if e == 0 else row >= first


def cross_forward(
    dec_len, enc_len, x, part, moved, gain, w_q, w_o, k_in, vt_in, after_out, q_out, att_out, lse_out, part_out
):
    tokens = x.shape[0]
    slots = 2 * tokens // 3
    steps = k_in.shape[0] // 2
    first = dec_len[:, 0:1]
    after = x[...].astype(f32) + (part[...] + moved[...])
    after_out[...] = after
    normed = (after * inverse_rms(after) * gain_row(gain)).astype(bf16)
    q_out[...] = nn(normed, w_q[...]).astype(bf16)
    flush(q_out)
    masks = half_masks()
    top = iota((pair_width, slots), 0) < head_width
    own = iota((tokens, 1), 0) < first
    lse_out[...] = jnp.zeros_like(lse_out)
    shift = tokens - slots
    for pair in range(q_out.shape[1] // pair_width):
        lanes = slice(pair * pair_width, (pair + 1) * pair_width)
        parts = []
        for e in range(2):
            q = q_out[e * shift : e * shift + slots, lanes]
            both = jnp.concatenate([q * masks[0], q * masks[1]], 0)
            scores = nt(k_in[e * steps : (e + 1) * steps, lanes], both)
            valid = iota((steps, 1), 0) < enc_len[:, e : e + 1]
            scores = jnp.where(valid, scores, masked_value)
            top_score = jnp.max(scores, 0, keepdims=True)
            weights = jnp.exp(scores - top_score)
            total = jnp.sum(weights, 0, keepdims=True)
            lse_out[2 * pair + e : 2 * pair + e + 1, :] = top_score + jnp.log(total)
            mixed = nn(
                vt_in[lanes, e * steps : (e + 1) * steps], (weights * (1.0 / total)).astype(bf16)
            )
            parts.append(jnp.where(top, mixed[:, :slots], mixed[:, slots:]).T)
        fill = jnp.zeros((shift, pair_width), f32)
        att_out[:, lanes] = jnp.where(
            own, jnp.concatenate([parts[0], fill], 0), jnp.concatenate([fill, parts[1]], 0)
        ).astype(bf16)
    flush(lse_out)
    part_out[...] = nn(att_out[...], w_o[...])


def ffn_both(
    after, part, moved, gain, low, w_in, w_out, *outs
):
    if len(outs) > 6:
        x_half, x_moved, *outs, x_rest = outs
        stack(x_rest, x_half, x_moved)
    after_out, normed_out, halves_out, act_out, hid_out, back_out = outs
    total = after[...] + (part[...] + moved[...])
    after_out[...] = total
    normed = (total * inverse_rms(total) * gain_row(gain)).astype(bf16)
    normed_out[...] = normed
    flush(normed_out)
    low_in = low[...]
    half = low_in.shape[0] // 2
    halves_out[:half, :] = own_half(low_in.astype(f32))
    halves_out[half:, :] = own_half(normed.astype(f32))
    hidden = w_in.shape[1]
    chunk = 512 if hidden % 512 == 0 else hidden
    for start in range(0, hidden, chunk):
        cols = slice(start, start + chunk)
        u = nn(normed, w_in[:, cols])
        t = jnp.tanh(curve * (u + cubic * (u * u * u)))
        act = (0.5 * u * (1.0 + t)).astype(bf16)
        slope = 0.5 * (1.0 + t) + 0.5 * u * (1.0 - t * t) * (curve * (1.0 + 3.0 * cubic * (u * u)))
        hid = (nt(low_in, w_out[cols, :]) * slope).astype(bf16)
        act_out[:, cols] = act
        hid_out[:, cols] = hid
        backward = nt(hid, w_in[:, cols])
        if start == 0:
            back_out[...] = backward
        else:
            back_out[...] += backward


def cross_backward(
    dec_len, enc_len, after, part, moved, gain, low, w_o, w_q, q_in, k_in, v_in, kt_in, lse,
    grad_out, low_out, dq_out, dk_out, dv_out, gain_out, part_out
):
    tokens = after.shape[0]
    slots = 2 * tokens // 3
    steps = k_in.shape[0] // 2
    first = dec_len[:, 0:1]
    shift = tokens - slots
    norm_in, gain_grad = norm_back(after[...], gain_row(gain), part[...] + moved[...])
    gain_out[...] = gain_grad
    flush(gain_out)
    grad = low[...].astype(f32) + norm_in
    grad_out[...] = grad
    flush(grad_out)
    low_grad = grad.astype(bf16)
    low_out[...] = low_grad
    flush(low_out)
    g_all = nt(low_grad, w_o[...])
    masks = half_masks()
    top = iota((pair_width, slots), 0) < head_width
    for pair in range(q_in.shape[1] // pair_width):
        lanes = slice(pair * pair_width, (pair + 1) * pair_width)
        parts = []
        for e in range(2):
            keys = slice(e * steps, (e + 1) * steps)
            window = slice(e * shift, e * shift + slots)
            q = q_in[window, lanes]
            g = jnp.where(cross_rows(first, tokens, slots, e), g_all[window, lanes], 0.0)
            g = g.astype(bf16)
            q_both = jnp.concatenate([q * masks[0], q * masks[1]], 0)
            g_both = jnp.concatenate([g * masks[0], g * masks[1]], 0)
            valid = iota((steps, 1), 0) < enc_len[:, e : e + 1]
            scores = jnp.where(valid, nt(k_in[keys, lanes], q_both), masked_value)
            p = jnp.exp(scores - lse[2 * pair + e : 2 * pair + e + 1, :])
            dp = nt(v_in[keys, lanes], g_both)
            ds = (p * (dp - jnp.sum(p * dp, 0, keepdims=True))).astype(bf16)
            dk_out[keys, lanes] = nn(ds, q_both).astype(bf16)
            dv_out[keys, lanes] = nn(p.astype(bf16), g_both).astype(bf16)
            dq = nn(kt_in[lanes, keys], ds)
            parts.append(jnp.where(top, dq[:, :slots], dq[:, slots:]).T)
        fill = jnp.zeros((shift, pair_width), f32)
        dq_out[:, lanes] = (
            jnp.concatenate([parts[0], fill], 0) + jnp.concatenate([fill, parts[1]], 0)
        ).astype(bf16)
    part_out[...] = nt(dq_out[...], w_q[...])


def self_grad(after, part, moved, gain, grad_in, grad_out, low_out, half_out, gain_out):
    norm_in, gain_grad = norm_back(after[...], gain_row(gain), part[...] + moved[...])
    gain_out[...] = gain_grad
    grad = grad_in[...] + norm_in
    grad_out[...] = grad
    low = grad.astype(bf16)
    low_out[...] = low
    half_out[...] = own_half(low.astype(f32))


def back_all(
    dec_len, low, bias, w_o, w_q, w_k, w_v, qkv, lse, dk, dv, w_ck, w_cv, act, w_ffn, dqkv_out, bias_out, part_out
):
    tokens = low.shape[0]
    self_backward(
        dec_len, low, bias, w_o, w_q, w_k, w_v, qkv, lse, dqkv_out, bias_out, part_out.at[pl.ds(0, tokens), :]
    )
    part_out[tokens : 2 * tokens, :] = nn(act[...], w_ffn[...])
    steps = dk.shape[0] // 2
    for e in range(2):
        rows = slice(e * steps, (e + 1) * steps)
        part_out[2 * tokens + e * steps : 2 * tokens + (e + 1) * steps, :] = nt(dk[rows, :], w_ck[...]) + nt(
            dv[rows, :], w_cv[...]
        )


def self_backward(dec_len, low, bias, w_o, w_q, w_k, w_v, qkv, lse, dqkv_out, bias_out, part_out):
    tokens = low.shape[0]
    heads = bias.shape[0]
    first = dec_len[:, 0:1]
    inner = w_q.shape[1]
    g_all = nt(low[...], w_o[...]).astype(bf16)
    reach = 4 * tokens // 3
    base = self_bias(bias, reach)
    allowed = self_allowed(first, tokens)
    masks = half_masks()
    top = iota((pair_width, tokens), 0) < head_width
    diagonals = []
    for pair in range(heads // 2):
        lanes = slice(pair * pair_width, (pair + 1) * pair_width)
        k_lanes = slice(inner + pair * pair_width, inner + (pair + 1) * pair_width)
        v_lanes = slice(2 * inner + pair * pair_width, 2 * inner + (pair + 1) * pair_width)
        q, k, v, g = qkv[:, lanes], qkv[:, k_lanes], qkv[:, v_lanes], g_all[:, lanes]
        k_t = k.astype(f32).T.astype(bf16)
        dk, dv, dq = 0.0, 0.0, []
        for side in range(2):
            head = 2 * pair + side
            q_half, g_half = q * masks[side], g * masks[side]
            scores = nt(k, q_half) + spread_bias(base, head, tokens)
            scores = jnp.where(allowed, scores, masked_value)
            p = jnp.exp(scores - lse[head : head + 1, :])
            dp = nt(v, g_half)
            ds = p * (dp - jnp.sum(p * dp, 0, keepdims=True))
            ds_low = ds.astype(bf16)
            dk += nn(ds_low, q_half)
            dv += nn(p.astype(bf16), g_half)
            dq.append(nn(k_t, ds_low))
            wide = jnp.concatenate([ds, jnp.zeros((tokens, reach - tokens), f32)], 1)
            total = wide[:8]
            for start in range(8, tokens, 8):
                total += pltpu.roll(wide[start : start + 8], reach - start, 1)
            diagonals.append(total)
        dqkv_out[:, lanes] = jnp.where(top, dq[0], dq[1]).T.astype(bf16)
        dqkv_out[:, k_lanes] = dk.astype(bf16)
        dqkv_out[:, v_lanes] = dv.astype(bf16)
    flush(dqkv_out)
    part_out[...] = (
        nt(dqkv_out[:, :inner], w_q[...])
        + nt(dqkv_out[:, inner : 2 * inner], w_k[...])
        + nt(dqkv_out[:, 2 * inner :], w_v[...])
    )
    total = jnp.concatenate(diagonals, 0)
    row = iota(total.shape, 0) & 7
    lined = jnp.zeros_like(total)
    for s in range(8):
        lined += jnp.where(row == s, pltpu.roll(total, (reach - s) % reach, 1), 0.0)
    head_of = ((iota((8, 8 * heads), 1) >> 3) == iota((8, 8 * heads), 0)).astype(f32)
    by_head = nn(head_of, lined, precision=lax.Precision.HIGHEST)
    bias_out[...] = nt(by_head, bucket_rows(bias.shape[1], reach), precision=lax.Precision.HIGHEST)


def unpacked(values, first, slots):
    tokens = values.shape[0]
    slot, row = iota((2 * slots, tokens), 0), iota((2 * slots, tokens), 1)
    limit = jnp.where(slot < slots, first, slots + tokens - first)
    wanted = jnp.where(slot < slots, slot, slot - slots + first)
    spread = ((row == wanted) & (slot < limit)).astype(f32).astype(bf16)
    return nn(spread, values.astype(bf16)).astype(bf16)


def finish_self_norm(
    heads, x, part, moved, gain, grad_in, gain_ffn, gain_cross, bias_grad, dec_out, small_out
):
    tokens, width = x.shape
    norm_in, gain_grad = norm_back(x[...].astype(f32), gain_row(gain), part[:tokens, :] + moved[:tokens, :])
    half, buckets = small_out.shape[1], bias_grad.shape[1]
    small_out[...] = jnp.zeros_like(small_out)
    for k, value in enumerate((gain_grad, gain_cross[...], gain_ffn[...])):
        small_out[2 * k : 2 * k + 1, :] = value[:, :half]
        small_out[2 * k + 1 : 2 * k + 2, :] = value[:, half:]
    small_out[6:7, : heads * buckets] = jnp.concatenate([bias_grad[h : h + 1, :] for h in range(heads)], 1)
    dec_out[...] = (grad_in[...] + norm_in).astype(bf16)


def finish_outputs(dec_len, dec, part, moved, after, dec_out, layer_out, enc_out, token):
    token[...] = jnp.zeros_like(token)
    tokens = dec.shape[0]
    first, slots = dec_len[:, 0:1], dec_out.shape[1]
    dec_out[...] = unpacked(dec[...], first, slots).reshape(dec_out.shape)
    total = after[...] + (part[tokens : 2 * tokens, :] + moved[tokens : 2 * tokens, :])
    layer_out[...] = unpacked(total, first, slots).reshape(layer_out.shape)
    enc_out[...] = (part[2 * tokens :, :] + moved[2 * tokens :, :]).astype(bf16).reshape(enc_out.shape)


def pause(out):
    out[...] = jnp.zeros_like(out)


def collect(low_half, low_a, halves, group_a, low_out, group_out):
    stack(low_out, low_half, low_a)
    stack(group_out, halves, group_a)


def gather_self(x_moved, x_rest, low_a, low_rest, out):
    stack(out, x_moved, x_rest, low_a, low_rest)


def relay(value, out):
    out[...] = value[...]


def gather_ffn(group_a, group_rest, out):
    stack(out, group_a, group_rest)


def place_of():
    return lax.axis_index("dp"), lax.axis_index("mp")


def own_bit(stage):
    place, core = place_of()
    shift = (core, 1 - core, 2 + core, 3 - core)[stage]
    return lax.shift_right_logical(place, shift) & 1


def entry(stage, step, bit):
    if stage % 2:
        return 2 * step + bit
    core = lax.axis_index("mp")
    return jnp.where(core == 0, 2 * step + bit, (step // 2) * 4 + 2 * bit + step % 2)


def pick_chunks(chunks, rows, width):
    gap = iota((rows, width), 1) - iota((rows, width), 0)
    return jnp.concatenate([(gap == chunk * rows).astype(f32) for chunk in chunks], 0).astype(bf16)


def half_pick(other, width):
    bit = own_bit(0)
    bit = 1 - bit if other else bit
    return pick_chunks([entry(0, step, bit) for step in range(8)], width // 16, width)


def fold_lanes(values):
    half = values.shape[0] // 2
    return jnp.concatenate([values[:half], values[half:]], 1)


def unfold_lanes(values):
    half = values.shape[1] // 2
    return jnp.concatenate([values[:, :half], values[:, half:]], 0)


def split_entries(stage, source, send_out, keep_out, rows):
    bit = own_bit(stage)
    for step in range(keep_out.shape[0] // rows):
        here = slice(step * rows, (step + 1) * rows)
        send_out[here, :] = source(entry(stage, step, 1 - bit))
        keep_out[here, :] = source(entry(stage, step, bit))


def pack_early(after, gain, att, early_out, own):
    width = after.shape[1]
    inner = att.shape[1]
    v = after[...]
    normed = (v * inverse_rms(v) * gain_row(gain)).astype(bf16)
    own[...] = nt(half_pick(0, width), normed).astype(bf16)
    early_out[:, :inner] = fold_lanes(nt(half_pick(1, width), normed))
    early_out[:, inner:] = att[...].astype(f32)


def stack(out, *parts):
    at = 0
    for part in parts:
        out[at : at + part.shape[0], :] = part[...]
        at += part.shape[0]


def cross_weights(enc, dk, dv, dq, low, late_out):
    steps, width = enc.shape[1:]
    inner = dk.shape[1]
    half = width // 2
    left = nt(half_pick(1, width), enc[...].reshape(2 * steps, width)).astype(bf16)
    late_out[:half, :inner] = nn(left, dk[...])
    late_out[:half, inner:] = nn(left, dv[...])
    late_out[half:, :inner] = dq[...].astype(f32)
    late_out[half:, inner:] = fold_lanes(nt(half_pick(1, width), low[...]))


def cross_keep(enc, dk, dv, keep_out):
    steps, width = enc.shape[1:]
    inner = dk.shape[1]
    left = nt(half_pick(0, width), enc[...].reshape(2 * steps, width)).astype(bf16)
    keep_out[:, :inner] = nn(left, dk[...])
    keep_out[:, inner:] = nn(left, dv[...])


def side_by_side(out, at, small):
    n = small.shape[1]
    out[at:, :n] = small[:8, :]
    out[at:, n : 2 * n] = small[8:, :]
    out[at:, 2 * n :] = jnp.zeros_like(out[at:, 2 * n :])


def above(rows, n):
    return jnp.concatenate([rows[:, :n], rows[:, n : 2 * n]], 0)


def cross_fold(keep, factors, moved, early, own, dq, low, att, small, small_moved, send_out, keep_out, small_out, total):
    width = low.shape[1]
    half, inner = own.shape[0], dq.shape[1]
    rows = width // 16
    total[:, :inner] = nn(own[...], dq[...]) + nn(
        unfold_lanes(early[:, :inner]).astype(bf16), factors[:, :inner].astype(bf16)
    )
    total[:, 3 * inner :] = nn(nt(half_pick(0, width), low[...]).astype(bf16), att[...]) + nn(
        unfold_lanes(factors[:, inner:]).astype(bf16), early[:, inner:].astype(bf16)
    )
    total[:, inner : 3 * inner] = keep[...] + moved[...]
    split_entries(1, lambda i: total[pl.ds(pl.multiple_of(i * rows, 8), rows), :], send_out, keep_out, rows)
    stack(small_out, small, small_moved)
    side_by_side(send_out, keep_out.shape[0], small_out)


def self_group(
    x, dqkv, low, att, here, there, gain, bias, w_q, w_k, w_v, w_o,
    send_out, keep_out, made, grads, total
):
    tokens, width = x.shape
    inner = att.shape[1]
    heads = bias.shape[0]
    half = tokens // 2
    place, core = place_of()
    rows = width // 16
    base = self_bias(bias, 4 * tokens // 3)
    masks = half_masks()
    top = iota((pair_width, tokens), 0) < head_width
    biases = [spread_bias(base, head, tokens) for head in range(heads)]
    tall = half + 8
    x_at, low_at = (0, tall, 2 * tall), (3 * tall, 3 * tall + half, 3 * tall + 2 * half)
    orders = ((0, 1), (1, 0), (2, 2))

    def joined(starts, mine, other):
        a, b = here[starts[mine] : starts[mine] + half, :], there[starts[other] : starts[other] + half, :]
        return [jnp.where(core == 0, a, b), jnp.where(core == 0, b, a)]

    v = jnp.concatenate([part for order in orders for part in joined(x_at, *order)], 0)
    normed = (v * inverse_rms(v) * gain_row(gain)).astype(bf16)
    low_all = jnp.concatenate([part for order in orders for part in joined(low_at, *order)], 0).astype(bf16)
    for k, w in enumerate((w_q, w_k, w_v)):
        made[:, k * inner : (k + 1) * inner] = nn(normed, w[...]).astype(bf16)
    made[:, 3 * inner :] = nt(low_all, w_o[...]).astype(bf16)
    grads[:tokens, : 3 * inner] = dqkv[...]
    grads[:tokens, 3 * inner :] = att[...]
    def one_chip(k, carry):
        first = here[pl.ds(pl.multiple_of(k * tall + half, 8), 8), :][0:1, 0:1].astype(jnp.int32)
        allowed = self_allowed(first, tokens)
        source = pl.ds(pl.multiple_of(k * tokens, 16), tokens)
        target = pl.ds(pl.multiple_of((k + 1) * tokens, 16), tokens)
        every = range(heads)
        lanes = [slice(pair * pair_width, (pair + 1) * pair_width) for pair in range(heads // 2)]
        q, key, value, g = (
            [made[source, n * inner + lane.start : n * inner + lane.stop] for lane in lanes] for n in range(4)
        )
        k_t = [part.astype(f32).T.astype(bf16) for part in key]
        v_t = [part.astype(f32).T.astype(bf16) for part in value]
        q_half = [q[h // 2] * masks[h % 2] for h in every]
        g_half = [g[h // 2] * masks[h % 2] for h in every]
        scores = [jnp.where(allowed, nt(key[h // 2], q_half[h]) + biases[h], masked_value) for h in every]
        weights = [jnp.exp(score - jnp.max(score, 0, keepdims=True)) for score in scores]
        p = [weight * (1.0 / jnp.sum(weight, 0, keepdims=True)) for weight in weights]
        dp = [nt(value[h // 2], g_half[h]) for h in every]
        ds = [(p[h] * (dp[h] - jnp.sum(p[h] * dp[h], 0, keepdims=True))).astype(bf16) for h in every]
        p = [part.astype(bf16) for part in p]
        dk = [nn(ds[h], q_half[h]) for h in every]
        dv = [nn(p[h], g_half[h]) for h in every]
        dq = [nn(k_t[h // 2], ds[h]) for h in every]
        mixed = [nn(v_t[h // 2], p[h]) for h in every]
        for pair, lane in enumerate(lanes):
            a, b = 2 * pair, 2 * pair + 1
            for n, part in enumerate(
                (jnp.where(top, dq[a], dq[b]).T, dk[a] + dk[b], dv[a] + dv[b], jnp.where(top, mixed[a], mixed[b]).T)
            ):
                grads[target, n * inner + lane.start : n * inner + lane.stop] = part.astype(bf16)
        return carry

    lax.fori_loop(0, 3, one_chip, 0)
    picked = pick_chunks([4 * z + (place & 3) for z in range(4)], rows, width)
    v = x[...].astype(f32)
    own = (v * inverse_rms(v) * gain_row(gain)).astype(bf16)
    left = jnp.concatenate([nt(picked, own), nt(picked, normed)], 1).astype(bf16)
    total[:, : 3 * inner] = nn(left, grads[:, : 3 * inner])
    left = jnp.concatenate([nt(picked, low[...]), nt(picked, low_all)], 1).astype(bf16)
    total[:, 3 * inner :] = nn(left, grads[:, 3 * inner :])
    split_entries(2, lambda i: total[pl.ds(pl.multiple_of(i * rows, 8), rows), :], send_out, keep_out, rows)


def chunk_of(ref, index, rows):
    return ref[pl.ds(pl.multiple_of(index * rows, 8), rows), :]


def entry_here(step):
    core, bit = lax.axis_index("mp"), own_bit(2)
    return jnp.where(core == 0, 2 * step + bit, 2 * bit + step)


def fold_z(rows, keep, small, first, out, small_out):
    for step in range(2):
        index = entry(2, step, 1 - own_bit(2))
        out[step * rows : (step + 1) * rows, :] = chunk_of(keep, index, rows) + chunk_of(first, index, rows)
    n = small.shape[1]
    total = four_sum(small[:8, :], small[8:, :], above(first[keep.shape[0] :, : 2 * n], n))
    small_out[...] = total
    out[2 * rows :, :n] = total
    out[2 * rows :, n:] = jnp.zeros_like(out[2 * rows :, n:])


def three_sum(rows, step, keep, first, second):
    index = entry_here(step)
    return chunk_of(keep, index, rows) + chunk_of(first, index, rows) + chunk_of(second, step, rows)


def fold_last(rows, keep, small, first, second, out, small_out):
    out[:rows, :] = three_sum(rows, 1 - own_bit(3), keep, first, second)
    small_out[:8, :] = small[...]
    small_out[8:, :] = second[2 * rows :, : small.shape[1]]
    side_by_side(out, rows, small_out)


def four_sum(mine, first, second):
    core = lax.axis_index("mp")
    near = mine + jnp.where(core == 0, first, second[:8])
    return near + (jnp.where(core == 0, second[:8], first) + second[8:])


def finish_cross(
    heads, rows, keep, first, second, sums, third, q_out, k_out, v_out, o_out, gain_s, gain_c, gain_f, bias_out
):
    inner = q_out.shape[1]
    total = three_sum(rows, own_bit(3), keep, first, second) + third[:rows, :]
    for k, out in enumerate((q_out, k_out, v_out, o_out)):
        out[...] = total[:, k * inner : (k + 1) * inner]
    width, buckets, n = gain_s.shape[0], bias_out.shape[1], sums.shape[1]
    small = four_sum(sums[:8, :], sums[8:, :], above(third[rows:, : 2 * n], n))
    for k, out in enumerate((gain_s, gain_c, gain_f)):
        out[...] = jnp.concatenate([small[2 * k : 2 * k + 1, :], small[2 * k + 1 : 2 * k + 2, :]], 1).reshape(width)
    bias_out[...] = jnp.concatenate([small[6:7, h * buckets : (h + 1) * buckets] for h in range(heads)], 0)


def self_fold(rows, keep, first, out):
    step = 1 - own_bit(3)
    out[...] = chunk_of(keep, step, rows) + chunk_of(first, step, rows)


def finish_self(rows, keep, first, second, q_out, k_out, v_out, o_out, token):
    token[...] = jnp.zeros_like(token)
    inner = q_out.shape[1]
    step = own_bit(3)
    total = chunk_of(keep, step, rows) + chunk_of(first, step, rows) + second[...]
    for k, out in enumerate((q_out, k_out, v_out, o_out)):
        out[...] = total[:, k * inner : (k + 1) * inner]


def ffn_fold(rows, keep, first, out):
    step = 1 - own_bit(1)
    out[...] = chunk_of(keep, step, rows) + chunk_of(first, step, rows)


def finish_ffn(rows, keep, first, second, in_out, out_out, token):
    token[...] = jnp.zeros_like(token)
    step = own_bit(1)
    total = chunk_of(keep, step, rows) + chunk_of(first, step, rows) + second[...]
    hidden = in_out.shape[1]
    in_out[...] = total[:, :hidden]
    out_out[...] = total[:, hidden:]


def ffn_group(normed, low, act, hid, here, there, w_in, w_out, send_out, keep_out, normed_all, low_all, total):
    tokens, width = normed.shape
    hidden = w_in.shape[1]
    half = tokens // 2
    rows = width // 16
    normed_all[:tokens, :] = normed[...]
    low_all[:tokens, :] = low[...]
    at = tokens
    for source in (here, there):
        for k in range(3):
            low_all[at : at + half, :] = source[2 * k * half : (2 * k + 1) * half, :].astype(bf16)
            normed_all[at : at + half, :] = source[(2 * k + 1) * half : (2 * k + 2) * half, :].astype(bf16)
            at += half
    place, core = place_of()
    first = lax.shift_right_logical(place, 2) * 4
    picked = pick_chunks([first + k for k in range(4)], rows, width)
    left_in = nt(picked, normed_all[...]).astype(bf16)
    left_out = nt(picked, low_all[...]).astype(bf16)
    chunk = 512 if hidden % 512 == 0 else hidden

    def one_chunk(k, carry):
        cols = pl.ds(pl.multiple_of(k * chunk, 128), chunk)
        u = nn(normed_all[tokens:, :], w_in[:, cols])
        t = jnp.tanh(curve * (u + cubic * (u * u * u)))
        other_act = (0.5 * u * (1.0 + t)).astype(bf16)
        slope = 0.5 * (1.0 + t) + 0.5 * u * (1.0 - t * t) * (curve * (1.0 + 3.0 * cubic * (u * u)))
        other_hid = (nt(low_all[tokens:, :], w_out[cols, :]) * slope).astype(bf16)
        total[:, cols] = nn(left_in[:, :tokens], hid[:, cols]) + nn(left_in[:, tokens:], other_hid)
        total[:, pl.ds(pl.multiple_of(hidden + k * chunk, 128), chunk)] = nn(
            left_out[:, :tokens], act[:, cols]
        ) + nn(left_out[:, tokens:], other_act)
        return carry

    lax.fori_loop(0, hidden // chunk, one_chunk, 0)
    split_entries(0, lambda i: total[pl.ds(pl.multiple_of(i * rows, 8), rows), :], send_out, keep_out, rows)


class Fetched:
    def __init__(self, ref, copy):
        self.ref, self.copy, self.shape, self.dtype = ref, copy, ref.shape, ref.dtype

    def arrive(self):
        if self.copy is not None:
            self.copy.wait()
            self.copy = None

    def __getitem__(self, place):
        self.arrive()
        return self.ref[place]


class Leaving:
    def __init__(self, ref, copy):
        self.ref, self.copy, self.shape, self.dtype = ref, copy, ref.shape, ref.dtype
        self.left = False

    def leave(self):
        if not self.left:
            self.copy.start()
            self.left = True

    def __getitem__(self, place):
        return self.ref[place]

    def __setitem__(self, place, value):
        self.ref[place] = value


SPACES = {"v": pltpu.VMEM, "h": pltpu.HBM, "a": pl.ANY}


def call(kernel, outs, args, scratch=(), after=(), limit=20, cost=1):
    kinds = [kind for _, kind, *_ in args]
    fetched = [k for k, kind in enumerate(kinds) if kind != "v"]
    written = [k for k, (_, _, kind) in enumerate(outs) if kind != "v"]

    def body(*refs):
        ins, rest = list(refs[: len(args)]), refs[len(args) + len(after) :]
        results, rest = list(rest[: len(outs)]), rest[len(outs) :]
        in_bufs, rest = rest[: len(fetched)], rest[len(fetched) :]
        out_bufs, rest = rest[: len(written)], rest[len(written) :]
        extra, rest = rest[: len(scratch)], rest[len(scratch) :]
        sems = rest[0] if rest else None
        waits = []
        for n, (k, buf) in enumerate(zip(fetched, in_bufs)):
            source = ins[k]
            if len(args[k]) > 2:
                source = source.at[pl.ds(args[k][2], buf.shape[0])]
            copy = pltpu.make_async_copy(source, buf, sems.at[n])
            copy.start()
            ins[k] = Fetched(buf, copy)
            waits.append(ins[k])
        leaving = []
        for n, (k, buf) in enumerate(zip(written, out_bufs)):
            results[k] = Leaving(buf, pltpu.make_async_copy(buf, results[k], sems.at[len(fetched) + n]))
            leaving.append(results[k])
        kernel(*ins, *results, *extra)
        for out in leaving:
            out.leave()
        for wait in waits:
            wait.arrive()
        for out in leaving:
            out.copy.wait()

    places = {kind: pl.BlockSpec(memory_space=space) for kind, space in SPACES.items()}
    shapes = [
        pltpu.VMEM((args[k][3:] or args[k][0].shape[:1]) + args[k][0].shape[1:], args[k][0].dtype) for k in fetched
    ]
    shapes += [pltpu.VMEM(outs[k][0], outs[k][1]) for k in written]
    shapes += [pltpu.VMEM(shape, kind) for shape, kind in scratch]
    if fetched or written:
        shapes.append(pltpu.SemaphoreType.DMA((len(fetched) + len(written),)))
    name = getattr(kernel, "__name__", None) or kernel.func.__name__
    return pl.pallas_call(
        body,
        out_shape=[
            pltpu.HBM(shape, kind) if place == "h" else jax.ShapeDtypeStruct(shape, kind) for shape, kind, place in outs
        ],
        in_specs=[places[kind] for kind in kinds] + [places["a"]] * len(after),
        out_specs=[places[kind] for _, _, kind in outs],
        scratch_shapes=shapes,
        compiler_params=pltpu.CompilerParams(vmem_limit_bytes=limit * 1024 * 1024),
        cost_estimate=pl.CostEstimate(flops=cost * 35 * 10**9, transcendentals=0, bytes_accessed=1000),
        name=name,
    )(
        *[
            pltpu.with_memory_space_constraint(value, pltpu.HBM) if kind == "h" else value
            for value, kind, *_ in args
        ],
        *after,
    )


def pair_swap(values):
    return lax.ppermute(values, "mp", [(0, 1), (1, 0)])


def swap_bit(values, bit, count):
    return lax.ppermute(values, "dp", [(k, k ^ (1 << bit)) for k in range(count)])


def stage_swap(values, stage, count):
    bits = ((0, 1), (1, 0), (2, 3), (3, 2))[stage]
    pairs = [(2 * k + core, 2 * (k ^ (1 << bits[core])) + core) for k in range(count) for core in range(2)]
    return lax.ppermute(values, ("dp", "mp"), pairs)


def half_of(values, dim, which):
    return lax.dynamic_index_in_dim(values, which, dim, keepdims=False)


def scatter_sum(blocks, order, count):
    place = lax.axis_index("dp")
    levels = len(order)
    left = list(reversed(range(levels)))
    blocks = blocks.reshape((2,) * levels + blocks.shape[1:])
    for bit in order:
        dim = left.index(bit)
        mine = (place >> bit) & 1
        moved = swap_bit(half_of(blocks, dim, 1 - mine), bit, count)
        blocks = half_of(blocks, dim, mine) + moved
        left.remove(bit)
    return blocks


def full_sum(values, count):
    for bit in range(count.bit_length() - 1):
        values = values + swap_bit(values, bit, count)
    return values


def on_device(
    dec_input, enc_output, dec_lengths, enc_lengths, self_query, self_key, self_value, self_output, self_gain,
    rel_bias, cross_query, cross_key, cross_value, cross_output, cross_gain, ffn_in, ffn_out, ffn_gain, cotangent
):
    slots, width = dec_input.shape[1:]
    steps = enc_output.shape[1]
    inner = self_query.shape[1]
    hidden = ffn_in.shape[1]
    tokens = 3 * slots // 2
    count = lax.axis_size("dp")
    quick = count == 16
    row, half_row = (tokens, width), (tokens // 2, width)
    part_of = (tokens, inner)
    wide = 4 * inner
    share = width // count

    bias_rows = rel_bias.T
    tall = tokens // 2 + 8
    x, low_ffn, qkv, att_self, lse_self, part_self, x_half = call(
        self_forward,
        [(row, bf16, "h"), (row, bf16, "h"), ((tokens, 3 * inner), bf16, "h"), (part_of, bf16, "v"),
         ((8, tokens), f32, "v"), (row, f32, "v"), ((tall, width), f32, "h")],
        [(dec_lengths, "h"), (dec_input, "h"), (self_gain, "h"), (self_query, "h"), (self_key, "h"), (self_value, "h"),
         (cotangent, "h"), (bias_rows, "h"), (self_output, "h")],
    )
    moved_self = pair_swap(part_self)
    if quick:
        x_moved = stage_swap(x_half, 0, count)
    keys, values_t, keys_far, values, keys_t = call(
        encoder_forward,
        [((2 * steps, inner), bf16, "v"), ((inner, 2 * steps), bf16, "v")] + [((2 * steps, inner), bf16, "h")] * 2
        + [((inner, 2 * steps), bf16, "h")],
        [(enc_output, "v"), (cross_key, "v"), (cross_value, "v")],
        after=(part_self,),
    )
    after_self, cross_q, att_cross, lse_cross, part_cross = call(
        cross_forward,
        [(row, f32, "v"), (part_of, bf16, "h"), (part_of, bf16, "v"), ((8, 2 * slots), f32, "v"), (row, f32, "v")],
        [(dec_lengths, "v"), (enc_lengths, "v"), (x, "v"), (part_self, "v"), (moved_self, "v"), (cross_gain, "v"),
         (cross_query, "v"), (cross_output, "v"), (keys, "v"), (values_t, "v")],
    )
    moved_cross = pair_swap(part_cross)
    after = (part_cross,)
    if quick:
        early, own_cross = call(
            pack_early,
            [(row, f32, "v"), ((width // 2, tokens), bf16, "v")],
            [(after_self, "v"), (cross_gain, "v"), (att_cross, "v")],
            after=after,
        )
        early_moved = stage_swap(early, 0, count)
        after = (early,)
    after_cross, normed_ffn, halves, act, hid, back, *x_two = call(
        ffn_both,
        [(row, f32, "v"), (row, bf16, "h"), (row, f32, "v"), ((tokens, hidden), bf16, "v"), ((tokens, hidden), bf16, "v"),
         (row, f32, "v")] + [((2 * tall, width), f32, "v")] * quick,
        [(after_self, "v"), (part_cross, "v"), (moved_cross, "v"), (ffn_gain, "v"), (low_ffn, "v"), (ffn_in, "v"),
         (ffn_out, "v")] + ([(x_half, "v"), (x_moved, "v")] if quick else []),
        after=after,
    )
    moved_back = pair_swap(back)
    if quick:
        group_a = stage_swap(halves, 2, count)
        x_rest = stage_swap(x_two[0], 1, count)
    grad_cross, low_cross, dq, dk, dv, gain_ffn_grad, part_dq = call(
        cross_backward,
        [(row, f32, "h"), (row, bf16, "v"), (part_of, bf16, "v")] + [((2 * steps, inner), bf16, "v")] * 2
        + [((1, width), f32, "v"), (row, f32, "v")],
        [(dec_lengths, "v"), (enc_lengths, "v"), (after_cross, "v"), (back, "v"), (moved_back, "v"), (ffn_gain, "v"),
         (low_ffn, "v"), (cross_output, "v"), (cross_query, "v"), (cross_q, "v"), (keys_far, "v"), (values, "v"),
         (keys_t, "v"), (lse_cross, "v")],
        after=(rest(back),),
    )
    moved_dq = pair_swap(part_dq)
    after = (rest(part_dq), early_moved) if quick else (rest(part_dq),)
    grad_self, low_self, self_half, gain_cross_grad = call(
        self_grad,
        [(row, f32, "v"), (row, bf16, "v"), ((tokens // 2, width), f32, "v"), ((1, width), f32, "v")],
        [(after_self, "v"), (part_dq, "v"), (moved_dq, "v"), (cross_gain, "v"), (grad_cross, "v")],
        after=after,
    )
    after = (low_self,)
    half = width // 2
    if quick:
        self_a = stage_swap(self_half, 0, count)
    dqkv, bias_grad, parts = call(
        back_all,
        [((tokens, 3 * inner), bf16, "v"), ((8, rel_bias.shape[0]), f32, "v"), ((2 * tokens + 2 * steps, width), f32, "v")],
        [(dec_lengths, "v"), (low_self, "v"), (bias_rows, "v"), (self_output, "v"), (self_query, "v"), (self_key, "v"),
         (self_value, "v"), (qkv, "v"), (lse_self, "v"), (dk, "v"), (dv, "v"), (cross_key, "v"), (cross_value, "v"),
         (act, "v"), (ffn_out, "v")],
        after=after,
    )
    parts_moved = pair_swap(parts)
    after = (rest(parts),)
    if quick:
        self_two, halves_two = call(
            collect,
            [(row, f32, "v"), ((2 * tokens, width), f32, "v")],
            [(self_half, "v"), (self_a, "v"), (halves, "v"), (group_a, "v")],
            after=(parts, x_rest),
        )
        self_rest = stage_swap(self_two, 1, count)
        group_rest = stage_swap(halves_two, 3, count)
        (late_cross,) = call(
            cross_weights,
            [((half + tokens, 2 * inner), f32, "v")],
            [(enc_output, "v"), (dk, "v"), (dv, "v"), (dq, "v"), (low_cross, "v")],
            after=(self_two,),
        )
        late_cross_moved = stage_swap(late_cross, 0, count)
        (self_here,) = call(
            gather_self,
            [((3 * tall + 3 * tokens // 2, width), f32, "v")],
            [(x_moved, "v"), (x_rest, "v"), (self_a, "v"), (self_rest, "v")],
            after=(late_cross,),
        )
        self_there = pair_swap(self_here)
        after = (rest(self_here),)
    dec_packed, small = call(
        named(finish_self_norm, rel_bias.shape[1]),
        [(row, bf16, "v"), ((8, half), f32, "v")],
        [(x, "v"), (parts, "v"), (parts_moved, "v"), (self_gain, "v"), (grad_self, "v"),
         (gain_ffn_grad, "v"), (gain_cross_grad, "v"), (bias_grad, "v")],
        after=after,
    )
    if quick:
        small_moved = stage_swap(small, 0, count)
    after = (small,)
    if quick:
        send_self, keep_self = call(
            self_group,
            [((2 * share, wide), f32, "v")] * 2,
            [(x, "v"), (dqkv, "v"), (low_self, "v"), (att_self, "v"), (self_here, "v"), (self_there, "v"),
             (self_gain, "v"), (bias_rows, "v"), (self_query, "v"), (self_key, "v"), (self_value, "v"), (self_output, "v")],
            scratch=[((3 * tokens, wide), bf16), ((4 * tokens, wide), bf16), ((4 * share, wide), f32)],
            after=after,
        )
        self_first = stage_swap(send_self, 2, count)
        after = (send_self,)
    mark = ((8, 128), f32, "v")

    def outputs(after):
        return call(
            finish_outputs,
            [(dec_input.shape, bf16, "v"), (dec_input.shape, bf16, "v"), (enc_output.shape, bf16, "v"), mark],
            [(dec_lengths, "v"), (dec_packed, "v"), (parts, "v"), (parts_moved, "v"), (after_cross, "v")],
            after=after,
        )

    if not quick:
        dec_grad, layer_out, enc_grad, done = outputs(after)
        return slow_sums(
            locals(), x, after_self, self_gain, cross_gain, rel_bias, enc_output, count
        )
    (keep_cross,) = call(
        cross_keep, [((half, 2 * inner), f32, "v")], [(enc_output, "v"), (dk, "v"), (dv, "v")], after=(send_self,)
    )
    send_cross, keep_cross, small_two = call(
        cross_fold,
        [((half // 2 + 8, wide), f32, "v"), ((half // 2, wide), f32, "v"), ((16, half), f32, "v")],
        [(keep_cross, "v"), (late_cross_moved, "a", half, tokens), (late_cross_moved, "a", 0, half), (early_moved, "v"), (own_cross, "v"), (dq, "v"),
         (low_cross, "v"), (att_cross, "v"), (small, "v"), (small_moved, "v")],
        scratch=[((half, wide), f32)],
        after=(keep_cross,),
    )
    cross_first = stage_swap(send_cross, 1, count)
    (ffn_here,) = call(
        gather_ffn, [((3 * tokens, width), f32, "v")], [(group_a, "v"), (group_rest, "v")], after=(send_cross,)
    )
    ffn_there = pair_swap(ffn_here)
    dec_grad, layer_out, enc_grad, done = outputs((ffn_here,))
    made_ffn, keep_ffn = call(
        ffn_group,
        [((2 * share, 2 * hidden), f32, "v")] * 2,
        [(normed_ffn, "v"), (low_ffn, "v"), (act, "v"), (hid, "v"), (ffn_here, "v"), (ffn_there, "v"), (ffn_in, "v"),
         (ffn_out, "v")],
        scratch=[((4 * tokens, width), bf16), ((4 * tokens, width), bf16), ((4 * share, 2 * hidden), f32)],
        after=(done,),
    )
    (send_self2,) = call(
        named(self_fold, share), [((share, wide), f32, "v")], [(keep_self, "v"), (self_first, "v")], after=(made_ffn,)
    )
    self_second = stage_swap(send_self2, 3, count)
    send_cross2, small_four = call(
        named(fold_z, share),
        [((half // 4 + 8, wide), f32, "v"), ((8, half), f32, "v")],
        [(keep_cross, "v"), (small_two, "v"), (cross_first, "v")],
        after=(send_self2,),
    )
    cross_second = stage_swap(send_cross2, 2, count)
    (send_ffn,) = call(relay, [((2 * share, 2 * hidden), f32, "v")], [(made_ffn, "v")], after=(send_cross2,))
    ffn_first = stage_swap(send_ffn, 0, count)
    *self_grads, self_out_grad, done = call(
        named(finish_self, share),
        [((share, inner), f32, "v")] * 4 + [mark],
        [(keep_self, "v"), (self_first, "v"), (self_second, "v")],
        after=(send_ffn,),
    )
    (send_ffn2,) = call(
        named(ffn_fold, share), [((share, 2 * hidden), f32, "v")], [(keep_ffn, "v"), (ffn_first, "v")], after=(done,)
    )
    ffn_second = stage_swap(send_ffn2, 1, count)
    send_cross3, small_last = call(
        named(fold_last, share),
        [((share + 8, wide), f32, "v"), ((16, half), f32, "v")],
        [(keep_cross, "v"), (small_four, "v"), (cross_first, "v"), (cross_second, "v")],
        after=(send_ffn2,),
    )
    cross_third = stage_swap(send_cross3, 3, count)
    grad_ffn_in, grad_ffn_out, done = call(
        named(finish_ffn, share),
        [((share, hidden), f32, "h")] * 2 + [mark],
        [(keep_ffn, "v"), (ffn_first, "v"), (ffn_second, "v")],
        after=(rest(send_cross3),),
    )
    *cross_grads, cross_out_grad, gain_self_sum, gain_cross_sum, gain_ffn_sum, bias_sum = call(
        named(finish_cross, rel_bias.shape[1], share),
        [((share, inner), f32, "h")] * 4 + [((width,), f32, "h")] * 3 + [(rel_bias.shape[::-1], f32, "h")],
        [(keep_cross, "v"), (cross_first, "v"), (cross_second, "v"), (small_last, "v"), (cross_third, "v")],
        after=(done,),
    )
    return (
        layer_out,
        dec_grad,
        enc_grad,
        *self_grads,
        self_out_grad.T,
        gain_self_sum,
        bias_sum.T,
        *cross_grads,
        cross_out_grad.T,
        gain_cross_sum,
        grad_ffn_in,
        grad_ffn_out.T,
        gain_ffn_sum,
    )


def rest(made):
    (out,) = call(pause, [((8, 128), f32, "v")], [], after=(made,))
    return out


def named(kernel, *given):
    def run(*refs):
        return kernel(*given, *refs)

    run.__name__ = kernel.__name__
    return run


def slow_sums(made, x, after_self, self_gain, cross_gain, rel_bias, enc_output, count):
    width = x.shape[1]
    heads, buckets = rel_bias.shape[1], rel_bias.shape[0]
    inner = made["dq"].shape[1]
    bits = list(range(count.bit_length() - 1))
    order_a, order_b = bits, bits[1::-1] + bits[2:]

    def scattered(order, *grads):
        parts = [grad.reshape(count, -1, grad.shape[1]) for grad in grads]
        widths = [part.shape[2] for part in parts]
        total = scatter_sum(jnp.concatenate(parts, axis=2), order, count)
        return jnp.split(total, np.cumsum(widths)[:-1].tolist(), axis=1)

    def outer(left, right):
        return jnp.einsum("rm,rn->mn", left, right, preferred_element_type=f32)

    def normed(values, gain):
        return (values * inverse_rms(values) * gain).astype(bf16)

    normed_self = normed(x.astype(f32), self_gain)
    normed_cross = normed(after_self, cross_gain)
    enc_flat = enc_output.reshape(-1, width)
    dqkv = made["dqkv"]
    (grad_ffn_in,) = scattered(order_a, outer(made["normed_ffn"], made["hid"]))
    (grad_ffn_out,) = scattered(order_b, outer(made["low_ffn"], made["act"]))
    cross_query, cross_key = scattered(order_a, outer(normed_cross, made["dq"]), outer(enc_flat, made["dk"]))
    cross_value, cross_output = scattered(
        order_b, outer(enc_flat, made["dv"]), outer(made["low_cross"], made["att_cross"])
    )
    self_query, self_key = scattered(
        order_a, outer(normed_self, dqkv[:, :inner]), outer(normed_self, dqkv[:, inner : 2 * inner])
    )
    self_value, self_output = scattered(
        order_b, outer(normed_self, dqkv[:, 2 * inner :]), outer(made["low_self"], made["att_self"])
    )
    small = full_sum(made["small"], count)
    return (
        made["layer_out"],
        made["dec_grad"],
        made["enc_grad"],
        self_query,
        self_key,
        self_value,
        self_output.T,
        small[0:2].reshape(-1),
        small[6, : heads * buckets].reshape(heads, buckets).T,
        cross_query,
        cross_key,
        cross_value,
        cross_output.T,
        small[2:4].reshape(-1),
        grad_ffn_in,
        grad_ffn_out.T,
        small[4:6].reshape(-1),
    )


def solution(mesh):
    in_specs = (
        P("dp", None, None),
        P("dp", None, None),
        P("dp", None),
        P("dp", None),
        P(None, "mp"),
        P(None, "mp"),
        P(None, "mp"),
        P("mp", None),
        P(),
        P(None, "mp"),
        P(None, "mp"),
        P(None, "mp"),
        P(None, "mp"),
        P("mp", None),
        P(),
        P(None, "mp"),
        P("mp", None),
        P(),
        P("dp", None, None),
    )
    out_specs = (
        P("dp", None, None),
        P("dp", None, None),
        P("dp", None, None),
        P("dp", "mp"),
        P("dp", "mp"),
        P("dp", "mp"),
        P("mp", "dp"),
        P(),
        P(None, "mp"),
        P("dp", "mp"),
        P("dp", "mp"),
        P("dp", "mp"),
        P("mp", "dp"),
        P(),
        P("dp", "mp"),
        P("mp", "dp"),
        P(),
    )
    return jax.shard_map(
        on_device, mesh=mesh, in_specs=in_specs, out_specs=out_specs, check_vma=False
    )
```

```python
import functools

import jax
import jax.numpy as jnp
import numpy as np
from jax import lax
from jax.experimental import pallas as pl
from jax.experimental.pallas import tpu as pltpu
from jax.sharding import PartitionSpec as P

epsilon = 1e-06
masked_value = -1e30
head_width = 64
pair_width = 2 * head_width
bf16 = jnp.bfloat16
f32 = jnp.float32
curve = 0.7978845608028654
cubic = 0.044715


def nn(left, right, precision=None):
    return lax.dot_general(
        left, right, (((1,), (0,)), ((), ())), precision=precision, preferred_element_type=f32
    )


def nt(left, right, precision=None):
    return lax.dot_general(
        left, right, (((1,), (1,)), ((), ())), precision=precision, preferred_element_type=f32
    )


def tn(left, right, precision=None):
    return lax.dot_general(
        left, right, (((0,), (0,)), ((), ())), precision=precision, preferred_element_type=f32
    )


def gain_row(gain):
    return gain[...].reshape(1, gain.shape[0])


def iota(shape, dim):
    return lax.broadcasted_iota(jnp.int32, shape, dim)


def inverse_rms(values):
    return lax.rsqrt(jnp.sum(values * values, -1, keepdims=True) / values.shape[-1] + epsilon)


def norm_back(values, gain, upstream):
    inverse = inverse_rms(values)
    scaled = upstream * gain
    mean = jnp.sum(scaled * values, -1, keepdims=True) / values.shape[-1]
    gain_grad = jnp.sum(upstream * values * inverse, 0, keepdims=True)
    return inverse * scaled - values * (inverse * inverse * inverse * mean), gain_grad


def bucket_bounds(buckets):
    half = buckets // 2
    return [int(b) for b in np.ceil(16.0 * 8.0 ** (np.arange(1, half) / half))]


def bucket_rows(buckets, width):
    distance = iota((buckets, width), 1)
    coarse = jnp.full((buckets, width), buckets // 2, jnp.int32)
    for bound in bucket_bounds(buckets):
        coarse += (distance >= bound).astype(jnp.int32)
    chosen = jnp.where(distance < buckets // 2, distance, coarse)
    return (chosen == iota((buckets, width), 0)).astype(f32)


def half_masks():
    lane = iota((1, pair_width), 1)
    low = (lane < head_width).astype(f32)
    return low.astype(bf16), (1.0 - low).astype(bf16)


def pick_rows(first, tokens, slots):
    row, col = iota((tokens, 2 * slots), 0), iota((tokens, 2 * slots), 1)
    return (col == jnp.where(row < first, row, row + (slots - first))).astype(f32).astype(bf16)


def self_bias(bias_ref, width):
    return nn(
        bias_ref[...], bucket_rows(bias_ref.shape[1], width), precision=lax.Precision.HIGHEST
    )


def self_allowed(first, tokens):
    key, query = iota((tokens, tokens), 0), iota((tokens, tokens), 1)
    return (key <= query) & ((key < first) == (query < first))


def spread_bias(base, head, tokens):
    width = base.shape[1]
    rows = jnp.broadcast_to(base[head : head + 1], (tokens, width))
    return pltpu.roll(rows, 0, 1, stride=1, stride_axis=0)[:, :tokens]


def own_half(values):
    half = values.shape[0] // 2
    return jnp.where(lax.axis_index("mp") == 0, values[:half], values[half:])


def flush(out):
    if isinstance(out, Leaving):
        out.leave()


def self_forward(
    dec_len, dec, gain, w_q, w_k, w_v, cot, bias, w_o, x_out, low_out, qkv_out, att_out, lse_out, part_out, x_half
):
    slots, width = dec.shape[1], dec.shape[2]
    tokens = x_out.shape[0]
    heads = bias.shape[0]
    first = dec_len[:, 0:1]
    picked = pick_rows(first, tokens, slots)
    x = nn(picked, dec[...].reshape(2 * slots, width))
    x_out[...] = x.astype(bf16)
    flush(x_out)
    half = tokens // 2
    x_half[:half, :] = own_half(x)
    x_half[half:, :] = jnp.broadcast_to(first.astype(f32), (8, width))
    flush(x_half)
    normed = (x * inverse_rms(x) * gain_row(gain)).astype(bf16)
    inner = w_q.shape[1]
    for k, w in enumerate((w_q, w_k, w_v)):
        qkv_out[:, k * inner : (k + 1) * inner] = nn(normed, w[...]).astype(bf16)
    flush(qkv_out)
    low_out[...] = nn(picked, cot[...].reshape(2 * slots, width)).astype(bf16)
    flush(low_out)
    base = self_bias(bias, 2 * slots)
    allowed = self_allowed(first, tokens)
    masks = half_masks()
    top = iota((pair_width, tokens), 0) < head_width
    lse_out[...] = jnp.zeros_like(lse_out)
    for pair in range(heads // 2):
        lanes = slice(pair * pair_width, (pair + 1) * pair_width)
        q = qkv_out[:, lanes]
        k = qkv_out[:, inner + pair * pair_width : inner + (pair + 1) * pair_width]
        v = qkv_out[:, 2 * inner + pair * pair_width : 2 * inner + (pair + 1) * pair_width]
        v_t = v.astype(f32).T.astype(bf16)
        mixed = []
        for side in range(2):
            head = 2 * pair + side
            scores = nt(k, q * masks[side]) + spread_bias(base, head, tokens)
            scores = jnp.where(allowed, scores, masked_value)
            top_score = jnp.max(scores, 0, keepdims=True)
            weights = jnp.exp(scores - top_score)
            total = jnp.sum(weights, 0, keepdims=True)
            lse_out[head : head + 1, :] = top_score + jnp.log(total)
            mixed.append(nn(v_t, (weights * (1.0 / total)).astype(bf16)))
        att_out[:, lanes] = jnp.where(top, mixed[0], mixed[1]).T.astype(bf16)
    flush(att_out)
    flush(lse_out)
    part_out[...] = nn(att_out[...], w_o[...])


def encoder_forward(enc, w_k, w_v, k_out, vt_out, k_far, v_far, kt_far):
    steps = enc.shape[1]
    for w, out, out_t in ((w_v, v_far, vt_out), (w_k, k_out, kt_far)):
        for e in range(enc.shape[0]):
            rows = slice(e * steps, (e + 1) * steps)
            made = nn(enc[e], w[...])
            out[rows, :] = made.astype(bf16)
            out_t[:, rows] = made.T.astype(bf16)
        if out is v_far:
            flush(v_far)
    k_far[...] = k_out[...]


def cross_rows(first, tokens, slots, e):
    row = iota((slots, 1), 0) + e * (tokens - slots)
    return row < first if e == 0 else row >= first


def cross_forward(
    dec_len, enc_len, x, part, moved, gain, w_q, w_o, k_in, vt_in, after_out, q_out, att_out, lse_out, part_out
):
    tokens = x.shape[0]
    slots = 2 * tokens // 3
    steps = k_in.shape[0] // 2
    first = dec_len[:, 0:1]
    after = x[...].astype(f32) + (part[...] + moved[...])
    after_out[...] = after
    normed = (after * inverse_rms(after) * gain_row(gain)).astype(bf16)
    q_out[...] = nn(normed, w_q[...]).astype(bf16)
    flush(q_out)
    masks = half_masks()
    top = iota((pair_width, slots), 0) < head_width
    own = iota((tokens, 1), 0) < first
    lse_out[...] = jnp.zeros_like(lse_out)
    shift = tokens - slots
    for pair in range(q_out.shape[1] // pair_width):
        lanes = slice(pair * pair_width, (pair + 1) * pair_width)
        parts = []
        for e in range(2):
            q = q_out[e * shift : e * shift + slots, lanes]
            both = jnp.concatenate([q * masks[0], q * masks[1]], 0)
            scores = nt(k_in[e * steps : (e + 1) * steps, lanes], both)
            valid = iota((steps, 1), 0) < enc_len[:, e : e + 1]
            scores = jnp.where(valid, scores, masked_value)
            top_score = jnp.max(scores, 0, keepdims=True)
            weights = jnp.exp(scores - top_score)
            total = jnp.sum(weights, 0, keepdims=True)
            lse_out[2 * pair + e : 2 * pair + e + 1, :] = top_score + jnp.log(total)
            mixed = nn(
                vt_in[lanes, e * steps : (e + 1) * steps], (weights * (1.0 / total)).astype(bf16)
            )
            parts.append(jnp.where(top, mixed[:, :slots], mixed[:, slots:]).T)
        fill = jnp.zeros((shift, pair_width), f32)
        att_out[:, lanes] = jnp.where(
            own, jnp.concatenate([parts[0], fill], 0), jnp.concatenate([fill, parts[1]], 0)
        ).astype(bf16)
    flush(lse_out)
    part_out[...] = nn(att_out[...], w_o[...])


def ffn_both(
    after, part, moved, gain, low, w_in, w_out, *outs
):
    if len(outs) > 6:
        x_half, x_moved, *outs, x_rest = outs
        stack(x_rest, x_half, x_moved)
    after_out, normed_out, halves_out, act_out, hid_out, back_out = outs
    total = after[...] + (part[...] + moved[...])
    after_out[...] = total
    normed = (total * inverse_rms(total) * gain_row(gain)).astype(bf16)
    normed_out[...] = normed
    flush(normed_out)
    low_in = low[...]
    half = low_in.shape[0] // 2
    halves_out[:half, :] = own_half(low_in.astype(f32))
    halves_out[half:, :] = own_half(normed.astype(f32))
    hidden = w_in.shape[1]
    chunk = 512 if hidden % 512 == 0 else hidden
    for start in range(0, hidden, chunk):
        cols = slice(start, start + chunk)
        u = nn(normed, w_in[:, cols])
        t = jnp.tanh(curve * (u + cubic * (u * u * u)))
        act = (0.5 * u * (1.0 + t)).astype(bf16)
        slope = 0.5 * (1.0 + t) + 0.5 * u * (1.0 - t * t) * (curve * (1.0 + 3.0 * cubic * (u * u)))
        hid = (nt(low_in, w_out[cols, :]) * slope).astype(bf16)
        act_out[:, cols] = act
        hid_out[:, cols] = hid
        backward = nt(hid, w_in[:, cols])
        if start == 0:
            back_out[...] = backward
        else:
            back_out[...] += backward


def cross_backward(
    dec_len, enc_len, after, part, moved, gain, low, w_o, w_q, q_in, k_in, v_in, kt_in, lse,
    grad_out, low_out, dq_out, dk_out, dv_out, gain_out, part_out
):
    tokens = after.shape[0]
    slots = 2 * tokens // 3
    steps = k_in.shape[0] // 2
    first = dec_len[:, 0:1]
    shift = tokens - slots
    norm_in, gain_grad = norm_back(after[...], gain_row(gain), part[...] + moved[...])
    gain_out[...] = gain_grad
    flush(gain_out)
    grad = low[...].astype(f32) + norm_in
    grad_out[...] = grad
    flush(grad_out)
    low_grad = grad.astype(bf16)
    low_out[...] = low_grad
    flush(low_out)
    g_all = nt(low_grad, w_o[...])
    masks = half_masks()
    top = iota((pair_width, slots), 0) < head_width
    for pair in range(q_in.shape[1] // pair_width):
        lanes = slice(pair * pair_width, (pair + 1) * pair_width)
        parts = []
        for e in range(2):
            keys = slice(e * steps, (e + 1) * steps)
            window = slice(e * shift, e * shift + slots)
            q = q_in[window, lanes]
            g = jnp.where(cross_rows(first, tokens, slots, e), g_all[window, lanes], 0.0)
            g = g.astype(bf16)
            q_both = jnp.concatenate([q * masks[0], q * masks[1]], 0)
            g_both = jnp.concatenate([g * masks[0], g * masks[1]], 0)
            valid = iota((steps, 1), 0) < enc_len[:, e : e + 1]
            scores = jnp.where(valid, nt(k_in[keys, lanes], q_both), masked_value)
            p = jnp.exp(scores - lse[2 * pair + e : 2 * pair + e + 1, :])
            dp = nt(v_in[keys, lanes], g_both)
            ds = (p * (dp - jnp.sum(p * dp, 0, keepdims=True))).astype(bf16)
            dk_out[keys, lanes] = nn(ds, q_both).astype(bf16)
            dv_out[keys, lanes] = nn(p.astype(bf16), g_both).astype(bf16)
            dq = nn(kt_in[lanes, keys], ds)
            parts.append(jnp.where(top, dq[:, :slots], dq[:, slots:]).T)
        fill = jnp.zeros((shift, pair_width), f32)
        dq_out[:, lanes] = (
            jnp.concatenate([parts[0], fill], 0) + jnp.concatenate([fill, parts[1]], 0)
        ).astype(bf16)
    part_out[...] = nt(dq_out[...], w_q[...])


def self_grad(after, part, moved, gain, grad_in, grad_out, low_out, half_out, gain_out):
    norm_in, gain_grad = norm_back(after[...], gain_row(gain), part[...] + moved[...])
    gain_out[...] = gain_grad
    grad = grad_in[...] + norm_in
    grad_out[...] = grad
    low = grad.astype(bf16)
    low_out[...] = low
    half_out[...] = own_half(low.astype(f32))


def back_all(
    dec_len, low, bias, w_o, w_q, w_k, w_v, qkv, lse, dk, dv, w_ck, w_cv, act, w_ffn, dqkv_out, bias_out, part_out
):
    tokens = low.shape[0]
    self_backward(
        dec_len, low, bias, w_o, w_q, w_k, w_v, qkv, lse, dqkv_out, bias_out, part_out.at[pl.ds(0, tokens), :]
    )
    part_out[tokens : 2 * tokens, :] = nn(act[...], w_ffn[...])
    steps = dk.shape[0] // 2
    for e in range(2):
        rows = slice(e * steps, (e + 1) * steps)
        part_out[2 * tokens + e * steps : 2 * tokens + (e + 1) * steps, :] = nt(dk[rows, :], w_ck[...]) + nt(
            dv[rows, :], w_cv[...]
        )


def self_backward(dec_len, low, bias, w_o, w_q, w_k, w_v, qkv, lse, dqkv_out, bias_out, part_out):
    tokens = low.shape[0]
    heads = bias.shape[0]
    first = dec_len[:, 0:1]
    inner = w_q.shape[1]
    g_all = nt(low[...], w_o[...]).astype(bf16)
    reach = 4 * tokens // 3
    base = self_bias(bias, reach)
    allowed = self_allowed(first, tokens)
    masks = half_masks()
    top = iota((pair_width, tokens), 0) < head_width
    diagonals = []
    for pair in range(heads // 2):
        lanes = slice(pair * pair_width, (pair + 1) * pair_width)
        k_lanes = slice(inner + pair * pair_width, inner + (pair + 1) * pair_width)
        v_lanes = slice(2 * inner + pair * pair_width, 2 * inner + (pair + 1) * pair_width)
        q, k, v, g = qkv[:, lanes], qkv[:, k_lanes], qkv[:, v_lanes], g_all[:, lanes]
        k_t = k.astype(f32).T.astype(bf16)
        dk, dv, dq = 0.0, 0.0, []
        for side in range(2):
            head = 2 * pair + side
            q_half, g_half = q * masks[side], g * masks[side]
            scores = nt(k, q_half) + spread_bias(base, head, tokens)
            scores = jnp.where(allowed, scores, masked_value)
            p = jnp.exp(scores - lse[head : head + 1, :])
            dp = nt(v, g_half)
            ds = p * (dp - jnp.sum(p * dp, 0, keepdims=True))
            ds_low = ds.astype(bf16)
            dk += nn(ds_low, q_half)
            dv += nn(p.astype(bf16), g_half)
            dq.append(nn(k_t, ds_low))
            wide = jnp.concatenate([ds, jnp.zeros((tokens, reach - tokens), f32)], 1)
            total = wide[:8]
            for start in range(8, tokens, 8):
                total += pltpu.roll(wide[start : start + 8], reach - start, 1)
            diagonals.append(total)
        dqkv_out[:, lanes] = jnp.where(top, dq[0], dq[1]).T.astype(bf16)
        dqkv_out[:, k_lanes] = dk.astype(bf16)
        dqkv_out[:, v_lanes] = dv.astype(bf16)
    flush(dqkv_out)
    part_out[...] = (
        nt(dqkv_out[:, :inner], w_q[...])
        + nt(dqkv_out[:, inner : 2 * inner], w_k[...])
        + nt(dqkv_out[:, 2 * inner :], w_v[...])
    )
    total = jnp.concatenate(diagonals, 0)
    row = iota(total.shape, 0) & 7
    lined = jnp.zeros_like(total)
    for s in range(8):
        lined += jnp.where(row == s, pltpu.roll(total, (reach - s) % reach, 1), 0.0)
    head_of = ((iota((8, 8 * heads), 1) >> 3) == iota((8, 8 * heads), 0)).astype(f32)
    by_head = nn(head_of, lined, precision=lax.Precision.HIGHEST)
    bias_out[...] = nt(by_head, bucket_rows(bias.shape[1], reach), precision=lax.Precision.HIGHEST)


def unpacked(values, first, slots):
    tokens = values.shape[0]
    slot, row = iota((2 * slots, tokens), 0), iota((2 * slots, tokens), 1)
    limit = jnp.where(slot < slots, first, slots + tokens - first)
    wanted = jnp.where(slot < slots, slot, slot - slots + first)
    spread = ((row == wanted) & (slot < limit)).astype(f32).astype(bf16)
    return nn(spread, values.astype(bf16)).astype(bf16)


def finish_self_norm(
    heads, x, part, moved, gain, grad_in, gain_ffn, gain_cross, bias_grad, dec_out, small_out
):
    tokens, width = x.shape
    norm_in, gain_grad = norm_back(x[...].astype(f32), gain_row(gain), part[:tokens, :] + moved[:tokens, :])
    half, buckets = small_out.shape[1], bias_grad.shape[1]
    small_out[...] = jnp.zeros_like(small_out)
    for k, value in enumerate((gain_grad, gain_cross[...], gain_ffn[...])):
        small_out[2 * k : 2 * k + 1, :] = value[:, :half]
        small_out[2 * k + 1 : 2 * k + 2, :] = value[:, half:]
    small_out[6:7, : heads * buckets] = jnp.concatenate([bias_grad[h : h + 1, :] for h in range(heads)], 1)
    dec_out[...] = (grad_in[...] + norm_in).astype(bf16)


def finish_outputs(dec_len, dec, part, moved, after, dec_out, layer_out, enc_out, token):
    token[...] = jnp.zeros_like(token)
    tokens = dec.shape[0]
    first, slots = dec_len[:, 0:1], dec_out.shape[1]
    dec_out[...] = unpacked(dec[...], first, slots).reshape(dec_out.shape)
    total = after[...] + (part[tokens : 2 * tokens, :] + moved[tokens : 2 * tokens, :])
    layer_out[...] = unpacked(total, first, slots).reshape(layer_out.shape)
    enc_out[...] = (part[2 * tokens :, :] + moved[2 * tokens :, :]).astype(bf16).reshape(enc_out.shape)


def pause(out):
    out[...] = jnp.zeros_like(out)


def collect(low_half, low_a, halves, group_a, low_out, group_out):
    stack(low_out, low_half, low_a)
    stack(group_out, halves, group_a)


def gather_self(x_moved, x_rest, low_a, low_rest, out):
    stack(out, x_moved, x_rest, low_a, low_rest)


def relay(value, out):
    out[...] = value[...]


def gather_ffn(group_a, group_rest, out):
    stack(out, group_a, group_rest)


def place_of():
    return lax.axis_index("dp"), lax.axis_index("mp")


def own_bit(stage):
    place, core = place_of()
    shift = (core, 1 - core, 2 + core, 3 - core)[stage]
    return lax.shift_right_logical(place, shift) & 1


def entry(stage, step, bit):
    if stage % 2:
        return 2 * step + bit
    core = lax.axis_index("mp")
    return jnp.where(core == 0, 2 * step + bit, (step // 2) * 4 + 2 * bit + step % 2)


def pick_chunks(chunks, rows, width):
    gap = iota((rows, width), 1) - iota((rows, width), 0)
    return jnp.concatenate([(gap == chunk * rows).astype(f32) for chunk in chunks], 0).astype(bf16)


def half_pick(other, width):
    bit = own_bit(0)
    bit = 1 - bit if other else bit
    return pick_chunks([entry(0, step, bit) for step in range(8)], width // 16, width)


def fold_lanes(values):
    half = values.shape[0] // 2
    return jnp.concatenate([values[:half], values[half:]], 1)


def unfold_lanes(values):
    half = values.shape[1] // 2
    return jnp.concatenate([values[:, :half], values[:, half:]], 0)


def split_entries(stage, source, send_out, keep_out, rows):
    bit = own_bit(stage)
    for step in range(keep_out.shape[0] // rows):
        here = slice(step * rows, (step + 1) * rows)
        send_out[here, :] = source(entry(stage, step, 1 - bit))
        keep_out[here, :] = source(entry(stage, step, bit))


def pack_early(after, gain, att, early_out, own):
    width = after.shape[1]
    inner = att.shape[1]
    v = after[...]
    normed = (v * inverse_rms(v) * gain_row(gain)).astype(bf16)
    own[...] = nt(half_pick(0, width), normed).astype(bf16)
    early_out[:, :inner] = fold_lanes(nt(half_pick(1, width), normed))
    early_out[:, inner:] = att[...].astype(f32)


def stack(out, *parts):
    at = 0
    for part in parts:
        out[at : at + part.shape[0], :] = part[...]
        at += part.shape[0]


def cross_weights(enc, dk, dv, dq, low, late_out):
    steps, width = enc.shape[1:]
    inner = dk.shape[1]
    half = width // 2
    left = nt(half_pick(1, width), enc[...].reshape(2 * steps, width)).astype(bf16)
    late_out[:half, :inner] = nn(left, dk[...])
    late_out[:half, inner:] = nn(left, dv[...])
    late_out[half:, :inner] = dq[...].astype(f32)
    late_out[half:, inner:] = fold_lanes(nt(half_pick(1, width), low[...]))


def cross_keep(enc, dk, dv, own, dq, low, att, keep_out):
    steps, width = enc.shape[1:]
    inner = dk.shape[1]
    left = nt(half_pick(0, width), enc[...].reshape(2 * steps, width)).astype(bf16)
    keep_out[:, :inner] = nn(own[...], dq[...])
    keep_out[:, inner : 2 * inner] = nn(left, dk[...])
    keep_out[:, 2 * inner : 3 * inner] = nn(left, dv[...])
    keep_out[:, 3 * inner :] = nn(nt(half_pick(0, width), low[...]).astype(bf16), att[...])


def side_by_side(out, at, small):
    n = small.shape[1]
    out[at:, :n] = small[:8, :]
    out[at:, n : 2 * n] = small[8:, :]
    out[at:, 2 * n :] = jnp.zeros_like(out[at:, 2 * n :])


def above(rows, n):
    return jnp.concatenate([rows[:, :n], rows[:, n : 2 * n]], 0)


def cross_fold(keep, factors, moved, early, small, small_moved, send_out, keep_out, small_out, total):
    half, inner = keep.shape[0], factors.shape[1] // 2
    rows = half // 8
    total[:, :inner] = keep[:, :inner] + nn(
        unfold_lanes(early[:, :inner]).astype(bf16), factors[:, :inner].astype(bf16)
    )
    total[:, 3 * inner :] = keep[:, 3 * inner :] + nn(
        unfold_lanes(factors[:, inner:]).astype(bf16), early[:, inner:].astype(bf16)
    )
    total[:, inner : 3 * inner] = keep[:, inner : 3 * inner] + moved[...]
    split_entries(1, lambda i: total[pl.ds(pl.multiple_of(i * rows, 8), rows), :], send_out, keep_out, rows)
    stack(small_out, small, small_moved)
    side_by_side(send_out, keep_out.shape[0], small_out)


def self_group(
    x, dqkv, low, att, here, there, gain, bias, w_q, w_k, w_v, w_o,
    send_out, keep_out, made, grads, total
):
    tokens, width = x.shape
    inner = att.shape[1]
    heads = bias.shape[0]
    half = tokens // 2
    place, core = place_of()
    rows = width // 16
    base = self_bias(bias, 4 * tokens // 3)
    masks = half_masks()
    top = iota((pair_width, tokens), 0) < head_width
    biases = [spread_bias(base, head, tokens) for head in range(heads)]
    tall = half + 8
    x_at, low_at = (0, tall, 2 * tall), (3 * tall, 3 * tall + half, 3 * tall + 2 * half)
    orders = ((0, 1), (1, 0), (2, 2))

    def joined(starts, mine, other):
        a, b = here[starts[mine] : starts[mine] + half, :], there[starts[other] : starts[other] + half, :]
        return [jnp.where(core == 0, a, b), jnp.where(core == 0, b, a)]

    v = jnp.concatenate([part for order in orders for part in joined(x_at, *order)], 0)
    normed = (v * inverse_rms(v) * gain_row(gain)).astype(bf16)
    low_all = jnp.concatenate([part for order in orders for part in joined(low_at, *order)], 0).astype(bf16)
    for k, w in enumerate((w_q, w_k, w_v)):
        made[:, k * inner : (k + 1) * inner] = nn(normed, w[...]).astype(bf16)
    made[:, 3 * inner :] = nt(low_all, w_o[...]).astype(bf16)
    grads[:tokens, : 3 * inner] = dqkv[...]
    grads[:tokens, 3 * inner :] = att[...]
    def one_chip(k, carry):
        first = here[pl.ds(pl.multiple_of(k * tall + half, 8), 8), :][0:1, 0:1].astype(jnp.int32)
        allowed = self_allowed(first, tokens)
        source = pl.ds(pl.multiple_of(k * tokens, 16), tokens)
        target = pl.ds(pl.multiple_of((k + 1) * tokens, 16), tokens)
        every = range(heads)
        lanes = [slice(pair * pair_width, (pair + 1) * pair_width) for pair in range(heads // 2)]
        q, key, value, g = (
            [made[source, n * inner + lane.start : n * inner + lane.stop] for lane in lanes] for n in range(4)
        )
        k_t = [part.astype(f32).T.astype(bf16) for part in key]
        v_t = [part.astype(f32).T.astype(bf16) for part in value]
        q_half = [q[h // 2] * masks[h % 2] for h in every]
        g_half = [g[h // 2] * masks[h % 2] for h in every]
        scores = [jnp.where(allowed, nt(key[h // 2], q_half[h]) + biases[h], masked_value) for h in every]
        weights = [jnp.exp(score - jnp.max(score, 0, keepdims=True)) for score in scores]
        p = [weight * (1.0 / jnp.sum(weight, 0, keepdims=True)) for weight in weights]
        dp = [nt(value[h // 2], g_half[h]) for h in every]
        ds = [(p[h] * (dp[h] - jnp.sum(p[h] * dp[h], 0, keepdims=True))).astype(bf16) for h in every]
        p = [part.astype(bf16) for part in p]
        dk = [nn(ds[h], q_half[h]) for h in every]
        dv = [nn(p[h], g_half[h]) for h in every]
        dq = [nn(k_t[h // 2], ds[h]) for h in every]
        mixed = [nn(v_t[h // 2], p[h]) for h in every]
        for pair, lane in enumerate(lanes):
            a, b = 2 * pair, 2 * pair + 1
            for n, part in enumerate(
                (jnp.where(top, dq[a], dq[b]).T, dk[a] + dk[b], dv[a] + dv[b], jnp.where(top, mixed[a], mixed[b]).T)
            ):
                grads[target, n * inner + lane.start : n * inner + lane.stop] = part.astype(bf16)
        return carry

    lax.fori_loop(0, 3, one_chip, 0)
    picked = pick_chunks([4 * z + (place & 3) for z in range(4)], rows, width)
    v = x[...].astype(f32)
    own = (v * inverse_rms(v) * gain_row(gain)).astype(bf16)
    left = jnp.concatenate([nt(picked, own), nt(picked, normed)], 1).astype(bf16)
    total[:, : 3 * inner] = nn(left, grads[:, : 3 * inner])
    left = jnp.concatenate([nt(picked, low[...]), nt(picked, low_all)], 1).astype(bf16)
    total[:, 3 * inner :] = nn(left, grads[:, 3 * inner :])
    split_entries(2, lambda i: total[pl.ds(pl.multiple_of(i * rows, 8), rows), :], send_out, keep_out, rows)


def chunk_of(ref, index, rows):
    return ref[pl.ds(pl.multiple_of(index * rows, 8), rows), :]


def entry_here(step):
    core, bit = lax.axis_index("mp"), own_bit(2)
    return jnp.where(core == 0, 2 * step + bit, 2 * bit + step)


def fold_z(rows, keep, small, first, out, small_out):
    for step in range(2):
        index = entry(2, step, 1 - own_bit(2))
        out[step * rows : (step + 1) * rows, :] = chunk_of(keep, index, rows) + chunk_of(first, index, rows)
    n = small.shape[1]
    total = four_sum(small[:8, :], small[8:, :], above(first[keep.shape[0] :, : 2 * n], n))
    small_out[...] = total
    out[2 * rows :, :n] = total
    out[2 * rows :, n:] = jnp.zeros_like(out[2 * rows :, n:])


def three_sum(rows, step, keep, first, second):
    index = entry_here(step)
    return chunk_of(keep, index, rows) + chunk_of(first, index, rows) + chunk_of(second, step, rows)


def fold_last(rows, keep, small, first, second, out, small_out):
    out[:rows, :] = three_sum(rows, 1 - own_bit(3), keep, first, second)
    small_out[:8, :] = small[...]
    small_out[8:, :] = second[2 * rows :, : small.shape[1]]
    side_by_side(out, rows, small_out)


def four_sum(mine, first, second):
    core = lax.axis_index("mp")
    near = mine + jnp.where(core == 0, first, second[:8])
    return near + (jnp.where(core == 0, second[:8], first) + second[8:])


def finish_cross(
    heads, rows, keep, first, second, sums, third, q_out, k_out, v_out, o_out, gain_s, gain_c, gain_f, bias_out
):
    inner = q_out.shape[1]
    total = three_sum(rows, own_bit(3), keep, first, second) + third[:rows, :]
    for k, out in enumerate((q_out, k_out, v_out, o_out)):
        out[...] = total[:, k * inner : (k + 1) * inner]
    width, buckets, n = gain_s.shape[0], bias_out.shape[1], sums.shape[1]
    small = four_sum(sums[:8, :], sums[8:, :], above(third[rows:, : 2 * n], n))
    for k, out in enumerate((gain_s, gain_c, gain_f)):
        out[...] = jnp.concatenate([small[2 * k : 2 * k + 1, :], small[2 * k + 1 : 2 * k + 2, :]], 1).reshape(width)
    bias_out[...] = jnp.concatenate([small[6:7, h * buckets : (h + 1) * buckets] for h in range(heads)], 0)


def self_fold(rows, keep, first, out):
    step = 1 - own_bit(3)
    out[...] = chunk_of(keep, step, rows) + chunk_of(first, step, rows)


def finish_self(rows, keep, first, second, q_out, k_out, v_out, o_out, token):
    token[...] = jnp.zeros_like(token)
    inner = q_out.shape[1]
    step = own_bit(3)
    total = chunk_of(keep, step, rows) + chunk_of(first, step, rows) + second[...]
    for k, out in enumerate((q_out, k_out, v_out, o_out)):
        out[...] = total[:, k * inner : (k + 1) * inner]


def ffn_fold(rows, keep, first, out):
    step = 1 - own_bit(1)
    out[...] = chunk_of(keep, step, rows) + chunk_of(first, step, rows)


def finish_ffn(rows, keep, first, second, in_out, out_out, token):
    token[...] = jnp.zeros_like(token)
    step = own_bit(1)
    total = chunk_of(keep, step, rows) + chunk_of(first, step, rows) + second[...]
    hidden = in_out.shape[1]
    in_out[...] = total[:, :hidden]
    out_out[...] = total[:, hidden:]


def ffn_group(normed, low, act, hid, here, there, w_in, w_out, send_out, keep_out, normed_all, low_all, total):
    tokens, width = normed.shape
    hidden = w_in.shape[1]
    half = tokens // 2
    rows = width // 16
    normed_all[:tokens, :] = normed[...]
    low_all[:tokens, :] = low[...]
    at = tokens
    for source in (here, there):
        for k in range(3):
            low_all[at : at + half, :] = source[2 * k * half : (2 * k + 1) * half, :].astype(bf16)
            normed_all[at : at + half, :] = source[(2 * k + 1) * half : (2 * k + 2) * half, :].astype(bf16)
            at += half
    place, core = place_of()
    first = lax.shift_right_logical(place, 2) * 4
    picked = pick_chunks([first + k for k in range(4)], rows, width)
    left_in = nt(picked, normed_all[...]).astype(bf16)
    left_out = nt(picked, low_all[...]).astype(bf16)
    chunk = 512 if hidden % 512 == 0 else hidden

    def one_chunk(k, carry):
        cols = pl.ds(pl.multiple_of(k * chunk, 128), chunk)
        u = nn(normed_all[tokens:, :], w_in[:, cols])
        t = jnp.tanh(curve * (u + cubic * (u * u * u)))
        other_act = (0.5 * u * (1.0 + t)).astype(bf16)
        slope = 0.5 * (1.0 + t) + 0.5 * u * (1.0 - t * t) * (curve * (1.0 + 3.0 * cubic * (u * u)))
        other_hid = (nt(low_all[tokens:, :], w_out[cols, :]) * slope).astype(bf16)
        total[:, cols] = nn(left_in[:, :tokens], hid[:, cols]) + nn(left_in[:, tokens:], other_hid)
        total[:, pl.ds(pl.multiple_of(hidden + k * chunk, 128), chunk)] = nn(
            left_out[:, :tokens], act[:, cols]
        ) + nn(left_out[:, tokens:], other_act)
        return carry

    lax.fori_loop(0, hidden // chunk, one_chunk, 0)
    split_entries(0, lambda i: total[pl.ds(pl.multiple_of(i * rows, 8), rows), :], send_out, keep_out, rows)


class Fetched:
    def __init__(self, ref, copy):
        self.ref, self.copy, self.shape, self.dtype = ref, copy, ref.shape, ref.dtype

    def arrive(self):
        if self.copy is not None:
            self.copy.wait()
            self.copy = None

    def __getitem__(self, place):
        self.arrive()
        return self.ref[place]


class Leaving:
    def __init__(self, ref, copy):
        self.ref, self.copy, self.shape, self.dtype = ref, copy, ref.shape, ref.dtype
        self.left = False

    def leave(self):
        if not self.left:
            self.copy.start()
            self.left = True

    def __getitem__(self, place):
        return self.ref[place]

    def __setitem__(self, place, value):
        self.ref[place] = value


SPACES = {"v": pltpu.VMEM, "h": pltpu.HBM, "a": pl.ANY}


def call(kernel, outs, args, scratch=(), after=(), limit=20, cost=1):
    kinds = [kind for _, kind, *_ in args]
    fetched = [k for k, kind in enumerate(kinds) if kind != "v"]
    written = [k for k, (_, _, kind) in enumerate(outs) if kind != "v"]

    def body(*refs):
        ins, rest = list(refs[: len(args)]), refs[len(args) + len(after) :]
        results, rest = list(rest[: len(outs)]), rest[len(outs) :]
        in_bufs, rest = rest[: len(fetched)], rest[len(fetched) :]
        out_bufs, rest = rest[: len(written)], rest[len(written) :]
        extra, rest = rest[: len(scratch)], rest[len(scratch) :]
        sems = rest[0] if rest else None
        waits = []
        for n, (k, buf) in enumerate(zip(fetched, in_bufs)):
            source = ins[k]
            if len(args[k]) > 2:
                source = source.at[pl.ds(args[k][2], buf.shape[0])]
            copy = pltpu.make_async_copy(source, buf, sems.at[n])
            copy.start()
            ins[k] = Fetched(buf, copy)
            waits.append(ins[k])
        leaving = []
        for n, (k, buf) in enumerate(zip(written, out_bufs)):
            results[k] = Leaving(buf, pltpu.make_async_copy(buf, results[k], sems.at[len(fetched) + n]))
            leaving.append(results[k])
        kernel(*ins, *results, *extra)
        for out in leaving:
            out.leave()
        for wait in waits:
            wait.arrive()
        for out in leaving:
            out.copy.wait()

    places = {kind: pl.BlockSpec(memory_space=space) for kind, space in SPACES.items()}
    shapes = [
        pltpu.VMEM((args[k][3:] or args[k][0].shape[:1]) + args[k][0].shape[1:], args[k][0].dtype) for k in fetched
    ]
    shapes += [pltpu.VMEM(outs[k][0], outs[k][1]) for k in written]
    shapes += [pltpu.VMEM(shape, kind) for shape, kind in scratch]
    if fetched or written:
        shapes.append(pltpu.SemaphoreType.DMA((len(fetched) + len(written),)))
    name = getattr(kernel, "__name__", None) or kernel.func.__name__
    return pl.pallas_call(
        body,
        out_shape=[
            pltpu.HBM(shape, kind) if place == "h" else jax.ShapeDtypeStruct(shape, kind) for shape, kind, place in outs
        ],
        in_specs=[places[kind] for kind in kinds] + [places["a"]] * len(after),
        out_specs=[places[kind] for _, _, kind in outs],
        scratch_shapes=shapes,
        compiler_params=pltpu.CompilerParams(vmem_limit_bytes=limit * 1024 * 1024),
        cost_estimate=pl.CostEstimate(flops=cost * 35 * 10**9, transcendentals=0, bytes_accessed=1000),
        name=name,
    )(
        *[
            pltpu.with_memory_space_constraint(value, pltpu.HBM) if kind == "h" else value
            for value, kind, *_ in args
        ],
        *after,
    )


def pair_swap(values):
    return lax.ppermute(values, "mp", [(0, 1), (1, 0)])


def swap_bit(values, bit, count):
    return lax.ppermute(values, "dp", [(k, k ^ (1 << bit)) for k in range(count)])


def stage_swap(values, stage, count):
    bits = ((0, 1), (1, 0), (2, 3), (3, 2))[stage]
    pairs = [(2 * k + core, 2 * (k ^ (1 << bits[core])) + core) for k in range(count) for core in range(2)]
    return lax.ppermute(values, ("dp", "mp"), pairs)


def half_of(values, dim, which):
    return lax.dynamic_index_in_dim(values, which, dim, keepdims=False)


def scatter_sum(blocks, order, count):
    place = lax.axis_index("dp")
    levels = len(order)
    left = list(reversed(range(levels)))
    blocks = blocks.reshape((2,) * levels + blocks.shape[1:])
    for bit in order:
        dim = left.index(bit)
        mine = (place >> bit) & 1
        moved = swap_bit(half_of(blocks, dim, 1 - mine), bit, count)
        blocks = half_of(blocks, dim, mine) + moved
        left.remove(bit)
    return blocks


def full_sum(values, count):
    for bit in range(count.bit_length() - 1):
        values = values + swap_bit(values, bit, count)
    return values


def on_device(
    dec_input, enc_output, dec_lengths, enc_lengths, self_query, self_key, self_value, self_output, self_gain,
    rel_bias, cross_query, cross_key, cross_value, cross_output, cross_gain, ffn_in, ffn_out, ffn_gain, cotangent
):
    slots, width = dec_input.shape[1:]
    steps = enc_output.shape[1]
    inner = self_query.shape[1]
    hidden = ffn_in.shape[1]
    tokens = 3 * slots // 2
    count = lax.axis_size("dp")
    quick = count == 16
    row, half_row = (tokens, width), (tokens // 2, width)
    part_of = (tokens, inner)
    wide = 4 * inner
    share = width // count

    bias_rows = rel_bias.T
    tall = tokens // 2 + 8
    x, low_ffn, qkv, att_self, lse_self, part_self, x_half = call(
        self_forward,
        [(row, bf16, "h"), (row, bf16, "h"), ((tokens, 3 * inner), bf16, "h"), (part_of, bf16, "v"),
         ((8, tokens), f32, "v"), (row, f32, "v"), ((tall, width), f32, "h")],
        [(dec_lengths, "h"), (dec_input, "h"), (self_gain, "h"), (self_query, "h"), (self_key, "h"), (self_value, "h"),
         (cotangent, "h"), (bias_rows, "h"), (self_output, "h")],
    )
    moved_self = pair_swap(part_self)
    if quick:
        x_moved = stage_swap(x_half, 0, count)
    keys, values_t, keys_far, values, keys_t = call(
        encoder_forward,
        [((2 * steps, inner), bf16, "v"), ((inner, 2 * steps), bf16, "v")] + [((2 * steps, inner), bf16, "h")] * 2
        + [((inner, 2 * steps), bf16, "h")],
        [(enc_output, "v"), (cross_key, "v"), (cross_value, "v")],
        after=(part_self,),
    )
    after_self, cross_q, att_cross, lse_cross, part_cross = call(
        cross_forward,
        [(row, f32, "v"), (part_of, bf16, "h"), (part_of, bf16, "v"), ((8, 2 * slots), f32, "v"), (row, f32, "v")],
        [(dec_lengths, "v"), (enc_lengths, "v"), (x, "v"), (part_self, "v"), (moved_self, "v"), (cross_gain, "v"),
         (cross_query, "v"), (cross_output, "v"), (keys, "v"), (values_t, "v")],
    )
    moved_cross = pair_swap(part_cross)
    after = (part_cross,)
    if quick:
        early, own_cross = call(
            pack_early,
            [(row, f32, "v"), ((width // 2, tokens), bf16, "v")],
            [(after_self, "v"), (cross_gain, "v"), (att_cross, "v")],
            after=after,
        )
        early_moved = stage_swap(early, 0, count)
        after = (early,)
    after_cross, normed_ffn, halves, act, hid, back, *x_two = call(
        ffn_both,
        [(row, f32, "v"), (row, bf16, "h"), (row, f32, "v"), ((tokens, hidden), bf16, "v"), ((tokens, hidden), bf16, "v"),
         (row, f32, "v")] + [((2 * tall, width), f32, "v")] * quick,
        [(after_self, "v"), (part_cross, "v"), (moved_cross, "v"), (ffn_gain, "v"), (low_ffn, "v"), (ffn_in, "v"),
         (ffn_out, "v")] + ([(x_half, "v"), (x_moved, "v")] if quick else []),
        after=after,
    )
    moved_back = pair_swap(back)
    if quick:
        group_a = stage_swap(halves, 2, count)
        x_rest = stage_swap(x_two[0], 1, count)
    grad_cross, low_cross, dq, dk, dv, gain_ffn_grad, part_dq = call(
        cross_backward,
        [(row, f32, "h"), (row, bf16, "v"), (part_of, bf16, "v")] + [((2 * steps, inner), bf16, "v")] * 2
        + [((1, width), f32, "v"), (row, f32, "v")],
        [(dec_lengths, "v"), (enc_lengths, "v"), (after_cross, "v"), (back, "v"), (moved_back, "v"), (ffn_gain, "v"),
         (low_ffn, "v"), (cross_output, "v"), (cross_query, "v"), (cross_q, "v"), (keys_far, "v"), (values, "v"),
         (keys_t, "v"), (lse_cross, "v")],
        after=(rest(back),),
    )
    moved_dq = pair_swap(part_dq)
    after = (rest(part_dq), early_moved) if quick else (rest(part_dq),)
    grad_self, low_self, self_half, gain_cross_grad = call(
        self_grad,
        [(row, f32, "v"), (row, bf16, "v"), ((tokens // 2, width), f32, "v"), ((1, width), f32, "v")],
        [(after_self, "v"), (part_dq, "v"), (moved_dq, "v"), (cross_gain, "v"), (grad_cross, "v")],
        after=after,
    )
    after = (low_self,)
    half = width // 2
    if quick:
        self_a = stage_swap(self_half, 0, count)
    dqkv, bias_grad, parts = call(
        back_all,
        [((tokens, 3 * inner), bf16, "v"), ((8, rel_bias.shape[0]), f32, "v"), ((2 * tokens + 2 * steps, width), f32, "v")],
        [(dec_lengths, "v"), (low_self, "v"), (bias_rows, "v"), (self_output, "v"), (self_query, "v"), (self_key, "v"),
         (self_value, "v"), (qkv, "v"), (lse_self, "v"), (dk, "v"), (dv, "v"), (cross_key, "v"), (cross_value, "v"),
         (act, "v"), (ffn_out, "v")],
        after=after,
    )
    parts_moved = pair_swap(parts)
    after = (rest(parts),)
    if quick:
        self_two, halves_two = call(
            collect,
            [(row, f32, "v"), ((2 * tokens, width), f32, "v")],
            [(self_half, "v"), (self_a, "v"), (halves, "v"), (group_a, "v")],
            after=(parts, x_rest),
        )
        self_rest = stage_swap(self_two, 1, count)
        group_rest = stage_swap(halves_two, 3, count)
        (late_cross,) = call(
            cross_weights,
            [((half + tokens, 2 * inner), f32, "v")],
            [(enc_output, "v"), (dk, "v"), (dv, "v"), (dq, "v"), (low_cross, "v")],
            after=(self_two,),
        )
        late_cross_moved = stage_swap(late_cross, 0, count)
        (self_here,) = call(
            gather_self,
            [((3 * tall + 3 * tokens // 2, width), f32, "v")],
            [(x_moved, "v"), (x_rest, "v"), (self_a, "v"), (self_rest, "v")],
            after=(late_cross,),
        )
        self_there = pair_swap(self_here)
        after = (rest(self_here),)
    dec_packed, small = call(
        named(finish_self_norm, rel_bias.shape[1]),
        [(row, bf16, "v"), ((8, half), f32, "v")],
        [(x, "v"), (parts, "v"), (parts_moved, "v"), (self_gain, "v"), (grad_self, "v"),
         (gain_ffn_grad, "v"), (gain_cross_grad, "v"), (bias_grad, "v")],
        after=after,
    )
    if quick:
        small_moved = stage_swap(small, 0, count)
    after = (small,)
    if quick:
        send_self, keep_self = call(
            self_group,
            [((2 * share, wide), f32, "v")] * 2,
            [(x, "v"), (dqkv, "v"), (low_self, "v"), (att_self, "v"), (self_here, "v"), (self_there, "v"),
             (self_gain, "v"), (bias_rows, "v"), (self_query, "v"), (self_key, "v"), (self_value, "v"), (self_output, "v")],
            scratch=[((3 * tokens, wide), bf16), ((4 * tokens, wide), bf16), ((4 * share, wide), f32)],
            after=after,
        )
        self_first = stage_swap(send_self, 2, count)
        after = (send_self,)
    mark = ((8, 128), f32, "v")

    def outputs(after):
        return call(
            finish_outputs,
            [(dec_input.shape, bf16, "v"), (dec_input.shape, bf16, "v"), (enc_output.shape, bf16, "v"), mark],
            [(dec_lengths, "v"), (dec_packed, "v"), (parts, "v"), (parts_moved, "v"), (after_cross, "v")],
            after=after,
        )

    if not quick:
        dec_grad, layer_out, enc_grad, done = outputs(after)
        return slow_sums(
            locals(), x, after_self, self_gain, cross_gain, rel_bias, enc_output, count
        )
    (keep_cross,) = call(
        cross_keep,
        [((half, wide), f32, "v")],
        [(enc_output, "v"), (dk, "v"), (dv, "v"), (own_cross, "v"), (dq, "v"), (low_cross, "v"), (att_cross, "v")],
        after=(send_self,)
    )
    send_cross, keep_cross, small_two = call(
        cross_fold,
        [((half // 2 + 8, wide), f32, "v"), ((half // 2, wide), f32, "v"), ((16, half), f32, "v")],
        [(keep_cross, "v"), (late_cross_moved, "a", half, tokens), (late_cross_moved, "a", 0, half), (early_moved, "v"),
         (small, "v"), (small_moved, "v")],
        scratch=[((half, wide), f32)],
        after=(keep_cross,),
    )
    cross_first = stage_swap(send_cross, 1, count)
    (ffn_here,) = call(
        gather_ffn, [((3 * tokens, width), f32, "v")], [(group_a, "v"), (group_rest, "v")], after=(send_cross,)
    )
    ffn_there = pair_swap(ffn_here)
    dec_grad, layer_out, enc_grad, done = outputs((ffn_here,))
    made_ffn, keep_ffn = call(
        ffn_group,
        [((2 * share, 2 * hidden), f32, "v")] * 2,
        [(normed_ffn, "v"), (low_ffn, "v"), (act, "v"), (hid, "v"), (ffn_here, "v"), (ffn_there, "v"), (ffn_in, "v"),
         (ffn_out, "v")],
        scratch=[((4 * tokens, width), bf16), ((4 * tokens, width), bf16), ((4 * share, 2 * hidden), f32)],
        after=(done,),
    )
    (send_self2,) = call(
        named(self_fold, share), [((share, wide), f32, "v")], [(keep_self, "v"), (self_first, "v")], after=(made_ffn,)
    )
    self_second = stage_swap(send_self2, 3, count)
    send_cross2, small_four = call(
        named(fold_z, share),
        [((half // 4 + 8, wide), f32, "v"), ((8, half), f32, "v")],
        [(keep_cross, "v"), (small_two, "v"), (cross_first, "v")],
        after=(send_self2,),
    )
    cross_second = stage_swap(send_cross2, 2, count)
    (send_ffn,) = call(relay, [((2 * share, 2 * hidden), f32, "v")], [(made_ffn, "v")], after=(send_cross2,))
    ffn_first = stage_swap(send_ffn, 0, count)
    *self_grads, self_out_grad, done = call(
        named(finish_self, share),
        [((share, inner), f32, "v")] * 4 + [mark],
        [(keep_self, "v"), (self_first, "v"), (self_second, "v")],
        after=(send_ffn,),
    )
    (send_ffn2,) = call(
        named(ffn_fold, share), [((share, 2 * hidden), f32, "v")], [(keep_ffn, "v"), (ffn_first, "v")], after=(done,)
    )
    ffn_second = stage_swap(send_ffn2, 1, count)
    send_cross3, small_last = call(
        named(fold_last, share),
        [((share + 8, wide), f32, "v"), ((16, half), f32, "v")],
        [(keep_cross, "v"), (small_four, "v"), (cross_first, "v"), (cross_second, "v")],
        after=(send_ffn2,),
    )
    cross_third = stage_swap(send_cross3, 3, count)
    grad_ffn_in, grad_ffn_out, done = call(
        named(finish_ffn, share),
        [((share, hidden), f32, "h")] * 2 + [mark],
        [(keep_ffn, "v"), (ffn_first, "v"), (ffn_second, "v")],
        after=(rest(send_cross3),),
    )
    *cross_grads, cross_out_grad, gain_self_sum, gain_cross_sum, gain_ffn_sum, bias_sum = call(
        named(finish_cross, rel_bias.shape[1], share),
        [((share, inner), f32, "h")] * 4 + [((width,), f32, "h")] * 3 + [(rel_bias.shape[::-1], f32, "h")],
        [(keep_cross, "v"), (cross_first, "v"), (cross_second, "v"), (small_last, "v"), (cross_third, "v")],
        after=(done,),
    )
    return (
        layer_out,
        dec_grad,
        enc_grad,
        *self_grads,
        self_out_grad.T,
        gain_self_sum,
        bias_sum.T,
        *cross_grads,
        cross_out_grad.T,
        gain_cross_sum,
        grad_ffn_in,
        grad_ffn_out.T,
        gain_ffn_sum,
    )


def rest(made):
    (out,) = call(pause, [((8, 128), f32, "v")], [], after=(made,))
    return out


def named(kernel, *given):
    def run(*refs):
        return kernel(*given, *refs)

    run.__name__ = kernel.__name__
    return run


def slow_sums(made, x, after_self, self_gain, cross_gain, rel_bias, enc_output, count):
    width = x.shape[1]
    heads, buckets = rel_bias.shape[1], rel_bias.shape[0]
    inner = made["dq"].shape[1]
    bits = list(range(count.bit_length() - 1))
    order_a, order_b = bits, bits[1::-1] + bits[2:]

    def scattered(order, *grads):
        parts = [grad.reshape(count, -1, grad.shape[1]) for grad in grads]
        widths = [part.shape[2] for part in parts]
        total = scatter_sum(jnp.concatenate(parts, axis=2), order, count)
        return jnp.split(total, np.cumsum(widths)[:-1].tolist(), axis=1)

    def outer(left, right):
        return jnp.einsum("rm,rn->mn", left, right, preferred_element_type=f32)

    def normed(values, gain):
        return (values * inverse_rms(values) * gain).astype(bf16)

    normed_self = normed(x.astype(f32), self_gain)
    normed_cross = normed(after_self, cross_gain)
    enc_flat = enc_output.reshape(-1, width)
    dqkv = made["dqkv"]
    (grad_ffn_in,) = scattered(order_a, outer(made["normed_ffn"], made["hid"]))
    (grad_ffn_out,) = scattered(order_b, outer(made["low_ffn"], made["act"]))
    cross_query, cross_key = scattered(order_a, outer(normed_cross, made["dq"]), outer(enc_flat, made["dk"]))
    cross_value, cross_output = scattered(
        order_b, outer(enc_flat, made["dv"]), outer(made["low_cross"], made["att_cross"])
    )
    self_query, self_key = scattered(
        order_a, outer(normed_self, dqkv[:, :inner]), outer(normed_self, dqkv[:, inner : 2 * inner])
    )
    self_value, self_output = scattered(
        order_b, outer(normed_self, dqkv[:, 2 * inner :]), outer(made["low_self"], made["att_self"])
    )
    small = full_sum(made["small"], count)
    return (
        made["layer_out"],
        made["dec_grad"],
        made["enc_grad"],
        self_query,
        self_key,
        self_value,
        self_output.T,
        small[0:2].reshape(-1),
        small[6, : heads * buckets].reshape(heads, buckets).T,
        cross_query,
        cross_key,
        cross_value,
        cross_output.T,
        small[2:4].reshape(-1),
        grad_ffn_in,
        grad_ffn_out.T,
        small[4:6].reshape(-1),
    )


def solution(mesh):
    in_specs = (
        P("dp", None, None),
        P("dp", None, None),
        P("dp", None),
        P("dp", None),
        P(None, "mp"),
        P(None, "mp"),
        P(None, "mp"),
        P("mp", None),
        P(),
        P(None, "mp"),
        P(None, "mp"),
        P(None, "mp"),
        P(None, "mp"),
        P("mp", None),
        P(),
        P(None, "mp"),
        P("mp", None),
        P(),
        P("dp", None, None),
    )
    out_specs = (
        P("dp", None, None),
        P("dp", None, None),
        P("dp", None, None),
        P("dp", "mp"),
        P("dp", "mp"),
        P("dp", "mp"),
        P("mp", "dp"),
        P(),
        P(None, "mp"),
        P("dp", "mp"),
        P("dp", "mp"),
        P("dp", "mp"),
        P("mp", "dp"),
        P(),
        P("dp", "mp"),
        P("mp", "dp"),
        P(),
    )
    return jax.shard_map(
        on_device, mesh=mesh, in_specs=in_specs, out_specs=out_specs, check_vma=False
    )
```
